256 devices in a mesh: cache: 16 (over y_lo, x, core), head: 16 (over z, y_hi).
Axes of the slice: x: 4, y: 4 (y_hi: 2, y_lo: 2; y = y_hi * 2 + y_lo), z: 8, core: 2. Of those that a mesh axis runs over, the one named last changes fastest.
Arguments:
- q_nope: bfloat16 [2048, 8192], P('cache', 'head'), may hold values from -6 to 6
- q_rope: bfloat16 [2048, 4096], P('cache', 'head'), may hold values from -8 to 8
- new_latent: bfloat16 [2048, 512], P('cache'), may hold values from -6 to 6
- new_rope: bfloat16 [16, 64, 128], P('cache'), may hold values from -6 to 6
- pool_latent: bfloat16 [64, 128, 512], P('cache'), may hold values from -6 to 6
- pool_rope: bfloat16 [64, 64, 128], P('cache'), may hold values from -8 to 8
- block_table: int32 [16, 32], replicated, may hold values from 0 to 63, as said below
- prefix_len: int32 [16], replicated, may hold values from 1025 to 4096
- w_uk: bfloat16 [64, 128, 512], P('head'), may hold values from -0.5 to 0.5
- w_uv: bfloat16 [64, 512, 128], P('head'), may hold values from -4 to 4
- w_out: bfloat16 [8192, 7168], P('head', 'cache'), may hold values from -0.0625 to 0.0625
Outputs:
- attended: bfloat16 [2048, 7168], P(('cache', 'head'))
The draws below stay inside these ranges and needn't reach their ends.
Inputs may be any that keep to these rules, and one draw needn't show every extreme that they name: `block_table`: row r lists the pool blocks that hold request r's prefix, in order; a row names a block at most once; the first 8 entries are the same in every row.
All inputs are finite; a program needn't handle non-finite values.
Results may differ from the reference program's by a relative error of at most 0.02.
Values may be sent and summed in bfloat16 or wider, within the bound.
No kernel may reach another device: no remote copies, remote signals or barrier semaphores. Data moves between devices by JAX's collectives and lax.ppermute only.
A program may use at most 128 MiB of HBM per device.

```python
import jax
import jax.numpy as jnp
from jax import lax

D = 7168
H = 64
LAT = 512
NOPE = 128
ROPE = 64
VD = 128
BLOCK = 128
TOK_DEV = 128
REQS = 16
TOKENS = 2048
NBLK = 64
MAXBLK = 32
SHARED = 8


def common_layout(key):
    order_blocks = jax.random.permutation(jax.random.fold_in(key, 101), NBLK).astype(jnp.int32)
    return order_blocks


def draw_block_table(key, part):
    order_blocks = common_layout(key)
    request_ids = jnp.arange(REQS, dtype=jnp.int32)[:, None]
    columns = jnp.arange(MAXBLK, dtype=jnp.int32)[None, :]
    free_span = NBLK - SHARED
    window_start = request_ids * free_span // REQS
    private = SHARED + (window_start + columns - SHARED) % free_span
    slot_index = jnp.where(columns < SHARED, columns, private)
    return order_blocks[slot_index].astype(jnp.int32)


def draw_prefix_len(key, part):
    key = jax.random.fold_in(key, 2)
    lengths = jax.random.randint(key, (REQS,), SHARED * BLOCK + 1, MAXBLK * BLOCK + 1)
    longest = jax.random.randint(jax.random.fold_in(key, 7), (), 0, REQS)
    return jnp.where(jnp.arange(REQS) == longest, MAXBLK * BLOCK, lengths).astype(jnp.int32)


def draw_q_rope(key, part):
    key = jax.random.fold_in(key, 3)
    values = jnp.clip(jax.random.normal(key, (TOKENS, H, ROPE)), -6.0, 6.0)
    return values.reshape(TOKENS, H * ROPE).astype(jnp.bfloat16)


def draw_pool_rope(key, part):
    key = jax.random.fold_in(key, 4)
    values = jnp.clip(jax.random.normal(key, (NBLK, ROPE, BLOCK)), -6.0, 6.0)
    return values.astype(jnp.bfloat16)


def block_scale(stream_key, shape, pieces, low, largest):
    def one(position, parts):
        steps = jax.random.uniform(jax.random.fold_in(jax.random.fold_in(stream_key, 6), position), (parts,), jnp.float32, low / len(pieces), largest / len(pieces))
        return jnp.repeat(jnp.exp(steps), shape[position] // parts).reshape((-1,) + (1,) * (len(shape) - position - 1))

    factor_of = one(*pieces[0])
    for cut in pieces[1:]:
        factor_of = factor_of * one(*cut)
    return factor_of


def noise(key, shape, deviation, limit, pieces=(), held_as=jnp.bfloat16):
    values = deviation * jax.random.normal(key, shape, jnp.float32)
    if pieces:
        values = values * block_scale(key, shape, pieces, -0.22, 0.18)
    return jnp.clip(values, -limit, limit).astype(held_as)


def setup_inputs(seed: int = 0) -> dict:
    splits = jax.random.split(jax.random.key(seed), 12)
    return {
        "q_nope": noise(splits[0], (TOKENS, H * NOPE), 1.0, 6.0, ((0, 16), (1, 16))),
        "q_rope": draw_q_rope(jax.random.fold_in(splits[11], 71), 0),
        "new_latent": noise(splits[2], (TOKENS, LAT), 1.0, 6.0, ((0, 16),)),
        "new_rope": noise(splits[3], (TOKENS // BLOCK, ROPE, BLOCK), 1.0, 6.0, ((0, 16),)),
        "pool_latent": noise(splits[4], (NBLK, BLOCK, LAT), 1.0, 6.0, ((0, 16),)),
        "pool_rope": draw_pool_rope(jax.random.fold_in(splits[11], 71), 0),
        "block_table": draw_block_table(jax.random.fold_in(splits[11], 71), 0),
        "prefix_len": draw_prefix_len(jax.random.fold_in(splits[11], 71), 0),
        "w_uk": noise(splits[8], (H, NOPE, LAT), NOPE ** -0.5, 0.5, ((0, 16),)),
        "w_uv": noise(splits[9], (H, LAT, VD), (max(1, LAT // 256)) ** -0.5, 4.0, ((0, 16),)),
        "w_out": noise(splits[10], (H * VD, D), (H * VD) ** -0.5, 0.0625, ((0, 16), (1, 16))),
    }


masked_score = -1.0e30


def rounded(values):
    return lax.optimization_barrier(values.astype(jnp.bfloat16))


def reference(q_nope, q_rope, new_latent, new_rope, pool_latent, pool_rope, block_table, prefix_len, w_uk, w_uv, w_out):
    softmax_scale = (NOPE + ROPE) ** -0.5
    q_lat = rounded(jnp.einsum('thn,hnc->thc', q_nope.reshape(TOKENS, H, NOPE).astype(jnp.float32), w_uk.astype(jnp.float32)))
    q_rot = q_rope.reshape(TOKENS, H, ROPE)
    blocks_new = TOK_DEV // BLOCK

    def one_request(request):
        first_row = (request * TOK_DEV).astype(jnp.int32)
        query_lat = lax.dynamic_slice_in_dim(q_lat, first_row, TOK_DEV, 0)
        query_rot = lax.dynamic_slice_in_dim(q_rot, first_row, TOK_DEV, 0)
        table_row = block_table[request]
        prefix_latent = pool_latent[table_row].reshape(MAXBLK * BLOCK, LAT)
        prefix_rope = jnp.transpose(pool_rope[table_row], (1, 0, 2)).reshape(ROPE, MAXBLK * BLOCK)
        own_latent = lax.dynamic_slice_in_dim(new_latent, first_row, TOK_DEV, 0)
        own_rope = lax.dynamic_slice_in_dim(new_rope, (request * blocks_new).astype(jnp.int32), blocks_new, 0)
        own_rope = jnp.transpose(own_rope, (1, 0, 2)).reshape(ROPE, TOK_DEV)
        key_latent = jnp.concatenate([prefix_latent, own_latent], axis=0)
        key_rope = jnp.concatenate([prefix_rope, own_rope], axis=1)
        score = jnp.einsum('thc,kc->thk', query_lat.astype(jnp.float32), key_latent.astype(jnp.float32))
        score = score + jnp.einsum('thr,rk->thk', query_rot.astype(jnp.float32), key_rope.astype(jnp.float32))
        score = score * softmax_scale
        prefix_ok = jnp.arange(MAXBLK * BLOCK, dtype=jnp.int32) < prefix_len[request]
        prefix_ok = jnp.broadcast_to(prefix_ok[None, :], (TOK_DEV, MAXBLK * BLOCK))
        causal = jnp.arange(TOK_DEV, dtype=jnp.int32)[None, :] <= jnp.arange(TOK_DEV, dtype=jnp.int32)[:, None]
        allowed = jnp.concatenate([prefix_ok, causal], axis=1)[:, None, :]
        highest = jnp.max(jnp.where(allowed, score, masked_score), axis=-1, keepdims=True)
        weights = jnp.where(allowed, jnp.exp(score - highest), 0.0)
        totals = jnp.sum(weights, axis=-1)
        summed = jnp.einsum('thk,kc->thc', rounded(weights).astype(jnp.float32), key_latent.astype(jnp.float32))
        latent_out = rounded(summed / totals[..., None])
        head_out = jnp.einsum('thc,hcv->thv', latent_out.astype(jnp.float32), w_uv.astype(jnp.float32)).astype(jnp.bfloat16)
        return jnp.dot(head_out.reshape(TOK_DEV, H * VD), w_out, preferred_element_type=jnp.float32).astype(jnp.bfloat16)

    results = lax.map(one_request, jnp.arange(REQS, dtype=jnp.int32))
    return results.reshape(TOKENS, D)
```

```python
import functools

import jax
import jax.numpy as jnp
from jax import lax
from jax.experimental import pallas as pl
from jax.experimental.pallas import tpu as pltpu
from jax.sharding import Mesh, PartitionSpec as P

LAT = 512
NOPE = 128
ROPE = 64
VD = 128
BLOCK = 128
HEADS = 4
TOK = 128
ROWS = HEADS * TOK
SLOTS = 4
LOG2E = 1.4426950408889634
SCALE2 = (NOPE + ROPE) ** -0.5 * LOG2E
LOW = -1e30
STAT = HEADS * VD
MSG = STAT + 128

VMEM = pltpu.VMEM
SMEM = pltpu.SMEM


def dot_nn(a, b):
    return lax.dot_general(a, b, (((1,), (0,)), ((), ())), preferred_element_type=jnp.float32)


def dot_nt(a, b):
    return lax.dot_general(a, b, (((1,), (1,)), ((), ())), preferred_element_type=jnp.float32)


def attention_kernel(slots, own, ids, table, lens, *refs):
    count = len(slots)
    refs = list(refs)

    def take(n):
        got = refs[:n]
        del refs[:n]
        return got

    queries = take(count)
    pools = take(4)
    w_uk, w_uv = take(2)
    new_latent, new_rope = take(2) if own else (None, None)
    outs = take(count)
    keys, rots, sems, q_lat, q_rot, acc, top, tot = refs
    yl, x, k = ids[0], ids[1], ids[2]

    def fetch(s, src, i, at):
        chunk, half = at // 2, pl.multiple_of((at % 2) * BLOCK, BLOCK)
        return (
            pltpu.make_async_copy(
                src.at[pl.ds(pl.multiple_of(i * BLOCK, BLOCK), BLOCK), :],
                keys.at[s, chunk, pl.ds(half, BLOCK), :],
                sems.at[s, at, 0],
            ),
            pltpu.make_async_copy(
                src.at[pl.ds(4 * BLOCK, ROPE), pl.ds(pl.multiple_of(i * BLOCK, BLOCK), BLOCK)],
                rots.at[s, chunk, :, pl.ds(half, BLOCK)],
                sems.at[s, at, 1],
            ),
        )

    counts, totals = [], []
    for s, slot in enumerate(slots):
        request = yl * 8 + ((x + slot) % 4) * 2 + k
        limit = lens[request]

        def scan(m, carry):
            found, valid = carry
            block = table[request, m]
            owner, i = block >> 2, block & 3
            here = jnp.logical_and(m * BLOCK < limit, ((owner >> 1) & 3) == x)
            source = ((owner >> 3) ^ yl) + 2 * ((owner & 1) ^ k)
            for j in range(4):

                @pl.when(jnp.logical_and(here, source == j))
                def _():
                    for copy in fetch(s, pools[j], i, found):
                        copy.start()

            step = here.astype(jnp.int32)
            return found + step, valid + step * jnp.minimum(limit - m * BLOCK, BLOCK)

        found, valid = lax.fori_loop(0, 32, scan, (jnp.int32(0), jnp.int32(0)))
        counts.append(found)
        totals.append(valid)

        @pl.when(found % 2 == 1)
        def _():
            keys[s, found // 2, BLOCK:, :] = jnp.zeros((BLOCK, LAT), jnp.bfloat16)
            rots[s, found // 2, :, BLOCK:] = jnp.zeros((ROPE, BLOCK), jnp.bfloat16)

    for s in range(count):
        for h in range(HEADS):
            rows = slice(h * TOK, (h + 1) * TOK)
            q_lat[rows, :] = dot_nn(queries[s][:, h * NOPE : (h + 1) * NOPE], w_uk[h]).astype(jnp.bfloat16)
            first = HEADS * NOPE + h * ROPE
            q_rot[rows, :] = queries[s][:, first : first + ROPE]
        if own:
            for g in range(2):
                rows = slice(g * 256, (g + 1) * 256)
                fresh = new_latent[...]
                score = dot_nt(q_lat[rows, :], fresh) + dot_nn(q_rot[rows, :], new_rope[...])
                at = lax.broadcasted_iota(jnp.int32, score.shape, 0) % TOK
                seen = lax.broadcasted_iota(jnp.int32, score.shape, 1) <= at
                score = jnp.where(seen, score, LOW)
                best = jnp.broadcast_to(jnp.max(score, axis=1, keepdims=True), (256, 128))
                weight = jnp.exp2((score - best) * SCALE2)
                top[rows, :] = best
                tot[rows, :] = weight
                acc[rows, :] = dot_nn(weight.astype(jnp.bfloat16), fresh)
        else:
            top[...] = jnp.full((ROWS, 128), LOW, jnp.float32)
            tot[...] = jnp.zeros((ROWS, 128), jnp.float32)
            acc[...] = jnp.zeros((ROWS, LAT), jnp.float32)

        def step(chunk, carry):
            for copy in fetch(s, pools[0], 0, chunk * 2):
                copy.wait()

            @pl.when(chunk * 2 + 1 < counts[s])
            def _():
                for copy in fetch(s, pools[0], 0, chunk * 2 + 1):
                    copy.wait()

            left = totals[s] - chunk * 2 * BLOCK
            for g in range(2):
                rows = slice(g * 256, (g + 1) * 256)
                latent = keys[s, chunk]
                score = dot_nt(q_lat[rows, :], latent) + dot_nn(q_rot[rows, :], rots[s, chunk])
                seen = lax.broadcasted_iota(jnp.int32, score.shape, 1) < left
                score = jnp.where(seen, score, LOW)
                before = top[rows, :]
                best = jnp.maximum(before, jnp.max(score, axis=1, keepdims=True))
                keep = jnp.exp2((before - best) * SCALE2)
                weight = jnp.exp2((score - jnp.concatenate([best, best], axis=1)) * SCALE2)
                top[rows, :] = best
                tot[rows, :] = tot[rows, :] * keep + weight[:, :128] + weight[:, 128:]
                acc[rows, :] = acc[rows, :] * jnp.concatenate([keep] * 4, axis=1) + dot_nn(
                    weight.astype(jnp.bfloat16), latent
                )
            return carry

        lax.fori_loop(0, (counts[s] + 1) // 2, step, 0)

        lane = lax.broadcasted_iota(jnp.int32, (TOK, 128), 1)
        stat = jnp.zeros((TOK, 128), jnp.float32)
        for h in range(HEADS):
            rows = slice(h * TOK, (h + 1) * TOK)
            total = jnp.broadcast_to(jnp.sum(tot[rows, :], axis=1, keepdims=True), (TOK, 128))
            some = total > 0.0
            safe = jnp.where(some, total, 1.0)
            inverse = 1.0 / safe
            latent_out = (acc[rows, :] * jnp.concatenate([inverse] * 4, axis=1)).astype(jnp.bfloat16)
            outs[s][:, h * VD : (h + 1) * VD] = dot_nn(latent_out, w_uv[h]).astype(jnp.bfloat16)
            level = jnp.where(some, top[rows, :] * SCALE2 + jnp.log2(safe), LOW)
            high = level.astype(jnp.bfloat16).astype(jnp.float32)
            middle = (level - high).astype(jnp.bfloat16).astype(jnp.float32)
            low = level - high - middle
            stat = jnp.where(lane == h, high, stat)
            stat = jnp.where(lane == HEADS + h, middle, stat)
            stat = jnp.where(lane == 2 * HEADS + h, low, stat)
        outs[s][:, STAT:] = stat.astype(jnp.bfloat16)


def attention(slots, own, ids, table, lens, queries, pools, w_uk, w_uv, fresh):
    count = len(slots)
    full = pl.BlockSpec(memory_space=VMEM)
    scalar = pl.BlockSpec(memory_space=SMEM)
    return pl.pallas_call(
        functools.partial(attention_kernel, slots, own),
        out_shape=[jax.ShapeDtypeStruct((TOK, MSG), jnp.bfloat16)] * count,
        in_specs=[scalar] * 3
        + [full] * count
        + [pl.BlockSpec(memory_space=pl.ANY)] * 4
        + [full] * (4 if own else 2),
        out_specs=[full] * count,
        scratch_shapes=[
            pltpu.VMEM((count, 8, 2 * BLOCK, LAT), jnp.bfloat16),
            pltpu.VMEM((count, 8, ROPE, 2 * BLOCK), jnp.bfloat16),
            pltpu.SemaphoreType.DMA((count, 16, 2)),
            pltpu.VMEM((ROWS, LAT), jnp.bfloat16),
            pltpu.VMEM((ROWS, ROPE), jnp.bfloat16),
            pltpu.VMEM((ROWS, LAT), jnp.float32),
            pltpu.VMEM((ROWS, 128), jnp.float32),
            pltpu.VMEM((ROWS, 128), jnp.float32),
        ],
        compiler_params=pltpu.CompilerParams(vmem_limit_bytes=40 * 2**20),
        cost_estimate=pl.CostEstimate(
            flops=count * 2 * ROWS * 1024 * 1088, bytes_accessed=count * 2**21, transcendentals=count * ROWS * 1024
        ),
        name="attend",
    )(ids, table, lens, *queries, *pools, w_uk, w_uv, *fresh)


def combine_kernel(*refs):
    parts, out = refs[:SLOTS], refs[SLOTS]
    stats = [p[:, STAT:].astype(jnp.float32) for p in parts]
    for h in range(HEADS):
        columns = slice(h * VD, (h + 1) * VD)
        levels = [
            s[:, h : h + 1] + s[:, HEADS + h : HEADS + h + 1] + s[:, 2 * HEADS + h : 2 * HEADS + h + 1]
            for s in stats
        ]
        best = functools.reduce(jnp.maximum, levels)
        shares = [jnp.exp2(v - best) for v in levels]
        inverse = 1.0 / sum(shares)
        out[:, columns] = sum(
            p[:, columns].astype(jnp.float32) * (share * inverse) for p, share in zip(parts, shares)
        ).astype(jnp.bfloat16)


def project_kernel(ids, *refs):
    heads, mine, other = refs[:8], refs[8:12], refs[12:16]
    outs = refs[16:20]
    weights, sems, stacked, total = refs[20:]
    yl, x, k, zb, a = ids[0], ids[1], ids[2], ids[3], ids[4]
    copies = []
    for j in range(4):
        for side, pieces in enumerate((mine, other)):
            first = pl.multiple_of((k ^ side) * 448, 64)
            copy = pltpu.make_async_copy(pieces[j], weights.at[j, pl.ds(first, 448), :], sems.at[j, side])
            copy.start()
            copies.append(copy)
    for m in range(8):
        stacked[a ^ (m & 3), pl.ds(pl.multiple_of((yl ^ (m >> 2)) * TOK, TOK), TOK), :] = heads[m][...]
    for copy in copies:
        copy.wait()
    value = None
    for j in range(4):
        part = dot_nt(stacked[(x + j) % 4], weights[j])
        value = part if value is None else value + part
    total[...] = value
    for d in range(4):
        first = pl.multiple_of(((zb + d) % 4) * 32, 32)
        for half in range(2):
            outs[d][half * 32 : (half + 1) * 32, :] = total[pl.ds(first + half * TOK, 32), :].astype(jnp.bfloat16)


def share_kernel(ids, *refs):
    parts, outs, total = refs[:4], refs[4:12], refs[12]
    yl, a = ids[0], ids[4]
    total[...] = sum(p[...].astype(jnp.float32) for p in parts)
    for m in range(8):
        first = (yl ^ (m >> 2)) * 32 + (a ^ (m & 3)) * 8
        outs[m][...] = total[pl.ds(pl.multiple_of(first, 8), 8), :]


def place_kernel(ids, *refs):
    parts, out = refs[:8], refs[8]
    yl, a = ids[0], ids[4]
    for m in range(8):
        first = ((yl ^ (m >> 2)) * 4 + (a ^ (m & 3))) * 896
        out[:, pl.ds(pl.multiple_of(first, 128), 896)] = parts[m][...].astype(jnp.bfloat16)


def simple(kernel, name, out_shape, args, scratch=(), any_from=None):
    full = pl.BlockSpec(memory_space=VMEM)
    specs = [
        pl.BlockSpec(memory_space=SMEM)
        if arg.dtype == jnp.int32
        else pl.BlockSpec(memory_space=pl.ANY)
        if any_from is not None and i >= any_from
        else full
        for i, arg in enumerate(args)
    ]
    return pl.pallas_call(
        kernel,
        out_shape=out_shape,
        in_specs=specs,
        out_specs=jax.tree.map(lambda _: full, out_shape),
        scratch_shapes=scratch,
        compiler_params=pltpu.CompilerParams(vmem_limit_bytes=40 * 2**20),
        name=name,
    )(*args)


GROUP = ("yl", "z0", "yh")


def turn(value, axis, size, shift):
    return lax.ppermute(value, axis, [((i + shift) % size, i) for i in range(size)])


def flip(value, axis, size, bits):
    return lax.ppermute(value, axis, [(i, i ^ bits) for i in range(size)])


def local(
    q_nope,
    q_rope,
    new_latent,
    new_rope,
    pool_latent,
    pool_rope,
    block_table,
    prefix_len,
    w_uk,
    w_uv,
    w_out,
):
    ids = jnp.stack(
        [
            lax.axis_index("yl"),
            lax.axis_index("x"),
            lax.axis_index("k"),
            lax.axis_index("zb"),
            lax.axis_index("z0") * 2 + lax.axis_index("yh"),
        ]
    ).astype(jnp.int32)
    query = jnp.concatenate([q_nope, q_rope], axis=1)
    pool = jnp.concatenate(
        [pool_latent.reshape(4 * BLOCK, LAT), jnp.transpose(pool_rope, (1, 0, 2)).reshape(ROPE, 4 * BLOCK)], axis=0
    )
    weight = w_out.T

    pool_y = flip(pool, "yl", 2, 1)
    queries = [turn(query, "x", 4, s) for s in (1, 2, 3)]
    pool_k = flip(pool, "k", 2, 1)
    pool_yk = flip(pool_y, "k", 2, 1)
    pools = [pool, pool_y, pool_k, pool_yk]

    turned = lax.ppermute(
        weight, ("x", "z0", "yh"), [(i * 4 + j, j * 4 + i) for i in range(4) for j in range(4)]
    )
    mine = [turned] + [turn(turned, "x", 4, s) for s in (1, 2, 3)]
    other = [flip(w, "k", 2, 1) for w in mine]

    away = attention((1, 2, 3), False, ids, block_table, prefix_len, queries, pools, w_uk, w_uv, ())
    came = [
        lax.ppermute(part, "x", [(i, (i + s) % 4) for i in range(4)]) for s, part in zip((1, 2, 3), away)
    ]
    (home,) = attention(
        (0,), True, ids, block_table, prefix_len, [query], pools, w_uk, w_uv, (new_latent, new_rope[0])
    )
    head_out = simple(
        combine_kernel, "combine", jax.ShapeDtypeStruct((TOK, HEADS * VD), jnp.bfloat16), [home, *came]
    )
    heads = [head_out] + [flip(head_out, GROUP, 8, m) for m in range(1, 8)]
    partial = simple(
        project_kernel,
        "project",
        [jax.ShapeDtypeStruct((64, 896), jnp.bfloat16)] * 4,
        [ids, *heads, *mine, *other],
        scratch=[
            pltpu.VMEM((4, 896, 512), jnp.bfloat16),
            pltpu.SemaphoreType.DMA((4, 2)),
            pltpu.VMEM((4, 256, 512), jnp.bfloat16),
            pltpu.VMEM((256, 896), jnp.float32),
        ],
        any_from=9,
    )
    sums = [partial[0]] + [
        lax.ppermute(partial[d], "zb", [(i, (i + d) % 4) for i in range(4)]) for d in (1, 2, 3)
    ]
    pieces = simple(
        share_kernel,
        "share",
        [jax.ShapeDtypeStruct((8, 896), jnp.float32)] * 8,
        [ids, *sums],
        scratch=[pltpu.VMEM((64, 896), jnp.float32)],
    )
    pieces = [pieces[0]] + [flip(pieces[m], GROUP, 8, m) for m in range(1, 8)]
    return simple(place_kernel, "place", jax.ShapeDtypeStruct((8, 7168), jnp.bfloat16), [ids, *pieces])


def solution(mesh):
    fine = Mesh(mesh.devices.reshape(2, 4, 2, 4, 2, 2), ("yl", "x", "k", "zb", "z0", "yh"))
    cache, head = ("yl", "x", "k"), ("zb", "z0", "yh")
    return jax.shard_map(
        local,
        mesh=fine,
        in_specs=(
            P(cache, head),
            P(cache, head),
            P(cache, None),
            P(cache, None, None),
            P(cache, None, None),
            P(cache, None, None),
            P(),
            P(),
            P(head, None, None),
            P(head, None, None),
            P(head, cache),
        ),
        out_specs=P(cache + head, None),
        check_vma=False,
    )
```

```python
import functools

import jax
import jax.numpy as jnp
from jax import lax
from jax.experimental import pallas as pl
from jax.experimental.pallas import tpu as pltpu
from jax.sharding import Mesh, PartitionSpec as P

LAT = 512
NOPE = 128
ROPE = 64
VD = 128
BLOCK = 128
HEADS = 4
TOK = 128
ROWS = HEADS * TOK
SLOTS = 4
STEP = 4
LOG2E = 1.4426950408889634
SCALE2 = (NOPE + ROPE) ** -0.5 * LOG2E
LOW = -1e30
STAT = HEADS * VD
MSG = STAT + 128

VMEM = pltpu.VMEM
SMEM = pltpu.SMEM


def dot_nn(a, b):
    return lax.dot_general(a, b, (((1,), (0,)), ((), ())), preferred_element_type=jnp.float32)


def dot_nt(a, b):
    return lax.dot_general(a, b, (((1,), (1,)), ((), ())), preferred_element_type=jnp.float32)


def attention_kernel(slots, own, ids, table, lens, *refs):
    count = len(slots)
    refs = list(refs)

    def take(n):
        got = refs[:n]
        del refs[:n]
        return got

    queries = take(count)
    pools = take(4)
    weights = take(2)
    new_latent, new_rope = take(2) if own else (None, None)
    outs = take(count)
    w_uk, w_uv, keys, rots, sems, weight_sems, found_of, valid_of, q_lat, q_rot, acc, top, tot, latents, levels = refs
    yl, x, k = ids[0], ids[1], ids[2]
    loads = [pltpu.make_async_copy(weights[i], (w_uk, w_uv)[i], weight_sems.at[i]) for i in range(2)]
    for load in loads:
        load.start()

    def fetch(s, src, i, at):
        chunk, part = at // STEP, pl.multiple_of((at % STEP) * BLOCK, BLOCK)
        return (
            pltpu.make_async_copy(
                src.at[pl.ds(pl.multiple_of(i * BLOCK, BLOCK), BLOCK), :],
                keys.at[s, chunk, pl.ds(part, BLOCK), :],
                sems.at[s, at, 0],
            ),
            pltpu.make_async_copy(
                src.at[pl.ds(4 * BLOCK, ROPE), pl.ds(pl.multiple_of(i * BLOCK, BLOCK), BLOCK)],
                rots.at[s, chunk, :, pl.ds(part, BLOCK)],
                sems.at[s, at, 1],
            ),
        )

    for s, slot in enumerate(slots):
        request = yl * 8 + ((x + slot) % 4) * 2 + k
        limit = lens[request]

        def scan(m, carry):
            found, valid = carry
            block = table[request, m]
            owner, i = block >> 2, block & 3
            here = ((owner >> 1) & 3) == x

            @pl.when(here)
            def _():
                source = ((owner >> 3) ^ yl) + 2 * ((owner & 1) ^ k)
                for j in range(4):

                    @pl.when(source == j)
                    def _():
                        for copy in fetch(s, pools[j], i, found):
                            copy.start()

            step = here.astype(jnp.int32)
            return found + step, valid + step * jnp.minimum(limit - m * BLOCK, BLOCK)

        blocks = jnp.minimum((limit + BLOCK - 1) // BLOCK, 32)
        found, valid = lax.fori_loop(0, blocks, scan, (jnp.int32(0), jnp.int32(0)))
        found_of[s] = found
        valid_of[s] = valid

    def clear(s):
        found = found_of[s]
        for extra in range(STEP):
            at = found + extra

            @pl.when(jnp.logical_and(at < jnp.maximum((found + STEP - 1) // STEP, 1) * STEP, at < 16))
            def _():
                part = pl.multiple_of((at % STEP) * BLOCK, BLOCK)
                keys[s, at // STEP, pl.ds(part, BLOCK), :] = jnp.zeros((BLOCK, LAT), jnp.bfloat16)
                rots[s, at // STEP, :, pl.ds(part, BLOCK)] = jnp.zeros((ROPE, BLOCK), jnp.bfloat16)

    for s in range(count):
        clear(s)
    loads[0].wait()
    for h in range(HEADS):
        rows = slice(h * TOK, (h + 1) * TOK)
        part = jnp.concatenate([q[:, h * NOPE : (h + 1) * NOPE] for q in queries], axis=0)
        part = dot_nn(part, w_uk[h]).astype(jnp.bfloat16)
        first = HEADS * NOPE + h * ROPE
        for s in range(count):
            q_lat[s, rows, :] = part[s * TOK : (s + 1) * TOK]
            q_rot[s, rows, :] = queries[s][:, first : first + ROPE]

    def wide(value, times):
        return jnp.concatenate([value] * times, axis=1)

    def begin(score, latent):
        best = jnp.broadcast_to(jnp.max(score, axis=1, keepdims=True), (ROWS, 128))
        times = score.shape[1] // 128
        weight = jnp.exp2((score - wide(best, times)) * SCALE2)
        top[...] = best
        tot[...] = sum(weight[:, i * 128 : (i + 1) * 128] for i in range(times))
        acc[...] = dot_nn(weight.astype(jnp.bfloat16), latent)

    def scores(s, chunk):
        for b in range(STEP):

            @pl.when(chunk * STEP + b < found_of[s])
            def _():
                for copy in fetch(s, pools[0], 0, chunk * STEP + b):
                    copy.wait()

        score = dot_nt(q_lat[s], keys[s, chunk]) + dot_nn(q_rot[s], rots[s, chunk])
        seen = lax.broadcasted_iota(jnp.int32, score.shape, 1) < valid_of[s] - chunk * STEP * BLOCK
        return jnp.where(seen, score, LOW)

    def one_slot(s, carry):
        if own:
            score = dot_nt(q_lat[s], new_latent[...]) + dot_nn(q_rot[s], new_rope[...])
            at = lax.broadcasted_iota(jnp.int32, score.shape, 0) % TOK
            seen = lax.broadcasted_iota(jnp.int32, score.shape, 1) <= at
            begin(jnp.where(seen, score, LOW), new_latent[...])
        else:
            begin(scores(s, 0), keys[s, 0])

        def step(chunk, inner):
            score = scores(s, chunk)
            before = top[...]
            best = jnp.maximum(before, jnp.max(score, axis=1, keepdims=True))
            keep = jnp.exp2((before - best) * SCALE2)
            weight = jnp.exp2((score - wide(best, STEP)) * SCALE2)
            top[...] = best
            tot[...] = tot[...] * keep + sum(weight[:, i * 128 : (i + 1) * 128] for i in range(STEP))
            acc[...] = acc[...] * wide(keep, 4) + dot_nn(weight.astype(jnp.bfloat16), keys[s, chunk])
            return inner

        lax.fori_loop(0 if own else 1, (found_of[s] + STEP - 1) // STEP, step, 0)
        total = jnp.broadcast_to(jnp.sum(tot[...], axis=1, keepdims=True), (ROWS, 128))
        latents[s] = (acc[...] * wide(1.0 / total, 4)).astype(jnp.bfloat16)
        level = top[...] * SCALE2 + jnp.log2(total)
        levels[s] = level if own else jnp.where(found_of[s] > 0, level, LOW)
        return carry

    lax.fori_loop(0, count, one_slot, 0)
    loads[1].wait()
    lane = lax.broadcasted_iota(jnp.int32, (TOK, 128), 1)
    for h in range(HEADS):
        rows = slice(h * TOK, (h + 1) * TOK)
        part = jnp.concatenate([latents[s, rows, :] for s in range(count)], axis=0)
        part = dot_nn(part, w_uv[h]).astype(jnp.bfloat16)
        for s in range(count):
            outs[s][:, h * VD : (h + 1) * VD] = part[s * TOK : (s + 1) * TOK]
    for s in range(count):
        level = levels[s, 0:TOK, :]
        for h in range(1, HEADS):
            level = jnp.where(lane % HEADS == h, levels[s, h * TOK : (h + 1) * TOK, :], level)
        high = level.astype(jnp.bfloat16).astype(jnp.float32)
        middle = (level - high).astype(jnp.bfloat16).astype(jnp.float32)
        low = level - high - middle
        stat = jnp.where(lane < HEADS, high, jnp.where(lane < 2 * HEADS, middle, low))
        outs[s][:, STAT:] = stat.astype(jnp.bfloat16)


def attention(slots, own, ids, table, lens, queries, pools, w_uk, w_uv, fresh):
    count = len(slots)
    full = pl.BlockSpec(memory_space=VMEM)
    scalar = pl.BlockSpec(memory_space=SMEM)
    free = pl.BlockSpec(memory_space=pl.ANY)
    chunks = 16 // STEP
    return pl.pallas_call(
        functools.partial(attention_kernel, slots, own),
        out_shape=[jax.ShapeDtypeStruct((TOK, MSG), jnp.bfloat16)] * count,
        in_specs=[scalar] * 3 + [full] * count + [free] * 6 + [full] * (2 if own else 0),
        out_specs=[full] * count,
        scratch_shapes=[
            pltpu.VMEM((HEADS, NOPE, LAT), jnp.bfloat16),
            pltpu.VMEM((HEADS, LAT, VD), jnp.bfloat16),
            pltpu.VMEM((count, chunks, STEP * BLOCK, LAT), jnp.bfloat16),
            pltpu.VMEM((count, chunks, ROPE, STEP * BLOCK), jnp.bfloat16),
            pltpu.SemaphoreType.DMA((count, 16, 2)),
            pltpu.SemaphoreType.DMA((2,)),
            pltpu.SMEM((count,), jnp.int32),
            pltpu.SMEM((count,), jnp.int32),
            pltpu.VMEM((count, ROWS, LAT), jnp.bfloat16),
            pltpu.VMEM((count, ROWS, ROPE), jnp.bfloat16),
            pltpu.VMEM((ROWS, LAT), jnp.float32),
            pltpu.VMEM((ROWS, 128), jnp.float32),
            pltpu.VMEM((ROWS, 128), jnp.float32),
            pltpu.VMEM((count, ROWS, LAT), jnp.bfloat16),
            pltpu.VMEM((count, ROWS, 128), jnp.float32),
        ],
        compiler_params=pltpu.CompilerParams(vmem_limit_bytes=40 * 2**20),
        cost_estimate=pl.CostEstimate(
            flops=count * 2 * ROWS * 1024 * 1088, bytes_accessed=count * 2**21, transcendentals=count * ROWS * 1024
        ),
        name="attend",
    )(ids, table, lens, *queries, *pools, w_uk, w_uv, *fresh)


def combine_kernel(*refs):
    parts, out = refs[:SLOTS], refs[SLOTS]
    stats = [p[:, STAT:].astype(jnp.float32) for p in parts]
    for h in range(HEADS):
        columns = slice(h * VD, (h + 1) * VD)
        levels = [
            s[:, h : h + 1] + s[:, HEADS + h : HEADS + h + 1] + s[:, 2 * HEADS + h : 2 * HEADS + h + 1]
            for s in stats
        ]
        best = functools.reduce(jnp.maximum, levels)
        shares = [jnp.exp2(v - best) for v in levels]
        inverse = 1.0 / sum(shares)
        out[:, columns] = sum(
            p[:, columns].astype(jnp.float32) * (share * inverse) for p, share in zip(parts, shares)
        ).astype(jnp.bfloat16)


def project_kernel(ids, *refs):
    heads, mine, other = refs[:8], refs[8:12], refs[12:16]
    outs = refs[16:20]
    weights, sems, stacked, total = refs[20:]
    yl, x, k, zb, a = ids[0], ids[1], ids[2], ids[3], ids[4]
    copies = []
    for j in range(4):
        for side, pieces in enumerate((mine, other)):
            first = pl.multiple_of((k ^ side) * 448, 64)
            copy = pltpu.make_async_copy(pieces[j], weights.at[j, pl.ds(first, 448), :], sems.at[j, side])
            copy.start()
            copies.append(copy)
    for m in range(8):
        stacked[a ^ (m & 3), pl.ds(pl.multiple_of((yl ^ (m >> 2)) * TOK, TOK), TOK), :] = heads[m][...]
    for copy in copies:
        copy.wait()
    value = None
    for j in range(4):
        part = dot_nt(stacked[(x + j) % 4], weights[j])
        value = part if value is None else value + part
    total[...] = value
    for d in range(4):
        first = pl.multiple_of(((zb + d) % 4) * 32, 32)
        for half in range(2):
            outs[d][half * 32 : (half + 1) * 32, :] = total[pl.ds(first + half * TOK, 32), :].astype(jnp.bfloat16)


def share_kernel(*refs):
    parts, out = refs[:4], refs[4]
    out[...] = sum(p[...].astype(jnp.float32) for p in parts).reshape(8, 8, 896)


def place_kernel(parts, out):
    for m in range(8):
        out[:, m * 896 : (m + 1) * 896] = parts[m].astype(jnp.bfloat16)


def tie_kernel(*refs):
    pass


def tie(value, *others):
    free = pl.BlockSpec(memory_space=pl.ANY)
    return pl.pallas_call(
        tie_kernel,
        out_shape=jax.ShapeDtypeStruct(value.shape, value.dtype),
        in_specs=[free] * (1 + len(others)),
        out_specs=free,
        input_output_aliases={0: 0},
        name="tie",
    )(value, *others)


def simple(kernel, name, out_shape, args, scratch=(), any_from=None):
    full = pl.BlockSpec(memory_space=VMEM)
    specs = [
        pl.BlockSpec(memory_space=SMEM)
        if arg.dtype == jnp.int32
        else pl.BlockSpec(memory_space=pl.ANY)
        if any_from is not None and i >= any_from
        else full
        for i, arg in enumerate(args)
    ]
    return pl.pallas_call(
        kernel,
        out_shape=out_shape,
        in_specs=specs,
        out_specs=jax.tree.map(lambda _: full, out_shape),
        scratch_shapes=scratch,
        compiler_params=pltpu.CompilerParams(vmem_limit_bytes=40 * 2**20),
        name=name,
    )(*args)


GROUP = ("yl", "z0", "yh")


def turn(value, axis, size, shift):
    return lax.ppermute(value, axis, [((i + shift) % size, i) for i in range(size)])


def flip(value, axis, size, bits):
    return lax.ppermute(value, axis, [(i, i ^ bits) for i in range(size)])


def local(
    q_nope,
    q_rope,
    new_latent,
    new_rope,
    pool_latent,
    pool_rope,
    block_table,
    prefix_len,
    w_uk,
    w_uv,
    w_out,
):
    ids = jnp.stack(
        [
            lax.axis_index("yl"),
            lax.axis_index("x"),
            lax.axis_index("k"),
            lax.axis_index("zb"),
            lax.axis_index("z0") * 2 + lax.axis_index("yh"),
        ]
    ).astype(jnp.int32)
    query = jnp.concatenate([q_nope, q_rope], axis=1)
    pool = jnp.concatenate(
        [pool_latent.reshape(4 * BLOCK, LAT), jnp.transpose(pool_rope, (1, 0, 2)).reshape(ROPE, 4 * BLOCK)], axis=0
    )
    weight = w_out.T

    pool_y = flip(pool, "yl", 2, 1)
    queries = [turn(query, "x", 4, s) for s in (1, 2, 3)]
    pool_k = flip(pool, "k", 2, 1)
    pool_y = tie(pool_y, pool_k, *queries)
    pool_yk = flip(pool_y, "k", 2, 1)
    pools = [pool, pool_y, pool_k, pool_yk]

    turned = lax.ppermute(
        weight, ("x", "z0", "yh"), [(i * 4 + j, j * 4 + i) for i in range(4) for j in range(4)]
    )
    mine = [turned] + [turn(turned, "x", 4, s) for s in (1, 2, 3)]
    other = [flip(w, "k", 2, 1) for w in mine]

    away = attention((1, 2, 3), False, ids, block_table, prefix_len, queries, pools, w_uk, w_uv, ())
    came = [
        lax.ppermute(part, "x", [(i, (i + s) % 4) for i in range(4)]) for s, part in zip((1, 2, 3), away)
    ]
    (home,) = attention(
        (0,), True, ids, block_table, prefix_len, [query], pools, w_uk, w_uv, (new_latent, new_rope[0])
    )
    head_out = simple(
        combine_kernel, "combine", jax.ShapeDtypeStruct((TOK, HEADS * VD), jnp.bfloat16), [home, *came]
    )
    heads = [head_out] + [flip(head_out, GROUP, 8, m) for m in range(1, 8)]
    partial = simple(
        project_kernel,
        "project",
        [jax.ShapeDtypeStruct((64, 896), jnp.bfloat16)] * 4,
        [ids, *heads, *mine, *other],
        scratch=[
            pltpu.VMEM((4, 896, 512), jnp.bfloat16),
            pltpu.SemaphoreType.DMA((4, 2)),
            pltpu.VMEM((4, 256, 512), jnp.bfloat16),
            pltpu.VMEM((256, 896), jnp.float32),
        ],
        any_from=9,
    )
    sums = [partial[0]] + [
        lax.ppermute(partial[d], "zb", [(i, (i + d) % 4) for i in range(4)]) for d in (1, 2, 3)
    ]
    pieces = simple(share_kernel, "share", jax.ShapeDtypeStruct((8, 8, 896), jnp.float32), sums)
    pieces = lax.all_to_all(pieces, GROUP, 0, 0, tiled=True)
    return simple(place_kernel, "place", jax.ShapeDtypeStruct((8, 7168), jnp.bfloat16), [pieces])


def solution(mesh):
    fine = Mesh(mesh.devices.reshape(2, 4, 2, 4, 2, 2), ("yl", "x", "k", "zb", "z0", "yh"))
    cache, head = ("yl", "x", "k"), ("zb", "z0", "yh")
    return jax.shard_map(
        local,
        mesh=fine,
        in_specs=(
            P(cache, head),
            P(cache, head),
            P(cache, None),
            P(cache, None, None),
            P(cache, None, None),
            P(cache, None, None),
            P(),
            P(),
            P(head, None, None),
            P(head, None, None),
            P(head, cache),
        ),
        out_specs=P(cache + head, None),
        check_vma=False,
    )
```

```python
import functools

import jax
import jax.numpy as jnp
from jax import lax
from jax.experimental import pallas as pl
from jax.experimental.pallas import tpu as pltpu
from jax.sharding import Mesh, PartitionSpec as P

LAT = 512
NOPE = 128
ROPE = 64
VD = 128
BLOCK = 128
HEADS = 4
TOK = 128
ROWS = HEADS * TOK
SLOTS = 4
STEP = 4
LOG2E = 1.4426950408889634
SCALE2 = (NOPE + ROPE) ** -0.5 * LOG2E
LOW = -1e30
STAT = HEADS * VD
MSG = STAT + 128

VMEM = pltpu.VMEM
SMEM = pltpu.SMEM


def dot_nn(a, b):
    return lax.dot_general(a, b, (((1,), (0,)), ((), ())), preferred_element_type=jnp.float32)


def dot_nt(a, b):
    return lax.dot_general(a, b, (((1,), (1,)), ((), ())), preferred_element_type=jnp.float32)


def prepare_kernel(ids, table, lens, *refs):
    queries = refs[:SLOTS]
    weight, q_lat, q_rot, lists, counts, w_uk, sem = refs[SLOTS:]
    yl, x, k = ids[0], ids[1], ids[2]
    load = pltpu.make_async_copy(weight, w_uk, sem)
    load.start()
    for s in range(SLOTS):
        limit = lens[yl * 8 + ((x + s) % 4) * 2 + k]

        def scan(m, carry):
            found, valid = carry
            block = table[yl * 8 + ((x + s) % 4) * 2 + k, m]
            owner = block >> 2
            here = ((owner >> 1) & 3) == x

            @pl.when(here)
            def _():
                source = ((owner >> 3) ^ yl) + 2 * ((owner & 1) ^ k)
                lists[s * 16 + found] = source * 4 + (block & 3)

            step = here.astype(jnp.int32)
            return found + step, valid + step * jnp.minimum(limit - m * BLOCK, BLOCK)

        blocks = jnp.minimum((limit + BLOCK - 1) // BLOCK, 32)
        found, valid = lax.fori_loop(0, blocks, scan, (jnp.int32(0), jnp.int32(0)))
        counts[s] = found
        counts[SLOTS + s] = valid
    load.wait()
    for h in range(HEADS):
        rows = slice(h * TOK, (h + 1) * TOK)
        part = jnp.concatenate([q[:, h * NOPE : (h + 1) * NOPE] for q in queries], axis=0)
        part = dot_nn(part, w_uk[h]).astype(jnp.bfloat16)
        first = HEADS * NOPE + h * ROPE
        for s in range(SLOTS):
            q_lat[s, rows, :] = part[s * TOK : (s + 1) * TOK]
            q_rot[s, rows, :] = queries[s][:, first : first + ROPE]


def prepare(ids, table, lens, queries, w_uk):
    full = pl.BlockSpec(memory_space=VMEM)
    scalar = pl.BlockSpec(memory_space=SMEM)
    return pl.pallas_call(
        prepare_kernel,
        out_shape=[
            jax.ShapeDtypeStruct((SLOTS, ROWS, LAT), jnp.bfloat16),
            jax.ShapeDtypeStruct((SLOTS, ROWS, ROPE), jnp.bfloat16),
            jax.ShapeDtypeStruct((SLOTS * 16,), jnp.int32),
            jax.ShapeDtypeStruct((2 * SLOTS,), jnp.int32),
        ],
        in_specs=[scalar] * 3 + [full] * SLOTS + [pl.BlockSpec(memory_space=pltpu.HBM)],
        out_specs=[full, full, scalar, scalar],
        scratch_shapes=[pltpu.VMEM((HEADS, NOPE, LAT), jnp.bfloat16), pltpu.SemaphoreType.DMA],
        compiler_params=pltpu.CompilerParams(vmem_limit_bytes=40 * 2**20),
        name="prepare",
    )(ids, table, lens, *queries, w_uk)


def attention_kernel(slots, own, lists, counts, q_lat, q_rot, *refs):
    count = len(slots)
    refs = list(refs)

    def take(n):
        got = refs[:n]
        del refs[:n]
        return got

    pools = take(4)
    (weight,) = take(1)
    new_latent, new_rope = take(2) if own else (None, None)
    outs = take(count)
    w_uv, keys, rots, sems, weight_sem, acc, top, tot, latents, levels = refs
    load = pltpu.make_async_copy(weight, w_uv, weight_sem)

    def fetch(s, src, i, at):
        chunk, part = at // STEP, pl.multiple_of((at % STEP) * BLOCK, BLOCK)
        return (
            pltpu.make_async_copy(
                src.at[pl.ds(pl.multiple_of(i * BLOCK, BLOCK), BLOCK), :],
                keys.at[s, chunk, pl.ds(part, BLOCK), :],
                sems.at[s, at, 0],
            ),
            pltpu.make_async_copy(
                src.at[pl.ds(4 * BLOCK, ROPE), pl.ds(pl.multiple_of(i * BLOCK, BLOCK), BLOCK)],
                rots.at[s, chunk, :, pl.ds(part, BLOCK)],
                sems.at[s, at, 1],
            ),
        )

    for s, slot in enumerate(slots):

        def bring(at, carry):
            code = lists[slot * 16 + at]
            for j in range(4):

                @pl.when((code >> 2) == j)
                def _():
                    for copy in fetch(s, pools[j], code & 3, at):
                        copy.start()

            return carry

        lax.fori_loop(0, counts[slot], bring, 0)
        if s == 0:
            load.start()

    for s, slot in enumerate(slots):
        found = counts[slot]
        for extra in range(STEP):
            at = found + extra

            @pl.when(at < jnp.maximum((found + STEP - 1) // STEP, 1) * STEP)
            def _():
                part = pl.multiple_of((at % STEP) * BLOCK, BLOCK)
                keys[s, at // STEP, pl.ds(part, BLOCK), :] = jnp.zeros((BLOCK, LAT), jnp.bfloat16)
                rots[s, at // STEP, :, pl.ds(part, BLOCK)] = jnp.zeros((ROPE, BLOCK), jnp.bfloat16)

    def wide(value, times):
        return jnp.concatenate([value] * times, axis=1)

    def begin(score, latent):
        best = jnp.broadcast_to(jnp.max(score, axis=1, keepdims=True), (ROWS, 128))
        times = score.shape[1] // 128
        weight = jnp.exp2((score - wide(best, times)) * SCALE2)
        top[...] = best
        tot[...] = sum(weight[:, i * 128 : (i + 1) * 128] for i in range(times))
        acc[...] = dot_nn(weight.astype(jnp.bfloat16), latent)

    def scores(s, found, valid, q, r, chunk):
        for b in range(STEP):

            @pl.when(chunk * STEP + b < found)
            def _():
                for copy in fetch(s, pools[0], 0, chunk * STEP + b):
                    copy.wait()

        score = dot_nt(q, keys[s, chunk]) + dot_nn(r, rots[s, chunk])
        seen = lax.broadcasted_iota(jnp.int32, score.shape, 1) < valid - chunk * STEP * BLOCK
        return jnp.where(seen, score, LOW)

    def one_slot(s, carry):
        slot = s + slots[0]
        found, valid = counts[slot], counts[SLOTS + slot]
        q, r = q_lat[slot], q_rot[slot]
        if own:
            score = dot_nt(q, new_latent[...]) + dot_nn(r, new_rope[...])
            at = lax.broadcasted_iota(jnp.int32, score.shape, 0) % TOK
            seen = lax.broadcasted_iota(jnp.int32, score.shape, 1) <= at
            begin(jnp.where(seen, score, LOW), new_latent[...])
        else:
            begin(scores(s, found, valid, q, r, 0), keys[s, 0])

        def step(chunk, inner):
            score = scores(s, found, valid, q_lat[slot], q_rot[slot], chunk)
            before = top[...]
            best = jnp.maximum(before, jnp.max(score, axis=1, keepdims=True))
            keep = jnp.exp2((before - best) * SCALE2)
            weight = jnp.exp2((score - wide(best, STEP)) * SCALE2)
            top[...] = best
            tot[...] = tot[...] * keep + sum(weight[:, i * 128 : (i + 1) * 128] for i in range(STEP))
            acc[...] = acc[...] * wide(keep, 4) + dot_nn(weight.astype(jnp.bfloat16), keys[s, chunk])
            return inner

        lax.fori_loop(0 if own else 1, (found + STEP - 1) // STEP, step, 0)
        total = jnp.broadcast_to(jnp.sum(tot[...], axis=1, keepdims=True), (ROWS, 128))
        latents[s] = (acc[...] * wide(1.0 / total, 4)).astype(jnp.bfloat16)
        level = top[...] * SCALE2 + jnp.log2(total)
        levels[s] = level if own else jnp.where(found > 0, level, LOW)
        return carry

    lax.fori_loop(0, count, one_slot, 0)
    load.wait()
    lane = lax.broadcasted_iota(jnp.int32, (TOK, 128), 1)
    for h in range(HEADS):
        rows = slice(h * TOK, (h + 1) * TOK)
        part = jnp.concatenate([latents[s, rows, :] for s in range(count)], axis=0)
        part = dot_nn(part, w_uv[h]).astype(jnp.bfloat16)
        for s in range(count):
            outs[s][:, h * VD : (h + 1) * VD] = part[s * TOK : (s + 1) * TOK]
    for s in range(count):
        level = levels[s, 0:TOK, :]
        for h in range(1, HEADS):
            level = jnp.where(lane % HEADS == h, levels[s, h * TOK : (h + 1) * TOK, :], level)
        high = level.astype(jnp.bfloat16).astype(jnp.float32)
        middle = (level - high).astype(jnp.bfloat16).astype(jnp.float32)
        low = level - high - middle
        stat = jnp.where(lane < HEADS, high, jnp.where(lane < 2 * HEADS, middle, low))
        outs[s][:, STAT:] = stat.astype(jnp.bfloat16)


def attention(slots, own, lists, counts, q_lat, q_rot, pools, w_uv, fresh):
    count = len(slots)
    full = pl.BlockSpec(memory_space=VMEM)
    scalar = pl.BlockSpec(memory_space=SMEM)
    chunks = 16 // STEP
    return pl.pallas_call(
        functools.partial(attention_kernel, slots, own),
        out_shape=[jax.ShapeDtypeStruct((TOK, MSG), jnp.bfloat16)] * count,
        in_specs=[scalar] * 2
        + [full] * 2
        + [pl.BlockSpec(memory_space=pl.ANY)] * 4
        + [pl.BlockSpec(memory_space=pltpu.HBM)]
        + [full] * (2 if own else 0),
        out_specs=[full] * count,
        scratch_shapes=[
            pltpu.VMEM((HEADS, LAT, VD), jnp.bfloat16),
            pltpu.VMEM((count, chunks, STEP * BLOCK, LAT), jnp.bfloat16),
            pltpu.VMEM((count, chunks, ROPE, STEP * BLOCK), jnp.bfloat16),
            pltpu.SemaphoreType.DMA((count, 16, 2)),
            pltpu.SemaphoreType.DMA,
            pltpu.VMEM((ROWS, LAT), jnp.float32),
            pltpu.VMEM((ROWS, 128), jnp.float32),
            pltpu.VMEM((ROWS, 128), jnp.float32),
            pltpu.VMEM((count, ROWS, LAT), jnp.bfloat16),
            pltpu.VMEM((count, ROWS, 128), jnp.float32),
        ],
        compiler_params=pltpu.CompilerParams(vmem_limit_bytes=40 * 2**20),
        name="attend",
    )(lists, counts, q_lat, q_rot, *pools, w_uv, *fresh)


def combine_kernel(*refs):
    parts, out = refs[:SLOTS], refs[SLOTS]
    stats = [p[:, STAT:].astype(jnp.float32) for p in parts]
    for h in range(HEADS):
        columns = slice(h * VD, (h + 1) * VD)
        levels = [
            s[:, h : h + 1] + s[:, HEADS + h : HEADS + h + 1] + s[:, 2 * HEADS + h : 2 * HEADS + h + 1]
            for s in stats
        ]
        best = functools.reduce(jnp.maximum, levels)
        shares = [jnp.exp2(v - best) for v in levels]
        inverse = 1.0 / sum(shares)
        out[:, columns] = sum(
            p[:, columns].astype(jnp.float32) * (share * inverse) for p, share in zip(parts, shares)
        ).astype(jnp.bfloat16)


def stack_kernel(*refs):
    for d in range(4):
        refs[4][d] = refs[d][...]


def assemble_kernel(ids, mine, other, out):
    k = ids[2]
    for side, pieces in enumerate((mine, other)):
        first = pl.multiple_of((k ^ side) * 448, 64)
        for d in range(4):
            out[d, pl.ds(first, 448), :] = pieces[d]


def project_kernel(ids, *refs):
    heads, weights = refs[:8], refs[8]
    outs, total = refs[9:13], refs[13]
    yl, zb = ids[0], ids[3]
    value = None
    for d in range(4):
        part = dot_nt(jnp.concatenate([heads[d][...], heads[4 + d][...]], axis=0), weights[d])
        value = part if value is None else value + part
    total[pl.ds(pl.multiple_of(yl * TOK, TOK), TOK), :] = value[:TOK]
    total[pl.ds(pl.multiple_of((1 - yl) * TOK, TOK), TOK), :] = value[TOK:]
    for d in range(4):
        first = pl.multiple_of(((zb + d) % 4) * 32, 32)
        for half in range(2):
            outs[d][half * 32 : (half + 1) * 32, :] = total[pl.ds(first + half * TOK, 32), :].astype(jnp.bfloat16)


def share_kernel(*refs):
    parts, out = refs[:4], refs[4]
    out[...] = sum(p[...].astype(jnp.float32) for p in parts).reshape(8, 8, 896)


def place_kernel(ids, parts, out):
    x = ids[1]
    for m in range(8):
        first = ((m // 4) * 4 + (x ^ (m % 4))) * 896
        out[:, pl.ds(pl.multiple_of(first, 128), 896)] = parts[m].astype(jnp.bfloat16)


def hold_kernel(value, *refs):
    refs[-1][...] = value[...]


def tie_kernel(*refs):
    pass


def tie(values, others):
    free = pl.BlockSpec(memory_space=pl.ANY)
    return pl.pallas_call(
        tie_kernel,
        out_shape=[jax.ShapeDtypeStruct(v.shape, v.dtype) for v in values],
        in_specs=[free] * (len(values) + len(others)),
        out_specs=[free] * len(values),
        input_output_aliases={i: i for i in range(len(values))},
        compiler_params=pltpu.CompilerParams(vmem_limit_bytes=2**20),
        name="tie",
    )(*values, *others)


def simple(kernel, name, out_shape, args, scratch=()):
    full = pl.BlockSpec(memory_space=VMEM)
    return pl.pallas_call(
        kernel,
        out_shape=out_shape,
        in_specs=[pl.BlockSpec(memory_space=SMEM) if arg.dtype == jnp.int32 else full for arg in args],
        out_specs=jax.tree.map(lambda _: full, out_shape),
        scratch_shapes=scratch,
        compiler_params=pltpu.CompilerParams(vmem_limit_bytes=40 * 2**20),
        name=name,
    )(*args)


GROUP = ("yl", "z0", "yh")


def turn(value, axis, size, shift):
    return lax.ppermute(value, axis, [((i + shift) % size, i) for i in range(size)])


def flip(value, axis, size, bits):
    return lax.ppermute(value, axis, [(i, i ^ bits) for i in range(size)])


def local(
    q_nope,
    q_rope,
    new_latent,
    new_rope,
    pool_latent,
    pool_rope,
    block_table,
    prefix_len,
    w_uk,
    w_uv,
    w_out,
):
    ids = jnp.stack(
        [
            lax.axis_index("yl"),
            lax.axis_index("x"),
            lax.axis_index("k"),
            lax.axis_index("zb"),
            lax.axis_index("z0") * 2 + lax.axis_index("yh"),
        ]
    ).astype(jnp.int32)
    query = jnp.concatenate([q_nope, q_rope], axis=1)
    pool = jnp.concatenate(
        [pool_latent.reshape(4 * BLOCK, LAT), jnp.transpose(pool_rope, (1, 0, 2)).reshape(ROPE, 4 * BLOCK)], axis=0
    )
    weight = w_out.T

    pool_y = flip(pool, "yl", 2, 1)
    queries = [query] + [turn(query, "x", 4, s) for s in (1, 2, 3)]
    pool_k = flip(pool, "k", 2, 1)
    weight = simple(
        hold_kernel, "hold", jax.ShapeDtypeStruct(weight.shape, weight.dtype), [weight, *queries[1:]]
    )
    (pool_y,) = tie([pool_y], [pool_k, weight])
    pool_yk = flip(pool_y, "k", 2, 1)
    pools = [pool, pool_y, pool_k, pool_yk]
    q_lat, q_rot, lists, counts = prepare(ids, block_table, prefix_len, queries, w_uk)
    mine = [
        lax.ppermute(
            weight,
            ("x", "z0", "yh"),
            [((i ^ a) * 4 + (a ^ d), i * 4 + a) for i in range(4) for a in range(4)],
        )
        for d in range(4)
    ]

    away = attention((1, 2, 3), False, lists, counts, q_lat, q_rot, pools, w_uv, ())
    came = [
        lax.ppermute(part, "x", [(i, (i + s) % 4) for i in range(4)]) for s, part in zip((1, 2, 3), away)
    ]
    (home,) = attention((0,), True, lists, counts, q_lat, q_rot, pools, w_uv, (new_latent, new_rope[0]))
    mine = simple(
        stack_kernel, "stack", jax.ShapeDtypeStruct((4, 448, 512), jnp.bfloat16), tie(mine, [home, *came])
    )
    weights = simple(
        assemble_kernel,
        "assemble",
        jax.ShapeDtypeStruct((4, 896, 512), jnp.bfloat16),
        [ids, mine, flip(mine, "k", 2, 1)],
    )
    head_out = simple(
        combine_kernel, "combine", jax.ShapeDtypeStruct((TOK, HEADS * VD), jnp.bfloat16), [home, *came]
    )
    heads = [head_out] + [flip(head_out, GROUP, 8, m) for m in range(1, 8)]
    partial = simple(
        project_kernel,
        "project",
        [jax.ShapeDtypeStruct((64, 896), jnp.bfloat16)] * 4,
        [ids, *heads, weights],
        scratch=[pltpu.VMEM((256, 896), jnp.float32)],
    )
    sums = [partial[0]] + [
        lax.ppermute(partial[d], "zb", [(i, (i + d) % 4) for i in range(4)]) for d in (1, 2, 3)
    ]
    pieces = simple(share_kernel, "share", jax.ShapeDtypeStruct((8, 8, 896), jnp.float32), sums)
    pieces = lax.all_to_all(pieces, GROUP, 0, 0, tiled=True)
    return simple(place_kernel, "place", jax.ShapeDtypeStruct((8, 7168), jnp.bfloat16), [ids, pieces])


def solution(mesh):
    fine = Mesh(mesh.devices.reshape(2, 4, 2, 4, 2, 2), ("yl", "x", "k", "zb", "z0", "yh"))
    cache, head = ("yl", "x", "k"), ("zb", "z0", "yh")
    return jax.shard_map(
        local,
        mesh=fine,
        in_specs=(
            P(cache, head),
            P(cache, head),
            P(cache, None),
            P(cache, None, None),
            P(cache, None, None),
            P(cache, None, None),
            P(),
            P(),
            P(head, None, None),
            P(head, None, None),
            P(head, cache),
        ),
        out_specs=P(cache + head, None),
        check_vma=False,
    )
```

```python
import functools

import jax
import jax.numpy as jnp
from jax import lax
from jax.experimental import pallas as pl
from jax.experimental.pallas import tpu as pltpu
from jax.sharding import Mesh, PartitionSpec as P

LAT = 512
NOPE = 128
ROPE = 64
VD = 128
BLOCK = 128
HEADS = 4
TOK = 128
ROWS = HEADS * TOK
SLOTS = 4
STEP = 4
LOG2E = 1.4426950408889634
SCALE2 = (NOPE + ROPE) ** -0.5 * LOG2E
LOW = -1e30
STAT = HEADS * VD
MSG = STAT + 128

VMEM = pltpu.VMEM
SMEM = pltpu.SMEM


def dot_nn(a, b):
    return lax.dot_general(a, b, (((1,), (0,)), ((), ())), preferred_element_type=jnp.float32)


def dot_nt(a, b):
    return lax.dot_general(a, b, (((1,), (1,)), ((), ())), preferred_element_type=jnp.float32)


def prepare_kernel(ids, table, lens, *refs):
    queries = refs[:SLOTS]
    weight, q_lat, q_rot, lists, counts, w_uk, sem = refs[SLOTS:]
    yl, x, k = ids[0], ids[1], ids[2]
    load = pltpu.make_async_copy(weight, w_uk, sem)
    load.start()
    for s in range(SLOTS):
        limit = lens[yl * 8 + ((x + s) % 4) * 2 + k]

        def scan(m, carry):
            found, valid = carry
            block = table[yl * 8 + ((x + s) % 4) * 2 + k, m]
            owner = block >> 2
            here = ((owner >> 1) & 3) == x

            @pl.when(here)
            def _():
                source = ((owner >> 3) ^ yl) + 2 * ((owner & 1) ^ k)
                lists[s * 16 + found] = source * 4 + (block & 3)

            step = here.astype(jnp.int32)
            return found + step, valid + step * jnp.minimum(limit - m * BLOCK, BLOCK)

        blocks = jnp.minimum((limit + BLOCK - 1) // BLOCK, 32)
        found, valid = lax.fori_loop(0, blocks, scan, (jnp.int32(0), jnp.int32(0)))
        counts[s] = found
        counts[SLOTS + s] = valid
    load.wait()
    for h in range(HEADS):
        rows = slice(h * TOK, (h + 1) * TOK)
        part = jnp.concatenate([q[:, h * NOPE : (h + 1) * NOPE] for q in queries], axis=0)
        part = dot_nn(part, w_uk[h]).astype(jnp.bfloat16)
        first = HEADS * NOPE + h * ROPE
        for s in range(SLOTS):
            q_lat[s, rows, :] = part[s * TOK : (s + 1) * TOK]
            q_rot[s, rows, :] = queries[s][:, first : first + ROPE]


def prepare(ids, table, lens, queries, w_uk):
    full = pl.BlockSpec(memory_space=VMEM)
    scalar = pl.BlockSpec(memory_space=SMEM)
    return pl.pallas_call(
        prepare_kernel,
        out_shape=[
            jax.ShapeDtypeStruct((SLOTS, ROWS, LAT), jnp.bfloat16),
            jax.ShapeDtypeStruct((SLOTS, ROWS, ROPE), jnp.bfloat16),
            jax.ShapeDtypeStruct((SLOTS * 16,), jnp.int32),
            jax.ShapeDtypeStruct((2 * SLOTS,), jnp.int32),
        ],
        in_specs=[scalar] * 3 + [full] * SLOTS + [pl.BlockSpec(memory_space=pltpu.HBM)],
        out_specs=[full, full, scalar, scalar],
        scratch_shapes=[pltpu.VMEM((HEADS, NOPE, LAT), jnp.bfloat16), pltpu.SemaphoreType.DMA],
        compiler_params=pltpu.CompilerParams(vmem_limit_bytes=40 * 2**20),
        name="prepare",
    )(ids, table, lens, *queries, w_uk)


def attention_kernel(slots, own, lists, counts, q_lat, q_rot, *refs):
    count = len(slots)
    refs = list(refs)

    def take(n):
        got = refs[:n]
        del refs[:n]
        return got

    pools = take(4)
    (weight,) = take(1)
    new_latent, new_rope = take(2) if own else (None, None)
    outs = take(count)
    w_uv, keys, rots, sems, weight_sem, acc, top, tot, latents, levels = refs
    load = pltpu.make_async_copy(weight, w_uv, weight_sem)

    def fetch(s, src, i, at):
        chunk, part = at // STEP, pl.multiple_of((at % STEP) * BLOCK, BLOCK)
        return (
            pltpu.make_async_copy(
                src.at[pl.ds(pl.multiple_of(i * BLOCK, BLOCK), BLOCK), :],
                keys.at[s, chunk, pl.ds(part, BLOCK), :],
                sems.at[s, at, 0],
            ),
            pltpu.make_async_copy(
                src.at[pl.ds(4 * BLOCK, ROPE), pl.ds(pl.multiple_of(i * BLOCK, BLOCK), BLOCK)],
                rots.at[s, chunk, :, pl.ds(part, BLOCK)],
                sems.at[s, at, 1],
            ),
        )

    for s, slot in enumerate(slots):

        def bring(at, carry):
            code = lists[slot * 16 + at]
            for j in range(4):

                @pl.when((code >> 2) == j)
                def _():
                    for copy in fetch(s, pools[j], code & 3, at):
                        copy.start()

            return carry

        lax.fori_loop(0, counts[slot], bring, 0)
        if s == 0:
            load.start()

    for s, slot in enumerate(slots):
        found = counts[slot]
        for extra in range(STEP):
            at = found + extra

            @pl.when(at < jnp.maximum((found + STEP - 1) // STEP, 1) * STEP)
            def _():
                part = pl.multiple_of((at % STEP) * BLOCK, BLOCK)
                keys[s, at // STEP, pl.ds(part, BLOCK), :] = jnp.zeros((BLOCK, LAT), jnp.bfloat16)
                rots[s, at // STEP, :, pl.ds(part, BLOCK)] = jnp.zeros((ROPE, BLOCK), jnp.bfloat16)

    def wide(value, times):
        return jnp.concatenate([value] * times, axis=1)

    def begin(score, latent):
        best = jnp.broadcast_to(jnp.max(score, axis=1, keepdims=True), (ROWS, 128))
        times = score.shape[1] // 128
        weight = jnp.exp2((score - wide(best, times)) * SCALE2)
        top[...] = best
        tot[...] = sum(weight[:, i * 128 : (i + 1) * 128] for i in range(times))
        acc[...] = dot_nn(weight.astype(jnp.bfloat16), latent)

    def scores(s, found, valid, q, r, chunk):
        for b in range(STEP):

            @pl.when(chunk * STEP + b < found)
            def _():
                for copy in fetch(s, pools[0], 0, chunk * STEP + b):
                    copy.wait()

        score = dot_nt(q, keys[s, chunk]) + dot_nn(r, rots[s, chunk])
        seen = lax.broadcasted_iota(jnp.int32, score.shape, 1) < valid - chunk * STEP * BLOCK
        return jnp.where(seen, score, LOW)

    def one_slot(s, carry):
        slot = s + slots[0]
        found, valid = counts[slot], counts[SLOTS + slot]
        q, r = q_lat[slot], q_rot[slot]
        if own:
            score = dot_nt(q, new_latent[...]) + dot_nn(r, new_rope[...])
            at = lax.broadcasted_iota(jnp.int32, score.shape, 0) % TOK
            seen = lax.broadcasted_iota(jnp.int32, score.shape, 1) <= at
            begin(jnp.where(seen, score, LOW), new_latent[...])
        else:
            begin(scores(s, found, valid, q, r, 0), keys[s, 0])

        def step(chunk, inner):
            score = scores(s, found, valid, q_lat[slot], q_rot[slot], chunk)
            before = top[...]
            best = jnp.maximum(before, jnp.max(score, axis=1, keepdims=True))
            keep = jnp.exp2((before - best) * SCALE2)
            weight = jnp.exp2((score - wide(best, STEP)) * SCALE2)
            top[...] = best
            tot[...] = tot[...] * keep + sum(weight[:, i * 128 : (i + 1) * 128] for i in range(STEP))
            acc[...] = acc[...] * wide(keep, 4) + dot_nn(weight.astype(jnp.bfloat16), keys[s, chunk])
            return inner

        lax.fori_loop(0 if own else 1, (found + STEP - 1) // STEP, step, 0)
        total = jnp.broadcast_to(jnp.sum(tot[...], axis=1, keepdims=True), (ROWS, 128))
        latents[s] = (acc[...] * wide(1.0 / total, 4)).astype(jnp.bfloat16)
        level = top[...] * SCALE2 + jnp.log2(total)
        levels[s] = level if own else jnp.where(found > 0, level, LOW)
        return carry

    lax.fori_loop(0, count, one_slot, 0)
    load.wait()
    lane = lax.broadcasted_iota(jnp.int32, (TOK, 128), 1)
    for h in range(HEADS):
        rows = slice(h * TOK, (h + 1) * TOK)
        part = jnp.concatenate([latents[s, rows, :] for s in range(count)], axis=0)
        part = dot_nn(part, w_uv[h]).astype(jnp.bfloat16)
        for s in range(count):
            outs[s][:, h * VD : (h + 1) * VD] = part[s * TOK : (s + 1) * TOK]
    for s in range(count):
        level = levels[s, 0:TOK, :]
        for h in range(1, HEADS):
            level = jnp.where(lane % HEADS == h, levels[s, h * TOK : (h + 1) * TOK, :], level)
        high = level.astype(jnp.bfloat16).astype(jnp.float32)
        middle = (level - high).astype(jnp.bfloat16).astype(jnp.float32)
        low = level - high - middle
        stat = jnp.where(lane < HEADS, high, jnp.where(lane < 2 * HEADS, middle, low))
        outs[s][:, STAT:] = stat.astype(jnp.bfloat16)


def attention(slots, own, lists, counts, q_lat, q_rot, pools, w_uv, fresh):
    count = len(slots)
    full = pl.BlockSpec(memory_space=VMEM)
    scalar = pl.BlockSpec(memory_space=SMEM)
    chunks = 16 // STEP
    return pl.pallas_call(
        functools.partial(attention_kernel, slots, own),
        out_shape=[jax.ShapeDtypeStruct((TOK, MSG), jnp.bfloat16)] * count,
        in_specs=[scalar] * 2
        + [full] * 2
        + [pl.BlockSpec(memory_space=pl.ANY)] * 4
        + [pl.BlockSpec(memory_space=pltpu.HBM)]
        + [full] * (2 if own else 0),
        out_specs=[full] * count,
        scratch_shapes=[
            pltpu.VMEM((HEADS, LAT, VD), jnp.bfloat16),
            pltpu.VMEM((count, chunks, STEP * BLOCK, LAT), jnp.bfloat16),
            pltpu.VMEM((count, chunks, ROPE, STEP * BLOCK), jnp.bfloat16),
            pltpu.SemaphoreType.DMA((count, 16, 2)),
            pltpu.SemaphoreType.DMA,
            pltpu.VMEM((ROWS, LAT), jnp.float32),
            pltpu.VMEM((ROWS, 128), jnp.float32),
            pltpu.VMEM((ROWS, 128), jnp.float32),
            pltpu.VMEM((count, ROWS, LAT), jnp.bfloat16),
            pltpu.VMEM((count, ROWS, 128), jnp.float32),
        ],
        compiler_params=pltpu.CompilerParams(vmem_limit_bytes=40 * 2**20),
        name="attend",
    )(lists, counts, q_lat, q_rot, *pools, w_uv, *fresh)


def combine_kernel(*refs):
    parts, out = refs[:SLOTS], refs[SLOTS]
    stats = [p[:, STAT:].astype(jnp.float32) for p in parts]
    for h in range(HEADS):
        columns = slice(h * VD, (h + 1) * VD)
        levels = [
            s[:, h : h + 1] + s[:, HEADS + h : HEADS + h + 1] + s[:, 2 * HEADS + h : 2 * HEADS + h + 1]
            for s in stats
        ]
        best = functools.reduce(jnp.maximum, levels)
        shares = [jnp.exp2(v - best) for v in levels]
        inverse = 1.0 / sum(shares)
        out[:, columns] = sum(
            p[:, columns].astype(jnp.float32) * (share * inverse) for p, share in zip(parts, shares)
        ).astype(jnp.bfloat16)


def project_kernel(ids, heads, weights, *refs):
    outs, total = refs[:4], refs[4]
    a = ids[4]
    total[...] = dot_nt(heads[...], weights[...])
    for d in range(4):
        first = pl.multiple_of((a ^ d) * 8, 8)
        rows = [total[pl.ds(zb * 32 + first, 8), :] for zb in range(4)]
        outs[d][...] = jnp.concatenate(rows, axis=0).astype(jnp.bfloat16)


def project(ids, heads, weights):
    wide = 1024
    return pl.pallas_call(
        project_kernel,
        out_shape=[jax.ShapeDtypeStruct((32, 7168), jnp.bfloat16)] * 4,
        grid=(7168 // wide,),
        in_specs=[
            pl.BlockSpec(memory_space=SMEM),
            pl.BlockSpec((TOK, 512), lambda j: (0, 0)),
            pl.BlockSpec((wide, 512), lambda j: (j, 0)),
        ],
        out_specs=[pl.BlockSpec((32, wide), lambda j: (0, j))] * 4,
        scratch_shapes=[pltpu.VMEM((TOK, wide), jnp.float32)],
        compiler_params=pltpu.CompilerParams(vmem_limit_bytes=16 * 2**20),
        name="project",
    )(ids, heads, weights)


def share_kernel(ids, *refs):
    parts, outs, total = refs[:4], refs[4:8], refs[8]
    zb = ids[3]
    total[...] = sum(p[...].astype(jnp.float32) for p in parts)
    for d in range(4):
        first = pl.multiple_of(((zb + d) % 4) * 8, 8)
        rows = [total[pl.ds(first, 8), q * 1792 : (q + 1) * 1792] for q in range(4)]
        outs[d][...] = jnp.concatenate(rows, axis=0).astype(jnp.bfloat16)


def place_kernel(*refs):
    parts, out = refs[:4], refs[4]
    total = sum(p[...].astype(jnp.float32) for p in parts)
    for q in range(4):
        out[:, q * 1792 : (q + 1) * 1792] = total[q * 8 : (q + 1) * 8].astype(jnp.bfloat16)


def tie_kernel(*refs):
    pass


def tie(values, others):
    free = pl.BlockSpec(memory_space=pl.ANY)
    return pl.pallas_call(
        tie_kernel,
        out_shape=[jax.ShapeDtypeStruct(v.shape, v.dtype) for v in values],
        in_specs=[free] * (len(values) + len(others)),
        out_specs=[free] * len(values),
        input_output_aliases={i: i for i in range(len(values))},
        compiler_params=pltpu.CompilerParams(vmem_limit_bytes=2**20),
        name="tie",
    )(*values, *others)


def simple(kernel, name, out_shape, args, scratch=()):
    full = pl.BlockSpec(memory_space=VMEM)
    return pl.pallas_call(
        kernel,
        out_shape=out_shape,
        in_specs=[pl.BlockSpec(memory_space=SMEM) if arg.dtype == jnp.int32 else full for arg in args],
        out_specs=jax.tree.map(lambda _: full, out_shape),
        scratch_shapes=scratch,
        compiler_params=pltpu.CompilerParams(vmem_limit_bytes=16 * 2**20),
        name=name,
    )(*args)


def turn(value, axis, size, shift):
    return lax.ppermute(value, axis, [((i + shift) % size, i) for i in range(size)])


def flip(value, axis, size, bits):
    return lax.ppermute(value, axis, [(i, i ^ bits) for i in range(size)])


def local(
    q_nope,
    q_rope,
    new_latent,
    new_rope,
    pool_latent,
    pool_rope,
    block_table,
    prefix_len,
    w_uk,
    w_uv,
    w_out,
):
    ids = jnp.stack(
        [
            lax.axis_index("yl"),
            lax.axis_index("x"),
            lax.axis_index("k"),
            lax.axis_index("zb"),
            lax.axis_index("z0") * 2 + lax.axis_index("yh"),
        ]
    ).astype(jnp.int32)
    query = jnp.concatenate([q_nope, q_rope], axis=1)
    pool = jnp.concatenate(
        [pool_latent.reshape(4 * BLOCK, LAT), jnp.transpose(pool_rope, (1, 0, 2)).reshape(ROPE, 4 * BLOCK)], axis=0
    )
    weights = lax.all_gather(w_out.T, ("yl", "x", "k"), axis=0, tiled=True)

    pool_y = flip(pool, "yl", 2, 1)
    queries = [query] + [turn(query, "x", 4, s) for s in (1, 2, 3)]
    pool_k = flip(pool, "k", 2, 1)
    (pool_y,) = tie([pool_y], [pool_k, *queries[1:]])
    pool_yk = flip(pool_y, "k", 2, 1)
    pools = [pool, pool_y, pool_k, pool_yk]
    q_lat, q_rot, lists, counts = prepare(ids, block_table, prefix_len, queries, w_uk)

    away = attention((1, 2, 3), False, lists, counts, q_lat, q_rot, pools, w_uv, ())
    came = [
        lax.ppermute(part, "x", [(i, (i + s) % 4) for i in range(4)]) for s, part in zip((1, 2, 3), away)
    ]
    (home,) = attention((0,), True, lists, counts, q_lat, q_rot, pools, w_uv, (new_latent, new_rope[0]))
    head_out = simple(
        combine_kernel, "combine", jax.ShapeDtypeStruct((TOK, HEADS * VD), jnp.bfloat16), [home, *came]
    )
    partial = project(ids, head_out, weights)
    sums = [partial[0]] + [flip(partial[d], ("z0", "yh"), 4, d) for d in (1, 2, 3)]
    pieces = simple(
        share_kernel,
        "share",
        [jax.ShapeDtypeStruct((32, 1792), jnp.bfloat16)] * 4,
        [ids, *sums],
        scratch=[pltpu.VMEM((32, 7168), jnp.float32)],
    )
    pieces = [pieces[0]] + [
        lax.ppermute(pieces[d], "zb", [(i, (i + d) % 4) for i in range(4)]) for d in (1, 2, 3)
    ]
    return simple(place_kernel, "place", jax.ShapeDtypeStruct((8, 7168), jnp.bfloat16), pieces)


def solution(mesh):
    fine = Mesh(mesh.devices.reshape(2, 4, 2, 4, 2, 2), ("yl", "x", "k", "zb", "z0", "yh"))
    cache, head = ("yl", "x", "k"), ("zb", "z0", "yh")
    return jax.shard_map(
        local,
        mesh=fine,
        in_specs=(
            P(cache, head),
            P(cache, head),
            P(cache, None),
            P(cache, None, None),
            P(cache, None, None),
            P(cache, None, None),
            P(),
            P(),
            P(head, None, None),
            P(head, None, None),
            P(head, cache),
        ),
        out_specs=P(cache + head, None),
        check_vma=False,
    )
```

```python
import functools

import jax
import jax.numpy as jnp
from jax import lax
from jax.experimental import pallas as pl
from jax.experimental.pallas import tpu as pltpu
from jax.sharding import Mesh, PartitionSpec as P

LAT = 512
NOPE = 128
ROPE = 64
VD = 128
BLOCK = 128
HEADS = 4
TOK = 128
ROWS = HEADS * TOK
SLOTS = 4
STEP = 4
LOG2E = 1.4426950408889634
SCALE2 = (NOPE + ROPE) ** -0.5 * LOG2E
LOW = -1e30
STAT = HEADS * VD
MSG = STAT + 128

VMEM = pltpu.VMEM
SMEM = pltpu.SMEM


def dot_nn(a, b):
    return lax.dot_general(a, b, (((1,), (0,)), ((), ())), preferred_element_type=jnp.float32)


def dot_nt(a, b):
    return lax.dot_general(a, b, (((1,), (1,)), ((), ())), preferred_element_type=jnp.float32)


def prepare_kernel(ids, table, lens, *refs):
    queries = refs[:SLOTS]
    weight, q_lat, q_rot, lists, counts, w_uk, sem = refs[SLOTS:]
    yl, x, k = ids[0], ids[1], ids[2]
    load = pltpu.make_async_copy(weight, w_uk, sem)
    load.start()
    for s in range(SLOTS):
        limit = lens[yl * 8 + ((x + s) % 4) * 2 + k]

        def scan(m, carry):
            found, valid = carry
            block = table[yl * 8 + ((x + s) % 4) * 2 + k, m]
            owner = block >> 2
            here = ((owner >> 1) & 3) == x

            @pl.when(here)
            def _():
                source = ((owner >> 3) ^ yl) + 2 * ((owner & 1) ^ k)
                lists[s * 16 + found] = source * 4 + (block & 3)

            step = here.astype(jnp.int32)
            return found + step, valid + step * jnp.minimum(limit - m * BLOCK, BLOCK)

        blocks = jnp.minimum((limit + BLOCK - 1) // BLOCK, 32)
        found, valid = lax.fori_loop(0, blocks, scan, (jnp.int32(0), jnp.int32(0)))
        counts[s] = found
        counts[SLOTS + s] = valid
    load.wait()
    for h in range(HEADS):
        rows = slice(h * TOK, (h + 1) * TOK)
        part = jnp.concatenate([q[:, h * NOPE : (h + 1) * NOPE] for q in queries], axis=0)
        part = dot_nn(part, w_uk[h]).astype(jnp.bfloat16)
        first = HEADS * NOPE + h * ROPE
        for s in range(SLOTS):
            q_lat[s, rows, :] = part[s * TOK : (s + 1) * TOK]
            q_rot[s, rows, :] = queries[s][:, first : first + ROPE]


def prepare(ids, table, lens, queries, w_uk):
    full = pl.BlockSpec(memory_space=VMEM)
    scalar = pl.BlockSpec(memory_space=SMEM)
    return pl.pallas_call(
        prepare_kernel,
        out_shape=[
            jax.ShapeDtypeStruct((SLOTS, ROWS, LAT), jnp.bfloat16),
            jax.ShapeDtypeStruct((SLOTS, ROWS, ROPE), jnp.bfloat16),
            jax.ShapeDtypeStruct((SLOTS * 16,), jnp.int32),
            jax.ShapeDtypeStruct((2 * SLOTS,), jnp.int32),
        ],
        in_specs=[scalar] * 3 + [full] * SLOTS + [pl.BlockSpec(memory_space=pltpu.HBM)],
        out_specs=[full, full, scalar, scalar],
        scratch_shapes=[pltpu.VMEM((HEADS, NOPE, LAT), jnp.bfloat16), pltpu.SemaphoreType.DMA],
        compiler_params=pltpu.CompilerParams(vmem_limit_bytes=16 * 2**20),
        name="prepare",
    )(ids, table, lens, *queries, w_uk)


def attention_kernel(slots, own, lists, counts, q_lat, q_rot, *refs):
    count = len(slots)
    refs = list(refs)

    def take(n):
        got = refs[:n]
        del refs[:n]
        return got

    pools = take(4)
    (weight,) = take(1)
    new_latent, new_rope = take(2) if own else (None, None)
    outs = take(count)
    w_uv, keys, rots, sems, weight_sem, acc, top, tot, latents, levels = refs
    load = pltpu.make_async_copy(weight, w_uv, weight_sem)

    def fetch(s, src, i, at):
        chunk, part = at // STEP, pl.multiple_of((at % STEP) * BLOCK, BLOCK)
        return (
            pltpu.make_async_copy(
                src.at[pl.ds(pl.multiple_of(i * BLOCK, BLOCK), BLOCK), :],
                keys.at[s, chunk, pl.ds(part, BLOCK), :],
                sems.at[s, at, 0],
            ),
            pltpu.make_async_copy(
                src.at[pl.ds(4 * BLOCK, ROPE), pl.ds(pl.multiple_of(i * BLOCK, BLOCK), BLOCK)],
                rots.at[s, chunk, :, pl.ds(part, BLOCK)],
                sems.at[s, at, 1],
            ),
        )

    for s, slot in enumerate(slots):

        def bring(at, carry):
            code = lists[slot * 16 + at]
            for j in range(4):

                @pl.when((code >> 2) == j)
                def _():
                    for copy in fetch(s, pools[j], code & 3, at):
                        copy.start()

            return carry

        lax.fori_loop(0, counts[slot], bring, 0)
        if s == 0:
            load.start()

    for s, slot in enumerate(slots):
        found = counts[slot]
        for extra in range(STEP):
            at = found + extra

            @pl.when(at < jnp.maximum((found + STEP - 1) // STEP, 1) * STEP)
            def _():
                part = pl.multiple_of((at % STEP) * BLOCK, BLOCK)
                keys[s, at // STEP, pl.ds(part, BLOCK), :] = jnp.zeros((BLOCK, LAT), jnp.bfloat16)
                rots[s, at // STEP, :, pl.ds(part, BLOCK)] = jnp.zeros((ROPE, BLOCK), jnp.bfloat16)

    def wide(value, times):
        return jnp.concatenate([value] * times, axis=1)

    def begin(score, latent):
        best = jnp.broadcast_to(jnp.max(score, axis=1, keepdims=True), (ROWS, 128))
        times = score.shape[1] // 128
        weight = jnp.exp2((score - wide(best, times)) * SCALE2)
        top[...] = best
        tot[...] = sum(weight[:, i * 128 : (i + 1) * 128] for i in range(times))
        acc[...] = dot_nn(weight.astype(jnp.bfloat16), latent)

    def scores(s, found, valid, q, r, chunk):
        for b in range(STEP):

            @pl.when(chunk * STEP + b < found)
            def _():
                for copy in fetch(s, pools[0], 0, chunk * STEP + b):
                    copy.wait()

        score = dot_nt(q, keys[s, chunk]) + dot_nn(r, rots[s, chunk])
        seen = lax.broadcasted_iota(jnp.int32, score.shape, 1) < valid - chunk * STEP * BLOCK
        return jnp.where(seen, score, LOW)

    def one_slot(s, carry):
        slot = s + slots[0]
        found, valid = counts[slot], counts[SLOTS + slot]
        q, r = q_lat[slot], q_rot[slot]
        if own:
            score = dot_nt(q, new_latent[...]) + dot_nn(r, new_rope[...])
            at = lax.broadcasted_iota(jnp.int32, score.shape, 0) % TOK
            seen = lax.broadcasted_iota(jnp.int32, score.shape, 1) <= at
            begin(jnp.where(seen, score, LOW), new_latent[...])
        else:
            begin(scores(s, found, valid, q, r, 0), keys[s, 0])

        def step(chunk, inner):
            score = scores(s, found, valid, q_lat[slot], q_rot[slot], chunk)
            before = top[...]
            best = jnp.maximum(before, jnp.max(score, axis=1, keepdims=True))
            keep = jnp.exp2((before - best) * SCALE2)
            weight = jnp.exp2((score - wide(best, STEP)) * SCALE2)
            top[...] = best
            tot[...] = tot[...] * keep + sum(weight[:, i * 128 : (i + 1) * 128] for i in range(STEP))
            acc[...] = acc[...] * wide(keep, 4) + dot_nn(weight.astype(jnp.bfloat16), keys[s, chunk])
            return inner

        lax.fori_loop(0 if own else 1, (found + STEP - 1) // STEP, step, 0)
        total = jnp.broadcast_to(jnp.sum(tot[...], axis=1, keepdims=True), (ROWS, 128))
        latents[s] = (acc[...] * wide(1.0 / total, 4)).astype(jnp.bfloat16)
        level = top[...] * SCALE2 + jnp.log2(total)
        levels[s] = level if own else jnp.where(found > 0, level, LOW)
        return carry

    lax.fori_loop(0, count, one_slot, 0)
    load.wait()
    lane = lax.broadcasted_iota(jnp.int32, (TOK, 128), 1)
    for h in range(HEADS):
        rows = slice(h * TOK, (h + 1) * TOK)
        part = jnp.concatenate([latents[s, rows, :] for s in range(count)], axis=0)
        part = dot_nn(part, w_uv[h]).astype(jnp.bfloat16)
        for s in range(count):
            outs[s][:, h * VD : (h + 1) * VD] = part[s * TOK : (s + 1) * TOK]
    for s in range(count):
        level = levels[s, 0:TOK, :]
        for h in range(1, HEADS):
            level = jnp.where(lane % HEADS == h, levels[s, h * TOK : (h + 1) * TOK, :], level)
        high = level.astype(jnp.bfloat16).astype(jnp.float32)
        middle = (level - high).astype(jnp.bfloat16).astype(jnp.float32)
        low = level - high - middle
        stat = jnp.where(lane < HEADS, high, jnp.where(lane < 2 * HEADS, middle, low))
        outs[s][:, STAT:] = stat.astype(jnp.bfloat16)


def attention(slots, own, lists, counts, q_lat, q_rot, pools, w_uv, fresh):
    count = len(slots)
    full = pl.BlockSpec(memory_space=VMEM)
    scalar = pl.BlockSpec(memory_space=SMEM)
    chunks = 16 // STEP
    return pl.pallas_call(
        functools.partial(attention_kernel, slots, own),
        out_shape=[jax.ShapeDtypeStruct((TOK, MSG), jnp.bfloat16)] * count,
        in_specs=[scalar] * 2
        + [full] * 2
        + [pl.BlockSpec(memory_space=pl.ANY)] * 4
        + [pl.BlockSpec(memory_space=pltpu.HBM)]
        + [full] * (2 if own else 0),
        out_specs=[full] * count,
        scratch_shapes=[
            pltpu.VMEM((HEADS, LAT, VD), jnp.bfloat16),
            pltpu.VMEM((count, chunks, STEP * BLOCK, LAT), jnp.bfloat16),
            pltpu.VMEM((count, chunks, ROPE, STEP * BLOCK), jnp.bfloat16),
            pltpu.SemaphoreType.DMA((count, 16, 2)),
            pltpu.SemaphoreType.DMA,
            pltpu.VMEM((ROWS, LAT), jnp.float32),
            pltpu.VMEM((ROWS, 128), jnp.float32),
            pltpu.VMEM((ROWS, 128), jnp.float32),
            pltpu.VMEM((count, ROWS, LAT), jnp.bfloat16),
            pltpu.VMEM((count, ROWS, 128), jnp.float32),
        ],
        compiler_params=pltpu.CompilerParams(vmem_limit_bytes=24 * 2**20),
        name="attend",
    )(lists, counts, q_lat, q_rot, *pools, w_uv, *fresh)


def combine_kernel(*refs):
    parts, out = refs[:SLOTS], refs[SLOTS]
    stats = [p[:, STAT:].astype(jnp.float32) for p in parts]
    for h in range(HEADS):
        columns = slice(h * VD, (h + 1) * VD)
        levels = [
            s[:, h : h + 1] + s[:, HEADS + h : HEADS + h + 1] + s[:, 2 * HEADS + h : 2 * HEADS + h + 1]
            for s in stats
        ]
        best = functools.reduce(jnp.maximum, levels)
        shares = [jnp.exp2(v - best) for v in levels]
        inverse = 1.0 / sum(shares)
        out[:, columns] = sum(
            p[:, columns].astype(jnp.float32) * (share * inverse) for p, share in zip(parts, shares)
        ).astype(jnp.bfloat16)


def stack_kernel(*refs):
    for d in range(4):
        refs[4][d] = refs[d][...]


def assemble_kernel(ids, mine, other, out):
    k = ids[2]
    for side, pieces in enumerate((mine, other)):
        first = pl.multiple_of((k ^ side) * 448, 64)
        for d in range(4):
            out[d, pl.ds(first, 448), :] = pieces[d]


def project_kernel(ids, *refs):
    heads, weights = refs[:8], refs[8]
    outs, total = refs[9:13], refs[13]
    yl, zb = ids[0], ids[3]
    value = None
    for d in range(4):
        part = dot_nt(jnp.concatenate([heads[d][...], heads[4 + d][...]], axis=0), weights[d])
        value = part if value is None else value + part
    total[pl.ds(pl.multiple_of(yl * TOK, TOK), TOK), :] = value[:TOK]
    total[pl.ds(pl.multiple_of((1 - yl) * TOK, TOK), TOK), :] = value[TOK:]
    for d in range(4):
        first = pl.multiple_of(((zb + d) % 4) * 32, 32)
        for half in range(2):
            outs[d][half * 32 : (half + 1) * 32, :] = total[pl.ds(first + half * TOK, 32), :].astype(jnp.bfloat16)


def share_kernel(*refs):
    parts, out = refs[:4], refs[4]
    out[...] = sum(p[...].astype(jnp.float32) for p in parts).reshape(8, 8, 896)


def place_kernel(ids, parts, out):
    x = ids[1]
    for m in range(8):
        first = ((m // 4) * 4 + (x ^ (m % 4))) * 896
        out[:, pl.ds(pl.multiple_of(first, 128), 896)] = parts[m].astype(jnp.bfloat16)


def tie_kernel(*refs):
    pass


def tie(values, others):
    free = pl.BlockSpec(memory_space=pl.ANY)
    return pl.pallas_call(
        tie_kernel,
        out_shape=[jax.ShapeDtypeStruct(v.shape, v.dtype) for v in values],
        in_specs=[free] * (len(values) + len(others)),
        out_specs=[free] * len(values),
        input_output_aliases={i: i for i in range(len(values))},
        compiler_params=pltpu.CompilerParams(vmem_limit_bytes=2**20),
        name="tie",
    )(*values, *others)


def simple(kernel, name, out_shape, args, scratch=()):
    full = pl.BlockSpec(memory_space=VMEM)
    return pl.pallas_call(
        kernel,
        out_shape=out_shape,
        in_specs=[pl.BlockSpec(memory_space=SMEM) if arg.dtype == jnp.int32 else full for arg in args],
        out_specs=jax.tree.map(lambda _: full, out_shape),
        scratch_shapes=scratch,
        compiler_params=pltpu.CompilerParams(vmem_limit_bytes=16 * 2**20),
        name=name,
    )(*args)


GROUP = ("yl", "z0", "yh")


def turn(value, axis, size, shift):
    return lax.ppermute(value, axis, [((i + shift) % size, i) for i in range(size)])


def flip(value, axis, size, bits):
    return lax.ppermute(value, axis, [(i, i ^ bits) for i in range(size)])


def local(
    q_nope,
    q_rope,
    new_latent,
    new_rope,
    pool_latent,
    pool_rope,
    block_table,
    prefix_len,
    w_uk,
    w_uv,
    w_out,
):
    ids = jnp.stack(
        [
            lax.axis_index("yl"),
            lax.axis_index("x"),
            lax.axis_index("k"),
            lax.axis_index("zb"),
            lax.axis_index("z0") * 2 + lax.axis_index("yh"),
        ]
    ).astype(jnp.int32)
    query = jnp.concatenate([q_nope, q_rope], axis=1)
    pool = jnp.concatenate(
        [pool_latent.reshape(4 * BLOCK, LAT), jnp.transpose(pool_rope, (1, 0, 2)).reshape(ROPE, 4 * BLOCK)], axis=0
    )
    weight = w_out.T

    def piece(value, d):
        pairs = [((i ^ a) * 4 + (a ^ d), i * 4 + a) for i in range(4) for a in range(4)]
        return lax.ppermute(value, ("x", "z0", "yh"), pairs)

    queries = [query] + [turn(query, "x", 4, s) for s in (1, 2, 3)]
    pool_y = flip(pool, "yl", 2, 1)
    mine = [piece(weight, 0)]
    mine[0], weight = tie([mine[0], weight], queries[1:])
    mine += [piece(weight, d) for d in (1, 2, 3)]
    q_lat, q_rot, lists, counts = prepare(ids, block_table, prefix_len, queries, w_uk)
    pool, pool_y = tie([pool, pool_y], [q_lat])
    pool_k = flip(pool, "k", 2, 1)
    pool_yk = flip(pool_y, "k", 2, 1)
    pools = [pool, pool_y, pool_k, pool_yk]

    away = attention((1, 2, 3), False, lists, counts, q_lat, q_rot, pools, w_uv, ())
    came = [
        lax.ppermute(part, "x", [(i, (i + s) % 4) for i in range(4)]) for s, part in zip((1, 2, 3), away)
    ]
    (home,) = attention((0,), True, lists, counts, q_lat, q_rot, pools, w_uv, (new_latent, new_rope[0]))
    mine = simple(
        stack_kernel, "stack", jax.ShapeDtypeStruct((4, 448, 512), jnp.bfloat16), tie(mine, [home, *came])
    )
    weights = simple(
        assemble_kernel,
        "assemble",
        jax.ShapeDtypeStruct((4, 896, 512), jnp.bfloat16),
        [ids, mine, flip(mine, "k", 2, 1)],
    )
    head_out = simple(
        combine_kernel, "combine", jax.ShapeDtypeStruct((TOK, HEADS * VD), jnp.bfloat16), [home, *came]
    )
    heads = [head_out] + [flip(head_out, GROUP, 8, m) for m in range(1, 8)]
    partial = simple(
        project_kernel,
        "project",
        [jax.ShapeDtypeStruct((64, 896), jnp.bfloat16)] * 4,
        [ids, *heads, weights],
        scratch=[pltpu.VMEM((256, 896), jnp.float32)],
    )
    sums = [partial[0]] + [
        lax.ppermute(partial[d], "zb", [(i, (i + d) % 4) for i in range(4)]) for d in (1, 2, 3)
    ]
    pieces = simple(share_kernel, "share", jax.ShapeDtypeStruct((8, 8, 896), jnp.float32), sums)
    pieces = lax.all_to_all(pieces, GROUP, 0, 0, tiled=True)
    return simple(place_kernel, "place", jax.ShapeDtypeStruct((8, 7168), jnp.bfloat16), [ids, pieces])


def solution(mesh):
    fine = Mesh(mesh.devices.reshape(2, 4, 2, 4, 2, 2), ("yl", "x", "k", "zb", "z0", "yh"))
    cache, head = ("yl", "x", "k"), ("zb", "z0", "yh")
    return jax.shard_map(
        local,
        mesh=fine,
        in_specs=(
            P(cache, head),
            P(cache, head),
            P(cache, None),
            P(cache, None, None),
            P(cache, None, None),
            P(cache, None, None),
            P(),
            P(),
            P(head, None, None),
            P(head, None, None),
            P(head, cache),
        ),
        out_specs=P(cache + head, None),
        check_vma=False,
    )
```

```python
import functools

import jax
import jax.numpy as jnp
from jax import lax
from jax.experimental import pallas as pl
from jax.experimental.pallas import tpu as pltpu
from jax.sharding import Mesh, PartitionSpec as P

LAT = 512
NOPE = 128
ROPE = 64
VD = 128
BLOCK = 128
HEADS = 4
TOK = 128
ROWS = HEADS * TOK
SLOTS = 4
STEP = 4
LOG2E = 1.4426950408889634
SCALE2 = (NOPE + ROPE) ** -0.5 * LOG2E
LOW = -1e30
STAT = HEADS * VD
MSG = STAT + 128

VMEM = pltpu.VMEM
SMEM = pltpu.SMEM


def dot_nn(a, b):
    return lax.dot_general(a, b, (((1,), (0,)), ((), ())), preferred_element_type=jnp.float32)


def dot_nt(a, b):
    return lax.dot_general(a, b, (((1,), (1,)), ((), ())), preferred_element_type=jnp.float32)


def prepare_kernel(ids, table, lens, *refs):
    queries = refs[:SLOTS]
    weight, q_lat, q_rot, lists, counts, w_uk, sem = refs[SLOTS:]
    yl, x, k = ids[0], ids[1], ids[2]
    load = pltpu.make_async_copy(weight, w_uk, sem)
    load.start()
    for s in range(SLOTS):
        limit = lens[yl * 8 + ((x + s) % 4) * 2 + k]

        def scan(m, carry):
            found, valid = carry
            block = table[yl * 8 + ((x + s) % 4) * 2 + k, m]
            owner = block >> 2
            here = ((owner >> 1) & 3) == x

            @pl.when(here)
            def _():
                source = ((owner >> 3) ^ yl) + 2 * ((owner & 1) ^ k)
                lists[s * 16 + found] = source * 4 + (block & 3)

            step = here.astype(jnp.int32)
            return found + step, valid + step * jnp.minimum(limit - m * BLOCK, BLOCK)

        blocks = jnp.minimum((limit + BLOCK - 1) // BLOCK, 32)
        found, valid = lax.fori_loop(0, blocks, scan, (jnp.int32(0), jnp.int32(0)))
        counts[s] = found
        counts[SLOTS + s] = valid
    load.wait()
    for h in range(HEADS):
        rows = slice(h * TOK, (h + 1) * TOK)
        part = jnp.concatenate([q[:, h * NOPE : (h + 1) * NOPE] for q in queries], axis=0)
        part = dot_nn(part, w_uk[h]).astype(jnp.bfloat16)
        first = HEADS * NOPE + h * ROPE
        for s in range(SLOTS):
            q_lat[s, rows, :] = part[s * TOK : (s + 1) * TOK]
            q_rot[s, rows, :] = queries[s][:, first : first + ROPE]


def prepare(ids, table, lens, queries, w_uk):
    full = pl.BlockSpec(memory_space=VMEM)
    scalar = pl.BlockSpec(memory_space=SMEM)
    return pl.pallas_call(
        prepare_kernel,
        out_shape=[
            jax.ShapeDtypeStruct((SLOTS, ROWS, LAT), jnp.bfloat16),
            jax.ShapeDtypeStruct((SLOTS, ROWS, ROPE), jnp.bfloat16),
            jax.ShapeDtypeStruct((SLOTS * 16,), jnp.int32),
            jax.ShapeDtypeStruct((2 * SLOTS,), jnp.int32),
        ],
        in_specs=[scalar] * 3 + [full] * SLOTS + [pl.BlockSpec(memory_space=pltpu.HBM)],
        out_specs=[full, full, scalar, scalar],
        scratch_shapes=[pltpu.VMEM((HEADS, NOPE, LAT), jnp.bfloat16), pltpu.SemaphoreType.DMA],
        compiler_params=pltpu.CompilerParams(vmem_limit_bytes=16 * 2**20),
        name="prepare",
    )(ids, table, lens, *queries, w_uk)


def attention_kernel(slots, own, lists, counts, q_lat, q_rot, *refs):
    count = len(slots)
    refs = list(refs)

    def take(n):
        got = refs[:n]
        del refs[:n]
        return got

    pools = take(4)
    (weight,) = take(1)
    new_latent, new_rope = take(2) if own else (None, None)
    outs = take(count)
    w_uv, keys, rots, sems, weight_sem, acc, top, tot, latents, levels = refs
    load = pltpu.make_async_copy(weight, w_uv, weight_sem)

    def fetch(s, src, i, at):
        chunk, part = at // STEP, pl.multiple_of((at % STEP) * BLOCK, BLOCK)
        return (
            pltpu.make_async_copy(
                src.at[pl.ds(pl.multiple_of(i * BLOCK, BLOCK), BLOCK), :],
                keys.at[s, chunk, pl.ds(part, BLOCK), :],
                sems.at[s, at, 0],
            ),
            pltpu.make_async_copy(
                src.at[pl.ds(4 * BLOCK, ROPE), pl.ds(pl.multiple_of(i * BLOCK, BLOCK), BLOCK)],
                rots.at[s, chunk, :, pl.ds(part, BLOCK)],
                sems.at[s, at, 1],
            ),
        )

    for s, slot in enumerate(slots):

        def bring(at, carry):
            code = lists[slot * 16 + at]
            for j in range(4):

                @pl.when((code >> 2) == j)
                def _():
                    for copy in fetch(s, pools[j], code & 3, at):
                        copy.start()

            return carry

        lax.fori_loop(0, counts[slot], bring, 0)
        if s == 0:
            load.start()

    for s, slot in enumerate(slots):
        found = counts[slot]
        for extra in range(STEP):
            at = found + extra

            @pl.when(at < jnp.maximum((found + STEP - 1) // STEP, 1) * STEP)
            def _():
                part = pl.multiple_of((at % STEP) * BLOCK, BLOCK)
                keys[s, at // STEP, pl.ds(part, BLOCK), :] = jnp.zeros((BLOCK, LAT), jnp.bfloat16)
                rots[s, at // STEP, :, pl.ds(part, BLOCK)] = jnp.zeros((ROPE, BLOCK), jnp.bfloat16)

    def wide(value, times):
        return jnp.concatenate([value] * times, axis=1)

    def begin(score, latent):
        best = jnp.broadcast_to(jnp.max(score, axis=1, keepdims=True), (ROWS, 128))
        times = score.shape[1] // 128
        weight = jnp.exp2((score - wide(best, times)) * SCALE2)
        top[...] = best
        tot[...] = sum(weight[:, i * 128 : (i + 1) * 128] for i in range(times))
        acc[...] = dot_nn(weight.astype(jnp.bfloat16), latent)

    def scores(s, found, valid, q, r, chunk):
        for b in range(STEP):

            @pl.when(chunk * STEP + b < found)
            def _():
                for copy in fetch(s, pools[0], 0, chunk * STEP + b):
                    copy.wait()

        score = dot_nt(q, keys[s, chunk]) + dot_nn(r, rots[s, chunk])
        seen = lax.broadcasted_iota(jnp.int32, score.shape, 1) < valid - chunk * STEP * BLOCK
        return jnp.where(seen, score, LOW)

    def one_slot(s, carry):
        slot = s + slots[0]
        found, valid = counts[slot], counts[SLOTS + slot]
        q, r = q_lat[slot], q_rot[slot]
        if own:
            score = dot_nt(q, new_latent[...]) + dot_nn(r, new_rope[...])
            at = lax.broadcasted_iota(jnp.int32, score.shape, 0) % TOK
            seen = lax.broadcasted_iota(jnp.int32, score.shape, 1) <= at
            begin(jnp.where(seen, score, LOW), new_latent[...])
        else:
            begin(scores(s, found, valid, q, r, 0), keys[s, 0])

        def step(chunk, inner):
            score = scores(s, found, valid, q_lat[slot], q_rot[slot], chunk)
            before = top[...]
            best = jnp.maximum(before, jnp.max(score, axis=1, keepdims=True))
            keep = jnp.exp2((before - best) * SCALE2)
            weight = jnp.exp2((score - wide(best, STEP)) * SCALE2)
            top[...] = best
            tot[...] = tot[...] * keep + sum(weight[:, i * 128 : (i + 1) * 128] for i in range(STEP))
            acc[...] = acc[...] * wide(keep, 4) + dot_nn(weight.astype(jnp.bfloat16), keys[s, chunk])
            return inner

        lax.fori_loop(0 if own else 1, (found + STEP - 1) // STEP, step, 0)
        total = jnp.broadcast_to(jnp.sum(tot[...], axis=1, keepdims=True), (ROWS, 128))
        latents[s] = (acc[...] * wide(1.0 / total, 4)).astype(jnp.bfloat16)
        level = top[...] * SCALE2 + jnp.log2(total)
        levels[s] = level if own else jnp.where(found > 0, level, LOW)
        return carry

    lax.fori_loop(0, count, one_slot, 0)
    load.wait()
    lane = lax.broadcasted_iota(jnp.int32, (TOK, 128), 1)
    for h in range(HEADS):
        rows = slice(h * TOK, (h + 1) * TOK)
        part = jnp.concatenate([latents[s, rows, :] for s in range(count)], axis=0)
        part = dot_nn(part, w_uv[h]).astype(jnp.bfloat16)
        for s in range(count):
            outs[s][:, h * VD : (h + 1) * VD] = part[s * TOK : (s + 1) * TOK]
    for s in range(count):
        level = levels[s, 0:TOK, :]
        for h in range(1, HEADS):
            level = jnp.where(lane % HEADS == h, levels[s, h * TOK : (h + 1) * TOK, :], level)
        high = level.astype(jnp.bfloat16).astype(jnp.float32)
        middle = (level - high).astype(jnp.bfloat16).astype(jnp.float32)
        low = level - high - middle
        stat = jnp.where(lane < HEADS, high, jnp.where(lane < 2 * HEADS, middle, low))
        outs[s][:, STAT:] = stat.astype(jnp.bfloat16)


def attention(slots, own, lists, counts, q_lat, q_rot, pools, w_uv, fresh):
    count = len(slots)
    full = pl.BlockSpec(memory_space=VMEM)
    scalar = pl.BlockSpec(memory_space=SMEM)
    chunks = 16 // STEP
    return pl.pallas_call(
        functools.partial(attention_kernel, slots, own),
        out_shape=[jax.ShapeDtypeStruct((TOK, MSG), jnp.bfloat16)] * count,
        in_specs=[scalar] * 2
        + [full] * 2
        + [pl.BlockSpec(memory_space=pl.ANY)] * 4
        + [pl.BlockSpec(memory_space=pltpu.HBM)]
        + [full] * (2 if own else 0),
        out_specs=[full] * count,
        scratch_shapes=[
            pltpu.VMEM((HEADS, LAT, VD), jnp.bfloat16),
            pltpu.VMEM((count, chunks, STEP * BLOCK, LAT), jnp.bfloat16),
            pltpu.VMEM((count, chunks, ROPE, STEP * BLOCK), jnp.bfloat16),
            pltpu.SemaphoreType.DMA((count, 16, 2)),
            pltpu.SemaphoreType.DMA,
            pltpu.VMEM((ROWS, LAT), jnp.float32),
            pltpu.VMEM((ROWS, 128), jnp.float32),
            pltpu.VMEM((ROWS, 128), jnp.float32),
            pltpu.VMEM((count, ROWS, LAT), jnp.bfloat16),
            pltpu.VMEM((count, ROWS, 128), jnp.float32),
        ],
        compiler_params=pltpu.CompilerParams(vmem_limit_bytes=24 * 2**20),
        name="attend",
    )(lists, counts, q_lat, q_rot, *pools, w_uv, *fresh)


def combine_kernel(ids, *refs):
    parts, outs, total = refs[:SLOTS], refs[SLOTS : SLOTS + 4], refs[SLOTS + 4]
    a = ids[4]
    stats = [p[:, STAT:].astype(jnp.float32) for p in parts]
    for h in range(HEADS):
        columns = slice(h * VD, (h + 1) * VD)
        levels = [
            s[:, h : h + 1] + s[:, HEADS + h : HEADS + h + 1] + s[:, 2 * HEADS + h : 2 * HEADS + h + 1]
            for s in stats
        ]
        best = functools.reduce(jnp.maximum, levels)
        shares = [jnp.exp2(v - best) for v in levels]
        inverse = 1.0 / sum(shares)
        total[:, columns] = sum(
            p[:, columns].astype(jnp.float32) * (share * inverse) for p, share in zip(parts, shares)
        )
    for d in range(4):
        first = pl.multiple_of((a ^ d) * 8, 8)
        rows = [total[pl.ds(first + q * 32, 8), :] for q in range(4)]
        outs[d][...] = jnp.concatenate(rows, axis=0).astype(jnp.bfloat16)


def join_kernel(*refs):
    for d in range(4):
        refs[4][:, d * 512 : (d + 1) * 512] = refs[d][...]


def pair_kernel(one, two, out):
    out[0] = one[...]
    out[1] = two[...]


def project_kernel(ids, *refs):
    heads, mine, other = refs[:4], refs[4:9], refs[9:14]
    outs, total = refs[14:18], refs[18]
    zb = ids[3]
    rows = jnp.concatenate([h[...] for h in heads], axis=0)
    for side_y in range(2):
        sides = []
        for pieces in (mine, other):
            value = None
            for d in range(4):
                m, dz = side_y * 2 + (d & 1), d >> 1
                weight = pieces[3 + dz][...] if m == 1 else pieces[max(m - 1, 0)][dz]
                part = dot_nt(rows[:, d * 512 : (d + 1) * 512], weight)
                value = part if value is None else value + part
            sides.append(value)
        total[:, side_y * 896 : (side_y + 1) * 896] = jnp.concatenate(sides, axis=1)
    for d in range(4):
        first = pl.multiple_of(((zb + d) % 4) * 8, 8)
        parts = [total[pl.ds(first + s * 32, 8), :] for s in range(4)]
        outs[d][...] = jnp.concatenate(parts, axis=0).astype(jnp.bfloat16)


def share_kernel(*refs):
    total = sum(p[...].astype(jnp.float32) for p in refs[:4])
    for s in range(4):
        refs[4 + s][...] = total[s * 8 : (s + 1) * 8]


def place_kernel(ids, *refs):
    parts, out = refs[:4], refs[4]
    yl, x, k = ids[0], ids[1], ids[2]
    for s in range(4):
        for side_y in range(2):
            first = ((yl ^ side_y) * 4 + (x - s + 4) % 4) * 896
            columns = pl.ds(pl.multiple_of(first, 128), 896)
            value = parts[s][:, side_y * 896 : (side_y + 1) * 896]
            swapped = jnp.concatenate([value[:, 448:], value[:, :448]], axis=1)
            out[:, columns] = jnp.where(k == 0, value, swapped).astype(jnp.bfloat16)


def tie_kernel(*refs):
    pass


def tie(values, others):
    free = pl.BlockSpec(memory_space=pl.ANY)
    return pl.pallas_call(
        tie_kernel,
        out_shape=[jax.ShapeDtypeStruct(v.shape, v.dtype) for v in values],
        in_specs=[free] * (len(values) + len(others)),
        out_specs=[free] * len(values),
        input_output_aliases={i: i for i in range(len(values))},
        compiler_params=pltpu.CompilerParams(vmem_limit_bytes=2**20),
        name="tie",
    )(*values, *others)


def simple(kernel, name, out_shape, args, scratch=()):
    full = pl.BlockSpec(memory_space=VMEM)
    return pl.pallas_call(
        kernel,
        out_shape=out_shape,
        in_specs=[pl.BlockSpec(memory_space=SMEM) if arg.dtype == jnp.int32 else full for arg in args],
        out_specs=jax.tree.map(lambda _: full, out_shape),
        scratch_shapes=scratch,
        compiler_params=pltpu.CompilerParams(vmem_limit_bytes=16 * 2**20),
        name=name,
    )(*args)


def turn(value, axis, size, shift):
    return lax.ppermute(value, axis, [((i + shift) % size, i) for i in range(size)])


def flip(value, axis, size, bits):
    return lax.ppermute(value, axis, [(i, i ^ bits) for i in range(size)])


def local(
    q_nope,
    q_rope,
    new_latent,
    new_rope,
    pool_latent,
    pool_rope,
    block_table,
    prefix_len,
    w_uk,
    w_uv,
    w_out,
):
    ids = jnp.stack(
        [
            lax.axis_index("yl"),
            lax.axis_index("x"),
            lax.axis_index("k"),
            lax.axis_index("zb"),
            lax.axis_index("z0") * 2 + lax.axis_index("yh"),
        ]
    ).astype(jnp.int32)
    query = jnp.concatenate([q_nope, q_rope], axis=1)
    pool = jnp.concatenate(
        [pool_latent.reshape(4 * BLOCK, LAT), jnp.transpose(pool_rope, (1, 0, 2)).reshape(ROPE, 4 * BLOCK)], axis=0
    )
    weight = w_out.T

    queries = [query] + [turn(query, "x", 4, s) for s in (1, 2, 3)]
    pool_y = flip(pool, "yl", 2, 1)
    weight_z = flip(weight, "z0", 2, 1)
    q_lat, q_rot, lists, counts = prepare(ids, block_table, prefix_len, queries, w_uk)
    pool, pool_y, weight_z = tie([pool, pool_y, weight_z], [q_lat])
    pool_k = flip(pool, "k", 2, 1)
    pool_yk = flip(pool_y, "k", 2, 1)
    pair = simple(
        pair_kernel, "pair", jax.ShapeDtypeStruct((2, 448, 512), jnp.bfloat16), [weight, weight_z]
    )
    ring = ("yl", "yh")
    mine = [pair, flip(pair, ring, 4, 2), flip(pair, ring, 4, 3)]
    other = [flip(pair, "k", 2, 1)]
    pool_k, other[0] = tie([pool_k, other[0]], [])
    pools = [pool, pool_y, pool_k, pool_yk]

    away = attention((1, 2, 3), False, lists, counts, q_lat, q_rot, pools, w_uv, ())
    *away, mine[1], mine[2] = tie([*away, mine[1], mine[2]], [])
    far = [flip(mine[2][0], ring, 4, 2), flip(mine[1][1], ring, 4, 3)]
    came = [
        lax.ppermute(part, "x", [(i, (i + s) % 4) for i in range(4)]) for s, part in zip((1, 2, 3), away)
    ]
    (home,) = attention((0,), True, lists, counts, q_lat, q_rot, pools, w_uv, (new_latent, new_rope[0]))
    mine[1], mine[2] = tie([mine[1], mine[2]], [*came, *far, home])
    other += [flip(m, "k", 2, 1) for m in mine[1:]]
    heads = simple(
        combine_kernel,
        "combine",
        [jax.ShapeDtypeStruct((32, HEADS * VD), jnp.bfloat16)] * 4,
        [ids, home, *came],
        scratch=[pltpu.VMEM((TOK, HEADS * VD), jnp.float32)],
    )
    heads = [heads[0]] + [flip(heads[d], ("z0", "yh"), 4, d) for d in (1, 2, 3)]
    heads = simple(join_kernel, "join", jax.ShapeDtypeStruct((32, 2048), jnp.bfloat16), heads)
    heads, *far = tie([heads, *far], other[1:])
    mine += far
    other += [flip(f, "k", 2, 1) for f in far]
    heads = [heads] + [turn(heads, "x", 4, s) for s in (1, 2, 3)]
    partial = simple(
        project_kernel,
        "project",
        [jax.ShapeDtypeStruct((32, 1792), jnp.bfloat16)] * 4,
        [ids, *heads, *mine, *other],
        scratch=[pltpu.VMEM((TOK, 1792), jnp.float32)],
    )
    sums = [partial[0]] + [
        lax.ppermute(partial[d], "zb", [(i, (i + d) % 4) for i in range(4)]) for d in (1, 2, 3)
    ]
    pieces = simple(share_kernel, "share", [jax.ShapeDtypeStruct((8, 1792), jnp.float32)] * 4, sums)
    pieces = [pieces[0]] + [
        lax.ppermute(pieces[s], "x", [(i, (i + s) % 4) for i in range(4)]) for s in (1, 2, 3)
    ]
    return simple(place_kernel, "place", jax.ShapeDtypeStruct((8, 7168), jnp.bfloat16), [ids, *pieces])


def solution(mesh):
    fine = Mesh(mesh.devices.reshape(2, 4, 2, 4, 2, 2), ("yl", "x", "k", "zb", "z0", "yh"))
    cache, head = ("yl", "x", "k"), ("zb", "z0", "yh")
    return jax.shard_map(
        local,
        mesh=fine,
        in_specs=(
            P(cache, head),
            P(cache, head),
            P(cache, None),
            P(cache, None, None),
            P(cache, None, None),
            P(cache, None, None),
            P(),
            P(),
            P(head, None, None),
            P(head, None, None),
            P(head, cache),
        ),
        out_specs=P(cache + head, None),
        check_vma=False,
    )
```

```python
import functools

import jax
import jax.numpy as jnp
from jax import lax
from jax.experimental import pallas as pl
from jax.experimental.pallas import tpu as pltpu
from jax.sharding import Mesh, PartitionSpec as P

LAT = 512
NOPE = 128
ROPE = 64
VD = 128
BLOCK = 128
HEADS = 4
TOK = 128
ROWS = HEADS * TOK
SLOTS = 4
STEP = 4
LOG2E = 1.4426950408889634
SCALE2 = (NOPE + ROPE) ** -0.5 * LOG2E
LOW = -1e30
STAT = HEADS * VD
MSG = STAT + 128

VMEM = pltpu.VMEM
SMEM = pltpu.SMEM


def dot_nn(a, b):
    return lax.dot_general(a, b, (((1,), (0,)), ((), ())), preferred_element_type=jnp.float32)


def dot_nt(a, b):
    return lax.dot_general(a, b, (((1,), (1,)), ((), ())), preferred_element_type=jnp.float32)


def plan_kernel(ids, table, lens, lists, counts):
    yl, x, k = ids[0], ids[1], ids[2]
    for s in range(SLOTS):
        limit = lens[yl * 8 + ((x + s) % 4) * 2 + k]

        def scan(m, carry):
            found, valid = carry
            block = table[yl * 8 + ((x + s) % 4) * 2 + k, m]
            owner = block >> 2
            here = ((owner >> 1) & 3) == x

            @pl.when(here)
            def _():
                source = ((owner >> 3) ^ yl) + 2 * ((owner & 1) ^ k)
                lists[s * 16 + found] = source * 4 + (block & 3)

            step = here.astype(jnp.int32)
            return found + step, valid + step * jnp.minimum(limit - m * BLOCK, BLOCK)

        blocks = jnp.minimum((limit + BLOCK - 1) // BLOCK, 32)
        found, valid = lax.fori_loop(0, blocks, scan, (jnp.int32(0), jnp.int32(0)))
        counts[s] = found
        counts[SLOTS + s] = valid


def plan(ids, table, lens):
    scalar = pl.BlockSpec(memory_space=SMEM)
    return pl.pallas_call(
        plan_kernel,
        out_shape=[jax.ShapeDtypeStruct((SLOTS * 16,), jnp.int32), jax.ShapeDtypeStruct((2 * SLOTS,), jnp.int32)],
        in_specs=[scalar] * 3,
        out_specs=[scalar] * 2,
        compiler_params=pltpu.CompilerParams(vmem_limit_bytes=2**20),
        name="plan",
    )(ids, table, lens)


def prepare_kernel(counts, *refs):
    queries = refs[:SLOTS]
    w_uk, q_lat, q_rot = refs[SLOTS : SLOTS + 3]
    for h in range(HEADS):
        rows = slice(h * TOK, (h + 1) * TOK)
        part = jnp.concatenate([q[:, h * NOPE : (h + 1) * NOPE] for q in queries], axis=0)
        part = dot_nn(part, w_uk[h]).astype(jnp.bfloat16)
        first = HEADS * NOPE + h * ROPE
        for s in range(SLOTS):
            q_lat[s, rows, :] = part[s * TOK : (s + 1) * TOK]
            q_rot[s, rows, :] = queries[s][:, first : first + ROPE]


def attention_kernel(slots, own, lists, counts, q_lat, q_rot, *refs):
    count = len(slots)
    refs = list(refs)

    def take(n):
        got = refs[:n]
        del refs[:n]
        return got

    pools = take(4)
    (weight,) = take(1)
    new_latent, new_rope = take(2) if own else (None, None)
    outs = take(count)
    w_uv, keys, rots, sems, weight_sem, acc, top, tot, latents, levels = refs
    load = pltpu.make_async_copy(weight, w_uv, weight_sem)

    def fetch(s, src, i, at):
        chunk, part = at // STEP, pl.multiple_of((at % STEP) * BLOCK, BLOCK)
        return (
            pltpu.make_async_copy(
                src.at[pl.ds(pl.multiple_of(i * BLOCK, BLOCK), BLOCK), :],
                keys.at[s, chunk, pl.ds(part, BLOCK), :],
                sems.at[s, at, 0],
            ),
            pltpu.make_async_copy(
                src.at[pl.ds(4 * BLOCK, ROPE), pl.ds(pl.multiple_of(i * BLOCK, BLOCK), BLOCK)],
                rots.at[s, chunk, :, pl.ds(part, BLOCK)],
                sems.at[s, at, 1],
            ),
        )

    for s, slot in enumerate(slots):

        def bring(at, carry):
            code = lists[slot * 16 + at]
            for j in range(4):

                @pl.when((code >> 2) == j)
                def _():
                    for copy in fetch(s, pools[j], code & 3, at):
                        copy.start()

            return carry

        lax.fori_loop(0, counts[slot], bring, 0)
        if s == 0:
            load.start()

    for s, slot in enumerate(slots):
        found = counts[slot]
        for extra in range(STEP):
            at = found + extra

            @pl.when(at < jnp.maximum((found + STEP - 1) // STEP, 1) * STEP)
            def _():
                part = pl.multiple_of((at % STEP) * BLOCK, BLOCK)
                keys[s, at // STEP, pl.ds(part, BLOCK), :] = jnp.zeros((BLOCK, LAT), jnp.bfloat16)
                rots[s, at // STEP, :, pl.ds(part, BLOCK)] = jnp.zeros((ROPE, BLOCK), jnp.bfloat16)

    def wide(value, times):
        return jnp.concatenate([value] * times, axis=1)

    def begin(score, latent):
        best = jnp.broadcast_to(jnp.max(score, axis=1, keepdims=True), (ROWS, 128))
        times = score.shape[1] // 128
        weight = jnp.exp2((score - wide(best, times)) * SCALE2)
        top[...] = best
        tot[...] = sum(weight[:, i * 128 : (i + 1) * 128] for i in range(times))
        acc[...] = dot_nn(weight.astype(jnp.bfloat16), latent)

    def scores(s, found, valid, q, r, chunk):
        for b in range(STEP):

            @pl.when(chunk * STEP + b < found)
            def _():
                for copy in fetch(s, pools[0], 0, chunk * STEP + b):
                    copy.wait()

        score = dot_nt(q, keys[s, chunk]) + dot_nn(r, rots[s, chunk])
        seen = lax.broadcasted_iota(jnp.int32, score.shape, 1) < valid - chunk * STEP * BLOCK
        return jnp.where(seen, score, LOW)

    def one_slot(s, carry):
        slot = s + slots[0]
        found, valid = counts[slot], counts[SLOTS + slot]
        q, r = q_lat[slot], q_rot[slot]
        if own:
            score = dot_nt(q, new_latent[...]) + dot_nn(r, new_rope[...])
            at = lax.broadcasted_iota(jnp.int32, score.shape, 0) % TOK
            seen = lax.broadcasted_iota(jnp.int32, score.shape, 1) <= at
            begin(jnp.where(seen, score, LOW), new_latent[...])
        else:
            begin(scores(s, found, valid, q, r, 0), keys[s, 0])

        def step(chunk, inner):
            score = scores(s, found, valid, q_lat[slot], q_rot[slot], chunk)
            before = top[...]
            best = jnp.maximum(before, jnp.max(score, axis=1, keepdims=True))
            keep = jnp.exp2((before - best) * SCALE2)
            weight = jnp.exp2((score - wide(best, STEP)) * SCALE2)
            top[...] = best
            tot[...] = tot[...] * keep + sum(weight[:, i * 128 : (i + 1) * 128] for i in range(STEP))
            acc[...] = acc[...] * wide(keep, 4) + dot_nn(weight.astype(jnp.bfloat16), keys[s, chunk])
            return inner

        lax.fori_loop(0 if own else 1, (found + STEP - 1) // STEP, step, 0)
        total = jnp.broadcast_to(jnp.sum(tot[...], axis=1, keepdims=True), (ROWS, 128))
        latents[s] = (acc[...] * wide(1.0 / total, 4)).astype(jnp.bfloat16)
        level = top[...] * SCALE2 + jnp.log2(total)
        levels[s] = level if own else jnp.where(found > 0, level, LOW)
        return carry

    lax.fori_loop(0, count, one_slot, 0)
    load.wait()
    lane = lax.broadcasted_iota(jnp.int32, (TOK, 128), 1)
    for h in range(HEADS):
        rows = slice(h * TOK, (h + 1) * TOK)
        part = jnp.concatenate([latents[s, rows, :] for s in range(count)], axis=0)
        part = dot_nn(part, w_uv[h]).astype(jnp.bfloat16)
        for s in range(count):
            outs[s][:, h * VD : (h + 1) * VD] = part[s * TOK : (s + 1) * TOK]
    for s in range(count):
        level = levels[s, 0:TOK, :]
        for h in range(1, HEADS):
            level = jnp.where(lane % HEADS == h, levels[s, h * TOK : (h + 1) * TOK, :], level)
        high = level.astype(jnp.bfloat16).astype(jnp.float32)
        middle = (level - high).astype(jnp.bfloat16).astype(jnp.float32)
        low = level - high - middle
        stat = jnp.where(lane < HEADS, high, jnp.where(lane < 2 * HEADS, middle, low))
        outs[s][:, STAT:] = stat.astype(jnp.bfloat16)


def attention(slots, own, lists, counts, q_lat, q_rot, pools, w_uv, fresh):
    count = len(slots)
    full = pl.BlockSpec(memory_space=VMEM)
    scalar = pl.BlockSpec(memory_space=SMEM)
    chunks = 16 // STEP
    return pl.pallas_call(
        functools.partial(attention_kernel, slots, own),
        out_shape=[jax.ShapeDtypeStruct((TOK, MSG), jnp.bfloat16)] * count,
        in_specs=[scalar] * 2
        + [full] * 2
        + [pl.BlockSpec(memory_space=pl.ANY)] * 4
        + [pl.BlockSpec(memory_space=pltpu.HBM)]
        + [full] * (2 if own else 0),
        out_specs=[full] * count,
        scratch_shapes=[
            pltpu.VMEM((HEADS, LAT, VD), jnp.bfloat16),
            pltpu.VMEM((count, chunks, STEP * BLOCK, LAT), jnp.bfloat16),
            pltpu.VMEM((count, chunks, ROPE, STEP * BLOCK), jnp.bfloat16),
            pltpu.SemaphoreType.DMA((count, 16, 2)),
            pltpu.SemaphoreType.DMA,
            pltpu.VMEM((ROWS, LAT), jnp.float32),
            pltpu.VMEM((ROWS, 128), jnp.float32),
            pltpu.VMEM((ROWS, 128), jnp.float32),
            pltpu.VMEM((count, ROWS, LAT), jnp.bfloat16),
            pltpu.VMEM((count, ROWS, 128), jnp.float32),
        ],
        compiler_params=pltpu.CompilerParams(vmem_limit_bytes=24 * 2**20),
        name="attend",
    )(lists, counts, q_lat, q_rot, *pools, w_uv, *fresh)


def combine_kernel(ids, *refs):
    parts, outs, total = refs[:SLOTS], refs[SLOTS : SLOTS + 4], refs[SLOTS + 4]
    a = ids[4]
    stats = [p[:, STAT:].astype(jnp.float32) for p in parts]
    for h in range(HEADS):
        columns = slice(h * VD, (h + 1) * VD)
        levels = [
            s[:, h : h + 1] + s[:, HEADS + h : HEADS + h + 1] + s[:, 2 * HEADS + h : 2 * HEADS + h + 1]
            for s in stats
        ]
        best = functools.reduce(jnp.maximum, levels)
        shares = [jnp.exp2(v - best) for v in levels]
        inverse = 1.0 / sum(shares)
        total[:, columns] = sum(
            p[:, columns].astype(jnp.float32) * (share * inverse) for p, share in zip(parts, shares)
        )
    for d in range(4):
        first = pl.multiple_of((a ^ d) * 8, 8)
        rows = [total[pl.ds(first + q * 32, 8), :] for q in range(4)]
        outs[d][...] = jnp.concatenate(rows, axis=0).astype(jnp.bfloat16)


def join_kernel(*refs):
    for d in range(4):
        refs[4][:, d * 512 : (d + 1) * 512] = refs[d][...]


def pair_kernel(one, two, out):
    out[0] = one[...]
    out[1] = two[...]


def rest_kernel(*refs):
    out = refs[4]
    for i in range(4):
        out[i] = refs[i // 2][i % 2]
    out[4] = refs[2][...]
    out[5] = refs[3][...]


def project_kernel(ids, *refs):
    heads, mine, other = refs[:4], refs[4:6], refs[6:8]
    outs, total = refs[8:12], refs[12]
    zb = ids[3]
    rows = jnp.concatenate([h[...] for h in heads], axis=0)
    for side_y in range(2):
        sides = []
        for pieces in (mine, other):
            value = None
            for d in range(4):
                m, dz = side_y * 2 + (d & 1), d >> 1
                weight = pieces[0][dz] if m == 0 else pieces[1][(0, 4, 0, 2)[m] + dz]
                part = dot_nt(rows[:, d * 512 : (d + 1) * 512], weight)
                value = part if value is None else value + part
            sides.append(value)
        total[:, side_y * 896 : (side_y + 1) * 896] = jnp.concatenate(sides, axis=1)
    for d in range(4):
        first = pl.multiple_of(((zb + d) % 4) * 8, 8)
        parts = [total[pl.ds(first + s * 32, 8), :] for s in range(4)]
        outs[d][...] = jnp.concatenate(parts, axis=0).astype(jnp.bfloat16)


def share_kernel(*refs):
    total = sum(p[...].astype(jnp.float32) for p in refs[:4])
    for s in range(4):
        refs[4 + s][...] = total[s * 8 : (s + 1) * 8]


def place_kernel(ids, *refs):
    parts, out = refs[:4], refs[4]
    yl, x, k = ids[0], ids[1], ids[2]
    for s in range(4):
        for side_y in range(2):
            first = ((yl ^ side_y) * 4 + (x - s + 4) % 4) * 896
            columns = pl.ds(pl.multiple_of(first, 128), 896)
            value = parts[s][:, side_y * 896 : (side_y + 1) * 896]
            swapped = jnp.concatenate([value[:, 448:], value[:, :448]], axis=1)
            out[:, columns] = jnp.where(k == 0, value, swapped).astype(jnp.bfloat16)


def tie_kernel(*refs):
    pass


def tie(values, others):
    free = pl.BlockSpec(memory_space=pl.ANY)
    return pl.pallas_call(
        tie_kernel,
        out_shape=[jax.ShapeDtypeStruct(v.shape, v.dtype) for v in values],
        in_specs=[free] * (len(values) + len(others)),
        out_specs=[free] * len(values),
        input_output_aliases={i: i for i in range(len(values))},
        compiler_params=pltpu.CompilerParams(vmem_limit_bytes=2**20),
        name="tie",
    )(*values, *others)


def simple(kernel, name, out_shape, args, scratch=()):
    full = pl.BlockSpec(memory_space=VMEM)
    return pl.pallas_call(
        kernel,
        out_shape=out_shape,
        in_specs=[pl.BlockSpec(memory_space=SMEM) if arg.dtype == jnp.int32 else full for arg in args],
        out_specs=jax.tree.map(lambda _: full, out_shape),
        scratch_shapes=scratch,
        compiler_params=pltpu.CompilerParams(vmem_limit_bytes=16 * 2**20),
        name=name,
    )(*args)


def turn(value, axis, size, shift):
    return lax.ppermute(value, axis, [((i + shift) % size, i) for i in range(size)])


def flip(value, axis, size, bits):
    return lax.ppermute(value, axis, [(i, i ^ bits) for i in range(size)])


def local(
    q_nope,
    q_rope,
    new_latent,
    new_rope,
    pool_latent,
    pool_rope,
    block_table,
    prefix_len,
    w_uk,
    w_uv,
    w_out,
):
    ids = jnp.stack(
        [
            lax.axis_index("yl"),
            lax.axis_index("x"),
            lax.axis_index("k"),
            lax.axis_index("zb"),
            lax.axis_index("z0") * 2 + lax.axis_index("yh"),
        ]
    ).astype(jnp.int32)
    query = jnp.concatenate([q_nope, q_rope], axis=1)
    pool = jnp.concatenate(
        [pool_latent.reshape(4 * BLOCK, LAT), jnp.transpose(pool_rope, (1, 0, 2)).reshape(ROPE, 4 * BLOCK)], axis=0
    )
    weight = w_out.T

    queries = [query] + [turn(query, "x", 4, s) for s in (1, 2, 3)]
    pool_y = flip(pool, "yl", 2, 1)
    weight_z = flip(weight, "z0", 2, 1)
    lists, counts = plan(ids, block_table, prefix_len)
    q_lat, q_rot = simple(
        prepare_kernel,
        "prepare",
        [
            jax.ShapeDtypeStruct((SLOTS, ROWS, LAT), jnp.bfloat16),
            jax.ShapeDtypeStruct((SLOTS, ROWS, ROPE), jnp.bfloat16),
        ],
        [counts, *queries, w_uk],
    )
    pool, pool_y, weight_z = tie([pool, pool_y, weight_z], [q_lat])
    pool_k = flip(pool, "k", 2, 1)
    pool_yk = flip(pool_y, "k", 2, 1)
    pair = simple(
        pair_kernel, "pair", jax.ShapeDtypeStruct((2, 448, 512), jnp.bfloat16), [weight, weight_z]
    )
    ring = ("yl", "yh")
    mine = [pair, flip(pair, ring, 4, 2), flip(pair, ring, 4, 3)]
    other = [flip(pair, "k", 2, 1)]
    pool_k, other[0] = tie([pool_k, other[0]], [])
    pools = [pool, pool_y, pool_k, pool_yk]

    away = attention((1, 2, 3), False, lists, counts, q_lat, q_rot, pools, w_uv, ())
    came = [
        lax.ppermute(part, "x", [(i, (i + s) % 4) for i in range(4)]) for s, part in zip((1, 2, 3), away)
    ]
    (home,) = attention((0,), True, lists, counts, q_lat, q_rot, pools, w_uv, (new_latent, new_rope[0]))
    mine[1], mine[2] = tie([mine[1], mine[2]], [*came, home])
    far = [flip(mine[2][0], ring, 4, 2), flip(mine[1][1], ring, 4, 3)]
    heads = simple(
        combine_kernel,
        "combine",
        [jax.ShapeDtypeStruct((32, HEADS * VD), jnp.bfloat16)] * 4,
        [ids, home, *came],
        scratch=[pltpu.VMEM((TOK, HEADS * VD), jnp.float32)],
    )
    heads = [heads[0]] + [flip(heads[d], ("z0", "yh"), 4, d) for d in (1, 2, 3)]
    heads = simple(join_kernel, "join", jax.ShapeDtypeStruct((32, 2048), jnp.bfloat16), heads)
    rest = simple(
        rest_kernel, "rest", jax.ShapeDtypeStruct((6, 448, 512), jnp.bfloat16), tie([*mine[1:], *far], [heads])
    )
    mine = [pair, rest]
    other.append(flip(rest, "k", 2, 1))
    heads = [heads] + [turn(heads, "x", 4, s) for s in (1, 2, 3)]
    partial = simple(
        project_kernel,
        "project",
        [jax.ShapeDtypeStruct((32, 1792), jnp.bfloat16)] * 4,
        [ids, *heads, *mine, *other],
        scratch=[pltpu.VMEM((TOK, 1792), jnp.float32)],
    )
    sums = [partial[0]] + [
        lax.ppermute(partial[d], "zb", [(i, (i + d) % 4) for i in range(4)]) for d in (1, 2, 3)
    ]
    pieces = simple(share_kernel, "share", [jax.ShapeDtypeStruct((8, 1792), jnp.float32)] * 4, sums)
    pieces = [pieces[0]] + [
        lax.ppermute(pieces[s], "x", [(i, (i + s) % 4) for i in range(4)]) for s in (1, 2, 3)
    ]
    return simple(place_kernel, "place", jax.ShapeDtypeStruct((8, 7168), jnp.bfloat16), [ids, *pieces])


def solution(mesh):
    fine = Mesh(mesh.devices.reshape(2, 4, 2, 4, 2, 2), ("yl", "x", "k", "zb", "z0", "yh"))
    cache, head = ("yl", "x", "k"), ("zb", "z0", "yh")
    return jax.shard_map(
        local,
        mesh=fine,
        in_specs=(
            P(cache, head),
            P(cache, head),
            P(cache, None),
            P(cache, None, None),
            P(cache, None, None),
            P(cache, None, None),
            P(),
            P(),
            P(head, None, None),
            P(head, None, None),
            P(head, cache),
        ),
        out_specs=P(cache + head, None),
        check_vma=False,
    )
```

```python
import functools

import jax
import jax.numpy as jnp
from jax import lax
from jax.experimental import pallas as pl
from jax.experimental.pallas import tpu as pltpu
from jax.sharding import Mesh, PartitionSpec as P

LAT = 512
NOPE = 128
ROPE = 64
VD = 128
BLOCK = 128
HEADS = 4
TOK = 128
ROWS = HEADS * TOK
SLOTS = 4
STEP = 4
LOG2E = 1.4426950408889634
SCALE2 = (NOPE + ROPE) ** -0.5 * LOG2E
LOW = -1e30
STAT = HEADS * VD
MSG = STAT + 128

VMEM = pltpu.VMEM
SMEM = pltpu.SMEM


def dot_nn(a, b):
    return lax.dot_general(a, b, (((1,), (0,)), ((), ())), preferred_element_type=jnp.float32)


def dot_nt(a, b):
    return lax.dot_general(a, b, (((1,), (1,)), ((), ())), preferred_element_type=jnp.float32)


def plan_kernel(ids, table, lens, lists, counts):
    yl, x, k = ids[0], ids[1], ids[2]
    for s in range(SLOTS):
        limit = lens[yl * 8 + ((x + s) % 4) * 2 + k]

        def scan(m, carry):
            found, valid = carry
            block = table[yl * 8 + ((x + s) % 4) * 2 + k, m]
            owner = block >> 2
            here = ((owner >> 1) & 3) == x

            @pl.when(here)
            def _():
                source = ((owner >> 3) ^ yl) + 2 * ((owner & 1) ^ k)
                lists[s * 16 + found] = source * 4 + (block & 3)

            step = here.astype(jnp.int32)
            return found + step, valid + step * jnp.minimum(limit - m * BLOCK, BLOCK)

        blocks = jnp.minimum((limit + BLOCK - 1) // BLOCK, 32)
        found, valid = lax.fori_loop(0, blocks, scan, (jnp.int32(0), jnp.int32(0)))
        counts[s] = found
        counts[SLOTS + s] = valid


def plan(ids, table, lens):
    scalar = pl.BlockSpec(memory_space=SMEM)
    return pl.pallas_call(
        plan_kernel,
        out_shape=[jax.ShapeDtypeStruct((SLOTS * 16,), jnp.int32), jax.ShapeDtypeStruct((2 * SLOTS,), jnp.int32)],
        in_specs=[scalar] * 3,
        out_specs=[scalar] * 2,
        compiler_params=pltpu.CompilerParams(vmem_limit_bytes=2**20),
        name="plan",
    )(ids, table, lens)


def prepare_kernel(counts, *refs):
    queries = refs[:SLOTS]
    w_uk, q_lat, q_rot = refs[SLOTS : SLOTS + 3]
    for h in range(HEADS):
        rows = slice(h * TOK, (h + 1) * TOK)
        part = jnp.concatenate([q[:, h * NOPE : (h + 1) * NOPE] for q in queries], axis=0)
        part = dot_nn(part, w_uk[h]).astype(jnp.bfloat16)
        first = HEADS * NOPE + h * ROPE
        for s in range(SLOTS):
            q_lat[s, rows, :] = part[s * TOK : (s + 1) * TOK]
            q_rot[s, rows, :] = queries[s][:, first : first + ROPE]


def attention_kernel(slots, own, lists, counts, q_lat, q_rot, *refs):
    count = len(slots)
    refs = list(refs)

    def take(n):
        got = refs[:n]
        del refs[:n]
        return got

    pools = take(4)
    (w_uv,) = take(1)
    new_latent, new_rope = take(2) if own else (None, None)
    outs = take(count)
    keys, rots, acc, top, tot, latents, levels = refs
    keys[...] = jnp.zeros_like(keys)
    rots[...] = jnp.zeros_like(rots)

    def wide(value, times):
        return jnp.concatenate([value] * times, axis=1)

    def begin(score, latent):
        best = jnp.broadcast_to(jnp.max(score, axis=1, keepdims=True), (ROWS, 128))
        times = score.shape[1] // 128
        weight = jnp.exp2((score - wide(best, times)) * SCALE2)
        top[...] = best
        tot[...] = sum(weight[:, i * 128 : (i + 1) * 128] for i in range(times))
        acc[...] = dot_nn(weight.astype(jnp.bfloat16), latent)

    def scores(slot, found, valid, q, r, chunk):
        for b in range(STEP):
            part = slice(b * BLOCK, (b + 1) * BLOCK)
            code = lists[slot * 16 + chunk * STEP + b]
            first = pl.multiple_of((code & 3) * BLOCK, BLOCK)
            for j in range(4):

                @pl.when(jnp.logical_and(chunk * STEP + b < found, (code >> 2) == j))
                def _():
                    keys[part, :] = pools[j][pl.ds(first, BLOCK), :]
                    rots[:, part] = pools[j][4 * BLOCK :, pl.ds(first, BLOCK)]

        score = dot_nt(q, keys[...]) + dot_nn(r, rots[...])
        seen = lax.broadcasted_iota(jnp.int32, score.shape, 1) < valid - chunk * STEP * BLOCK
        return jnp.where(seen, score, LOW)

    def one_slot(s, carry):
        slot = s + slots[0]
        found, valid = counts[slot], counts[SLOTS + slot]
        q, r = q_lat[slot], q_rot[slot]
        if own:
            score = dot_nt(q, new_latent[...]) + dot_nn(r, new_rope[...])
            at = lax.broadcasted_iota(jnp.int32, score.shape, 0) % TOK
            seen = lax.broadcasted_iota(jnp.int32, score.shape, 1) <= at
            begin(jnp.where(seen, score, LOW), new_latent[...])
        else:
            begin(scores(slot, found, valid, q, r, 0), keys[...])

        def step(chunk, inner):
            score = scores(slot, found, valid, q_lat[slot], q_rot[slot], chunk)
            before = top[...]
            best = jnp.maximum(before, jnp.max(score, axis=1, keepdims=True))
            keep = jnp.exp2((before - best) * SCALE2)
            weight = jnp.exp2((score - wide(best, STEP)) * SCALE2)
            top[...] = best
            tot[...] = tot[...] * keep + sum(weight[:, i * 128 : (i + 1) * 128] for i in range(STEP))
            acc[...] = acc[...] * wide(keep, 4) + dot_nn(weight.astype(jnp.bfloat16), keys[...])
            return inner

        lax.fori_loop(0 if own else 1, (found + STEP - 1) // STEP, step, 0)
        total = jnp.broadcast_to(jnp.sum(tot[...], axis=1, keepdims=True), (ROWS, 128))
        latents[s] = (acc[...] * wide(1.0 / total, 4)).astype(jnp.bfloat16)
        level = top[...] * SCALE2 + jnp.log2(total)
        levels[s] = level if own else jnp.where(found > 0, level, LOW)
        return carry

    lax.fori_loop(0, count, one_slot, 0)
    lane = lax.broadcasted_iota(jnp.int32, (TOK, 128), 1)
    for h in range(HEADS):
        rows = slice(h * TOK, (h + 1) * TOK)
        part = jnp.concatenate([latents[s, rows, :] for s in range(count)], axis=0)
        part = dot_nn(part, w_uv[h]).astype(jnp.bfloat16)
        for s in range(count):
            outs[s][:, h * VD : (h + 1) * VD] = part[s * TOK : (s + 1) * TOK]
    for s in range(count):
        level = levels[s, 0:TOK, :]
        for h in range(1, HEADS):
            level = jnp.where(lane % HEADS == h, levels[s, h * TOK : (h + 1) * TOK, :], level)
        high = level.astype(jnp.bfloat16).astype(jnp.float32)
        middle = (level - high).astype(jnp.bfloat16).astype(jnp.float32)
        low = level - high - middle
        stat = jnp.where(lane < HEADS, high, jnp.where(lane < 2 * HEADS, middle, low))
        outs[s][:, STAT:] = stat.astype(jnp.bfloat16)


def attention(slots, own, lists, counts, q_lat, q_rot, pools, w_uv, fresh):
    count = len(slots)
    full = pl.BlockSpec(memory_space=VMEM)
    scalar = pl.BlockSpec(memory_space=SMEM)
    return pl.pallas_call(
        functools.partial(attention_kernel, slots, own),
        out_shape=[jax.ShapeDtypeStruct((TOK, MSG), jnp.bfloat16)] * count,
        in_specs=[scalar] * 2 + [full] * (9 if own else 7),
        out_specs=[full] * count,
        scratch_shapes=[
            pltpu.VMEM((STEP * BLOCK, LAT), jnp.bfloat16),
            pltpu.VMEM((ROPE, STEP * BLOCK), jnp.bfloat16),
            pltpu.VMEM((ROWS, LAT), jnp.float32),
            pltpu.VMEM((ROWS, 128), jnp.float32),
            pltpu.VMEM((ROWS, 128), jnp.float32),
            pltpu.VMEM((count, ROWS, LAT), jnp.bfloat16),
            pltpu.VMEM((count, ROWS, 128), jnp.float32),
        ],
        compiler_params=pltpu.CompilerParams(vmem_limit_bytes=24 * 2**20),
        name="attend",
    )(lists, counts, q_lat, q_rot, *pools, w_uv, *fresh)


def combine_kernel(ids, *refs):
    parts, outs, total = refs[:SLOTS], refs[SLOTS : SLOTS + 4], refs[SLOTS + 4]
    a = ids[4]
    stats = [p[:, STAT:].astype(jnp.float32) for p in parts]
    for h in range(HEADS):
        columns = slice(h * VD, (h + 1) * VD)
        levels = [
            s[:, h : h + 1] + s[:, HEADS + h : HEADS + h + 1] + s[:, 2 * HEADS + h : 2 * HEADS + h + 1]
            for s in stats
        ]
        best = functools.reduce(jnp.maximum, levels)
        shares = [jnp.exp2(v - best) for v in levels]
        inverse = 1.0 / sum(shares)
        total[:, columns] = sum(
            p[:, columns].astype(jnp.float32) * (share * inverse) for p, share in zip(parts, shares)
        )
    for d in range(4):
        first = pl.multiple_of((a ^ d) * 8, 8)
        rows = [total[pl.ds(first + q * 32, 8), :] for q in range(4)]
        outs[d][...] = jnp.concatenate(rows, axis=0).astype(jnp.bfloat16)


def join_kernel(*refs):
    for d in range(4):
        refs[4][:, d * 512 : (d + 1) * 512] = refs[d][...]


def pair_kernel(one, two, out):
    out[0] = one[...]
    out[1] = two[...]


def rest_kernel(*refs):
    out = refs[4]
    for i in range(4):
        out[i] = refs[i // 2][i % 2]
    out[4] = refs[2][...]
    out[5] = refs[3][...]


def project_kernel(ids, *refs):
    heads, mine, other = refs[:4], refs[4:6], refs[6:8]
    outs, total = refs[8:12], refs[12]
    zb = ids[3]
    rows = jnp.concatenate([h[...] for h in heads], axis=0)
    for side_y in range(2):
        sides = []
        for pieces in (mine, other):
            value = None
            for d in range(4):
                m, dz = side_y * 2 + (d & 1), d >> 1
                weight = pieces[0][dz] if m == 0 else pieces[1][(0, 4, 0, 2)[m] + dz]
                part = dot_nt(rows[:, d * 512 : (d + 1) * 512], weight)
                value = part if value is None else value + part
            sides.append(value)
        total[:, side_y * 896 : (side_y + 1) * 896] = jnp.concatenate(sides, axis=1)
    for d in range(4):
        first = pl.multiple_of(((zb + d) % 4) * 8, 8)
        parts = [total[pl.ds(first + s * 32, 8), :] for s in range(4)]
        outs[d][...] = jnp.concatenate(parts, axis=0).astype(jnp.bfloat16)


def share_kernel(*refs):
    total = sum(p[...].astype(jnp.float32) for p in refs[:4])
    for s in range(4):
        refs[4 + s][...] = total[s * 8 : (s + 1) * 8]


def place_kernel(ids, *refs):
    parts, out = refs[:4], refs[4]
    yl, x, k = ids[0], ids[1], ids[2]
    for s in range(4):
        for side_y in range(2):
            first = ((yl ^ side_y) * 4 + (x - s + 4) % 4) * 896
            columns = pl.ds(pl.multiple_of(first, 128), 896)
            value = parts[s][:, side_y * 896 : (side_y + 1) * 896]
            swapped = jnp.concatenate([value[:, 448:], value[:, :448]], axis=1)
            out[:, columns] = jnp.where(k == 0, value, swapped).astype(jnp.bfloat16)


def tie_kernel(*refs):
    pass


def tie(values, others):
    free = pl.BlockSpec(memory_space=pl.ANY)
    return pl.pallas_call(
        tie_kernel,
        out_shape=[jax.ShapeDtypeStruct(v.shape, v.dtype) for v in values],
        in_specs=[free] * (len(values) + len(others)),
        out_specs=[free] * len(values),
        input_output_aliases={i: i for i in range(len(values))},
        compiler_params=pltpu.CompilerParams(vmem_limit_bytes=2**20),
        name="tie",
    )(*values, *others)


def simple(kernel, name, out_shape, args, scratch=()):
    full = pl.BlockSpec(memory_space=VMEM)
    return pl.pallas_call(
        kernel,
        out_shape=out_shape,
        in_specs=[pl.BlockSpec(memory_space=SMEM) if arg.dtype == jnp.int32 else full for arg in args],
        out_specs=jax.tree.map(lambda _: full, out_shape),
        scratch_shapes=scratch,
        compiler_params=pltpu.CompilerParams(vmem_limit_bytes=16 * 2**20),
        name=name,
    )(*args)


def turn(value, axis, size, shift):
    return lax.ppermute(value, axis, [((i + shift) % size, i) for i in range(size)])


def flip(value, axis, size, bits):
    return lax.ppermute(value, axis, [(i, i ^ bits) for i in range(size)])


def local(
    q_nope,
    q_rope,
    new_latent,
    new_rope,
    pool_latent,
    pool_rope,
    block_table,
    prefix_len,
    w_uk,
    w_uv,
    w_out,
):
    ids = jnp.stack(
        [
            lax.axis_index("yl"),
            lax.axis_index("x"),
            lax.axis_index("k"),
            lax.axis_index("zb"),
            lax.axis_index("z0") * 2 + lax.axis_index("yh"),
        ]
    ).astype(jnp.int32)
    query = jnp.concatenate([q_nope, q_rope], axis=1)
    pool = jnp.concatenate(
        [pool_latent.reshape(4 * BLOCK, LAT), jnp.transpose(pool_rope, (1, 0, 2)).reshape(ROPE, 4 * BLOCK)], axis=0
    )
    weight = w_out.T

    queries = [query] + [turn(query, "x", 4, s) for s in (1, 2, 3)]
    pool_y = flip(pool, "yl", 2, 1)
    weight_z = flip(weight, "z0", 2, 1)
    lists, counts = plan(ids, block_table, prefix_len)
    pool, pool_y, counts, weight_z = tie([pool, pool_y, counts, weight_z], queries[1:])
    q_lat, q_rot = simple(
        prepare_kernel,
        "prepare",
        [
            jax.ShapeDtypeStruct((SLOTS, ROWS, LAT), jnp.bfloat16),
            jax.ShapeDtypeStruct((SLOTS, ROWS, ROPE), jnp.bfloat16),
        ],
        [counts, *queries, w_uk],
    )
    pool_k = flip(pool, "k", 2, 1)
    pool_yk = flip(pool_y, "k", 2, 1)
    pair = simple(
        pair_kernel, "pair", jax.ShapeDtypeStruct((2, 448, 512), jnp.bfloat16), [weight, weight_z]
    )
    ring = ("yl", "yh")
    mine = [pair, flip(pair, ring, 4, 2), flip(pair, ring, 4, 3)]
    other = [flip(pair, "k", 2, 1)]
    pool_k, other[0] = tie([pool_k, other[0]], [])
    pools = [pool, pool_y, pool_k, pool_yk]

    away = attention((1, 2, 3), False, lists, counts, q_lat, q_rot, pools, w_uv, ())
    came = [
        lax.ppermute(part, "x", [(i, (i + s) % 4) for i in range(4)]) for s, part in zip((1, 2, 3), away)
    ]
    (home,) = attention((0,), True, lists, counts, q_lat, q_rot, pools, w_uv, (new_latent, new_rope[0]))
    mine[1], mine[2] = tie([mine[1], mine[2]], [*came, home])
    far = [flip(mine[2][0], ring, 4, 2), flip(mine[1][1], ring, 4, 3)]
    heads = simple(
        combine_kernel,
        "combine",
        [jax.ShapeDtypeStruct((32, HEADS * VD), jnp.bfloat16)] * 4,
        [ids, home, *came],
        scratch=[pltpu.VMEM((TOK, HEADS * VD), jnp.float32)],
    )
    heads = [heads[0]] + [flip(heads[d], ("z0", "yh"), 4, d) for d in (1, 2, 3)]
    heads = simple(join_kernel, "join", jax.ShapeDtypeStruct((32, 2048), jnp.bfloat16), heads)
    rest = simple(
        rest_kernel, "rest", jax.ShapeDtypeStruct((6, 448, 512), jnp.bfloat16), tie([*mine[1:], *far], [heads])
    )
    mine = [pair, rest]
    other.append(flip(rest, "k", 2, 1))
    heads = [heads] + [turn(heads, "x", 4, s) for s in (1, 2, 3)]
    partial = simple(
        project_kernel,
        "project",
        [jax.ShapeDtypeStruct((32, 1792), jnp.bfloat16)] * 4,
        [ids, *heads, *mine, *other],
        scratch=[pltpu.VMEM((TOK, 1792), jnp.float32)],
    )
    sums = [partial[0]] + [
        lax.ppermute(partial[d], "zb", [(i, (i + d) % 4) for i in range(4)]) for d in (1, 2, 3)
    ]
    pieces = simple(share_kernel, "share", [jax.ShapeDtypeStruct((8, 1792), jnp.float32)] * 4, sums)
    pieces = [pieces[0]] + [
        lax.ppermute(pieces[s], "x", [(i, (i + s) % 4) for i in range(4)]) for s in (1, 2, 3)
    ]
    return simple(place_kernel, "place", jax.ShapeDtypeStruct((8, 7168), jnp.bfloat16), [ids, *pieces])


def solution(mesh):
    fine = Mesh(mesh.devices.reshape(2, 4, 2, 4, 2, 2), ("yl", "x", "k", "zb", "z0", "yh"))
    cache, head = ("yl", "x", "k"), ("zb", "z0", "yh")
    return jax.shard_map(
        local,
        mesh=fine,
        in_specs=(
            P(cache, head),
            P(cache, head),
            P(cache, None),
            P(cache, None, None),
            P(cache, None, None),
            P(cache, None, None),
            P(),
            P(),
            P(head, None, None),
            P(head, None, None),
            P(head, cache),
        ),
        out_specs=P(cache + head, None),
        check_vma=False,
    )
```

```python
import functools

import jax
import jax.numpy as jnp
from jax import lax
from jax.experimental import pallas as pl
from jax.experimental.pallas import tpu as pltpu
from jax.sharding import Mesh, PartitionSpec as P

LAT = 512
NOPE = 128
ROPE = 64
VD = 128
BLOCK = 128
HEADS = 4
TOK = 128
ROWS = HEADS * TOK
SLOTS = 4
STEP = 4
LOG2E = 1.4426950408889634
SCALE2 = (NOPE + ROPE) ** -0.5 * LOG2E
LOW = -1e30
STAT = HEADS * VD
MSG = STAT + 128

VMEM = pltpu.VMEM
SMEM = pltpu.SMEM


def dot_nn(a, b):
    return lax.dot_general(a, b, (((1,), (0,)), ((), ())), preferred_element_type=jnp.float32)


def dot_nt(a, b):
    return lax.dot_general(a, b, (((1,), (1,)), ((), ())), preferred_element_type=jnp.float32)


def plan_kernel(ids, table, lens, lists, counts):
    yl, x, k = ids[0], ids[1], ids[2]
    for s in range(SLOTS):
        limit = lens[yl * 8 + (x ^ s) * 2 + k]

        def scan(m, carry):
            found, valid = carry
            block = table[yl * 8 + (x ^ s) * 2 + k, m]
            owner = block >> 2
            here = ((owner >> 1) & 3) == x

            @pl.when(here)
            def _():
                source = ((owner >> 3) ^ yl) + 2 * ((owner & 1) ^ k)
                lists[s * 16 + found] = source * 4 + (block & 3)

            step = here.astype(jnp.int32)
            return found + step, valid + step * jnp.minimum(limit - m * BLOCK, BLOCK)

        blocks = jnp.minimum((limit + BLOCK - 1) // BLOCK, 32)
        found, valid = lax.fori_loop(0, blocks, scan, (jnp.int32(0), jnp.int32(0)))
        counts[s] = found
        counts[SLOTS + s] = valid


def plan(ids, table, lens):
    scalar = pl.BlockSpec(memory_space=SMEM)
    return pl.pallas_call(
        plan_kernel,
        out_shape=[jax.ShapeDtypeStruct((SLOTS * 16,), jnp.int32), jax.ShapeDtypeStruct((2 * SLOTS,), jnp.int32)],
        in_specs=[scalar] * 3,
        out_specs=[scalar] * 2,
        compiler_params=pltpu.CompilerParams(vmem_limit_bytes=2**20),
        cost_estimate=pl.CostEstimate(flops=1, bytes_accessed=1, transcendentals=0),
        name="plan",
    )(ids, table, lens)


def prepare_kernel(counts, *refs):
    queries = refs[:SLOTS]
    w_uk, q_lat, q_rot = refs[SLOTS : SLOTS + 3]
    for h in range(HEADS):
        rows = slice(h * TOK, (h + 1) * TOK)
        part = jnp.concatenate([q[:, h * NOPE : (h + 1) * NOPE] for q in queries], axis=0)
        part = dot_nn(part, w_uk[h]).astype(jnp.bfloat16)
        first = HEADS * NOPE + h * ROPE
        for s in range(SLOTS):
            q_lat[s, rows, :] = part[s * TOK : (s + 1) * TOK]
            q_rot[s, rows, :] = queries[s][:, first : first + ROPE]


def attention_kernel(slots, own, lists, counts, q_lat, q_rot, *refs):
    count = len(slots)
    refs = list(refs)

    def take(n):
        got = refs[:n]
        del refs[:n]
        return got

    pools = take(4)
    (w_uv,) = take(1)
    new_latent, new_rope = take(2) if own else (None, None)
    outs = take(count)
    keys, rots, acc, top, tot, latents, levels = refs
    keys[...] = jnp.zeros_like(keys)
    rots[...] = jnp.zeros_like(rots)

    def wide(value, times):
        return jnp.concatenate([value] * times, axis=1)

    def begin(score, latent):
        best = jnp.broadcast_to(jnp.max(score, axis=1, keepdims=True), (ROWS, 128))
        times = score.shape[1] // 128
        weight = jnp.exp2((score - wide(best, times)) * SCALE2)
        top[...] = best
        tot[...] = sum(weight[:, i * 128 : (i + 1) * 128] for i in range(times))
        acc[...] = dot_nn(weight.astype(jnp.bfloat16), latent)

    def scores(slot, found, valid, q, r, chunk):
        for b in range(STEP):
            part = slice(b * BLOCK, (b + 1) * BLOCK)
            code = lists[slot * 16 + chunk * STEP + b]
            first = pl.multiple_of((code & 3) * BLOCK, BLOCK)
            for j in range(4):

                @pl.when(jnp.logical_and(chunk * STEP + b < found, (code >> 2) == j))
                def _():
                    keys[part, :] = pools[j][pl.ds(first, BLOCK), :]
                    rots[:, part] = pools[j][4 * BLOCK :, pl.ds(first, BLOCK)]

        score = dot_nt(q, keys[...]) + dot_nn(r, rots[...])
        seen = lax.broadcasted_iota(jnp.int32, score.shape, 1) < valid - chunk * STEP * BLOCK
        return jnp.where(seen, score, LOW)

    def one_slot(s, carry):
        slot = s + slots[0]
        found, valid = counts[slot], counts[SLOTS + slot]
        q, r = q_lat[slot], q_rot[slot]
        if own:
            score = dot_nt(q, new_latent[...]) + dot_nn(r, new_rope[...])
            at = lax.broadcasted_iota(jnp.int32, score.shape, 0) % TOK
            seen = lax.broadcasted_iota(jnp.int32, score.shape, 1) <= at
            begin(jnp.where(seen, score, LOW), new_latent[...])
        else:
            begin(scores(slot, found, valid, q, r, 0), keys[...])

        def step(chunk, inner):
            score = scores(slot, found, valid, q_lat[slot], q_rot[slot], chunk)
            before = top[...]
            best = jnp.maximum(before, jnp.max(score, axis=1, keepdims=True))
            keep = jnp.exp2((before - best) * SCALE2)
            weight = jnp.exp2((score - wide(best, STEP)) * SCALE2)
            top[...] = best
            tot[...] = tot[...] * keep + sum(weight[:, i * 128 : (i + 1) * 128] for i in range(STEP))
            acc[...] = acc[...] * wide(keep, 4) + dot_nn(weight.astype(jnp.bfloat16), keys[...])
            return inner

        lax.fori_loop(0 if own else 1, (found + STEP - 1) // STEP, step, 0)
        total = jnp.broadcast_to(jnp.sum(tot[...], axis=1, keepdims=True), (ROWS, 128))
        latents[s] = (acc[...] * wide(1.0 / total, 4)).astype(jnp.bfloat16)
        level = top[...] * SCALE2 + jnp.log2(total)
        levels[s] = level if own else jnp.where(found > 0, level, LOW)
        return carry

    lax.fori_loop(0, count, one_slot, 0)
    lane = lax.broadcasted_iota(jnp.int32, (TOK, 128), 1)
    for h in range(HEADS):
        rows = slice(h * TOK, (h + 1) * TOK)
        part = jnp.concatenate([latents[s, rows, :] for s in range(count)], axis=0)
        part = dot_nn(part, w_uv[h]).astype(jnp.bfloat16)
        for s in range(count):
            outs[s][:, h * VD : (h + 1) * VD] = part[s * TOK : (s + 1) * TOK]
    for s in range(count):
        level = levels[s, 0:TOK, :]
        for h in range(1, HEADS):
            level = jnp.where(lane % HEADS == h, levels[s, h * TOK : (h + 1) * TOK, :], level)
        high = level.astype(jnp.bfloat16).astype(jnp.float32)
        middle = (level - high).astype(jnp.bfloat16).astype(jnp.float32)
        low = level - high - middle
        stat = jnp.where(lane < HEADS, high, jnp.where(lane < 2 * HEADS, middle, low))
        outs[s][:, STAT:] = stat.astype(jnp.bfloat16)


def attention(slots, own, lists, counts, q_lat, q_rot, pools, w_uv, fresh):
    count = len(slots)
    full = pl.BlockSpec(memory_space=VMEM)
    scalar = pl.BlockSpec(memory_space=SMEM)
    return pl.pallas_call(
        functools.partial(attention_kernel, slots, own),
        out_shape=[jax.ShapeDtypeStruct((TOK, MSG), jnp.bfloat16)] * count,
        in_specs=[scalar] * 2 + [full] * (9 if own else 7),
        out_specs=[full] * count,
        scratch_shapes=[
            pltpu.VMEM((STEP * BLOCK, LAT), jnp.bfloat16),
            pltpu.VMEM((ROPE, STEP * BLOCK), jnp.bfloat16),
            pltpu.VMEM((ROWS, LAT), jnp.float32),
            pltpu.VMEM((ROWS, 128), jnp.float32),
            pltpu.VMEM((ROWS, 128), jnp.float32),
            pltpu.VMEM((count, ROWS, LAT), jnp.bfloat16),
            pltpu.VMEM((count, ROWS, 128), jnp.float32),
        ],
        compiler_params=pltpu.CompilerParams(vmem_limit_bytes=24 * 2**20),
        cost_estimate=pl.CostEstimate(flops=1, bytes_accessed=1, transcendentals=0),
        name="attend",
    )(lists, counts, q_lat, q_rot, *pools, w_uv, *fresh)


def combine_kernel(ids, *refs):
    parts, outs, total = refs[:SLOTS], refs[SLOTS : SLOTS + 4], refs[SLOTS + 4]
    a = ids[4]
    stats = [p[:, STAT:].astype(jnp.float32) for p in parts]
    for h in range(HEADS):
        columns = slice(h * VD, (h + 1) * VD)
        levels = [
            s[:, h : h + 1] + s[:, HEADS + h : HEADS + h + 1] + s[:, 2 * HEADS + h : 2 * HEADS + h + 1]
            for s in stats
        ]
        best = functools.reduce(jnp.maximum, levels)
        shares = [jnp.exp2(v - best) for v in levels]
        inverse = 1.0 / sum(shares)
        total[:, columns] = sum(
            p[:, columns].astype(jnp.float32) * (share * inverse) for p, share in zip(parts, shares)
        )
    for d in range(4):
        first = pl.multiple_of((a ^ d) * 8, 8)
        rows = [total[pl.ds(first + q * 32, 8), :] for q in range(4)]
        outs[d][...] = jnp.concatenate(rows, axis=0).astype(jnp.bfloat16)


def join_kernel(*refs):
    for d in range(4):
        refs[4][:, d * 512 : (d + 1) * 512] = refs[d][...]


def pair_kernel(one, two, out):
    out[0] = one[...]
    out[1] = two[...]


def rest_kernel(*refs):
    out = refs[4]
    for i in range(4):
        out[i] = refs[i // 2][i % 2]
    out[4] = refs[2][...]
    out[5] = refs[3][...]


def project_kernel(ids, *refs):
    heads, mine, other = refs[:4], refs[4:6], refs[6:8]
    outs, total = refs[8:12], refs[12]
    zb = ids[3]
    rows = jnp.concatenate([h[...] for h in heads], axis=0)
    for side_y in range(2):
        sides = []
        for pieces in (mine, other):
            value = None
            for d in range(4):
                m, dz = side_y * 2 + (d & 1), d >> 1
                weight = pieces[0][dz] if m == 0 else pieces[1][(0, 4, 0, 2)[m] + dz]
                part = dot_nt(rows[:, d * 512 : (d + 1) * 512], weight)
                value = part if value is None else value + part
            sides.append(value)
        total[:, side_y * 896 : (side_y + 1) * 896] = jnp.concatenate(sides, axis=1)
    for d in range(4):
        first = pl.multiple_of((zb ^ d) * 8, 8)
        parts = [total[pl.ds(first + s * 32, 8), :] for s in range(4)]
        outs[d][...] = jnp.concatenate(parts, axis=0).astype(jnp.bfloat16)


def share_kernel(*refs):
    total = sum(p[...].astype(jnp.float32) for p in refs[:4])
    for s in range(4):
        refs[4 + s][...] = total[s * 8 : (s + 1) * 8]


def place_kernel(ids, *refs):
    parts, out = refs[:4], refs[4]
    yl, x, k = ids[0], ids[1], ids[2]
    for s in range(4):
        for side_y in range(2):
            first = ((yl ^ side_y) * 4 + (x ^ s)) * 896
            columns = pl.ds(pl.multiple_of(first, 128), 896)
            value = parts[s][:, side_y * 896 : (side_y + 1) * 896]
            swapped = jnp.concatenate([value[:, 448:], value[:, :448]], axis=1)
            out[:, columns] = jnp.where(k == 0, value, swapped).astype(jnp.bfloat16)


def tie_kernel(*refs):
    pass


def tie(values, others):
    free = pl.BlockSpec(memory_space=pl.ANY)
    return pl.pallas_call(
        tie_kernel,
        out_shape=[jax.ShapeDtypeStruct(v.shape, v.dtype) for v in values],
        in_specs=[free] * (len(values) + len(others)),
        out_specs=[free] * len(values),
        input_output_aliases={i: i for i in range(len(values))},
        compiler_params=pltpu.CompilerParams(vmem_limit_bytes=2**20),
        cost_estimate=pl.CostEstimate(flops=1, bytes_accessed=1, transcendentals=0),
        name="tie",
    )(*values, *others)


def simple(kernel, name, out_shape, args, scratch=()):
    full = pl.BlockSpec(memory_space=VMEM)
    return pl.pallas_call(
        kernel,
        out_shape=out_shape,
        in_specs=[pl.BlockSpec(memory_space=SMEM) if arg.dtype == jnp.int32 else full for arg in args],
        out_specs=jax.tree.map(lambda _: full, out_shape),
        scratch_shapes=scratch,
        compiler_params=pltpu.CompilerParams(vmem_limit_bytes=16 * 2**20),
        cost_estimate=pl.CostEstimate(flops=1, bytes_accessed=1, transcendentals=0),
        name=name,
    )(*args)


def flip(value, axis, size, bits):
    return lax.ppermute(value, axis, [(i, i ^ bits) for i in range(size)])


def local(
    q_nope,
    q_rope,
    new_latent,
    new_rope,
    pool_latent,
    pool_rope,
    block_table,
    prefix_len,
    w_uk,
    w_uv,
    w_out,
):
    ids = jnp.stack(
        [
            lax.axis_index("yl"),
            lax.axis_index("x"),
            lax.axis_index("k"),
            lax.axis_index("zb"),
            lax.axis_index("z0") * 2 + lax.axis_index("yh"),
        ]
    ).astype(jnp.int32)
    query = jnp.concatenate([q_nope, q_rope], axis=1)
    pool = jnp.concatenate(
        [pool_latent.reshape(4 * BLOCK, LAT), jnp.transpose(pool_rope, (1, 0, 2)).reshape(ROPE, 4 * BLOCK)], axis=0
    )
    weight = w_out.T

    queries = [query] + [flip(query, "x", 4, s) for s in (1, 2, 3)]
    pool_y = flip(pool, "yl", 2, 1)
    weight_z = flip(weight, "z0", 2, 1)
    lists, counts = plan(ids, block_table, prefix_len)
    (weight_z,) = tie([weight_z], [counts])
    pool, pool_y, counts = tie([pool, pool_y, counts], queries[1:])
    q_lat, q_rot = simple(
        prepare_kernel,
        "prepare",
        [
            jax.ShapeDtypeStruct((SLOTS, ROWS, LAT), jnp.bfloat16),
            jax.ShapeDtypeStruct((SLOTS, ROWS, ROPE), jnp.bfloat16),
        ],
        [counts, *queries, w_uk],
    )
    pool_k = flip(pool, "k", 2, 1)
    pool_yk = flip(pool_y, "k", 2, 1)
    pair = simple(
        pair_kernel, "pair", jax.ShapeDtypeStruct((2, 448, 512), jnp.bfloat16), [weight, weight_z]
    )
    ring = ("yl", "yh")
    mine = [pair, flip(pair, ring, 4, 2), flip(pair, ring, 4, 3)]
    other = [flip(pair, "k", 2, 1)]
    pool_k, other[0] = tie([pool_k, other[0]], [])
    pools = [pool, pool_y, pool_k, pool_yk]

    away = attention((1, 2, 3), False, lists, counts, q_lat, q_rot, pools, w_uv, ())
    came = [flip(part, "x", 4, s) for s, part in zip((1, 2, 3), away)]
    (home,) = attention((0,), True, lists, counts, q_lat, q_rot, pools, w_uv, (new_latent, new_rope[0]))
    mine[1], mine[2] = tie([mine[1], mine[2]], [*came, home])
    far = [flip(mine[2][0], ring, 4, 2), flip(mine[1][1], ring, 4, 3)]
    heads = simple(
        combine_kernel,
        "combine",
        [jax.ShapeDtypeStruct((32, HEADS * VD), jnp.bfloat16)] * 4,
        [ids, home, *came],
        scratch=[pltpu.VMEM((TOK, HEADS * VD), jnp.float32)],
    )
    heads = [heads[0]] + [flip(heads[d], ("z0", "yh"), 4, d) for d in (1, 2, 3)]
    heads = simple(join_kernel, "join", jax.ShapeDtypeStruct((32, 2048), jnp.bfloat16), heads)
    rest = simple(
        rest_kernel, "rest", jax.ShapeDtypeStruct((6, 448, 512), jnp.bfloat16), tie([*mine[1:], *far], [heads])
    )
    mine = [pair, rest]
    other.append(flip(rest, "k", 2, 1))
    heads = [heads] + [flip(heads, "x", 4, s) for s in (1, 2, 3)]
    partial = simple(
        project_kernel,
        "project",
        [jax.ShapeDtypeStruct((32, 1792), jnp.bfloat16)] * 4,
        [ids, *heads, *mine, *other],
        scratch=[pltpu.VMEM((TOK, 1792), jnp.float32)],
    )
    sums = [partial[0]] + [flip(partial[d], "zb", 4, d) for d in (1, 2, 3)]
    pieces = simple(share_kernel, "share", [jax.ShapeDtypeStruct((8, 1792), jnp.float32)] * 4, sums)
    pieces = [pieces[0]] + [flip(pieces[s], "x", 4, s) for s in (1, 2, 3)]
    return simple(place_kernel, "place", jax.ShapeDtypeStruct((8, 7168), jnp.bfloat16), [ids, *pieces])


def solution(mesh):
    fine = Mesh(mesh.devices.reshape(2, 4, 2, 4, 2, 2), ("yl", "x", "k", "zb", "z0", "yh"))
    cache, head = ("yl", "x", "k"), ("zb", "z0", "yh")
    return jax.shard_map(
        local,
        mesh=fine,
        in_specs=(
            P(cache, head),
            P(cache, head),
            P(cache, None),
            P(cache, None, None),
            P(cache, None, None),
            P(cache, None, None),
            P(),
            P(),
            P(head, None, None),
            P(head, None, None),
            P(head, cache),
        ),
        out_specs=P(cache + head, None),
        check_vma=False,
    )
```

```python
import functools

import jax
import jax.numpy as jnp
from jax import lax
from jax.experimental import pallas as pl
from jax.experimental.pallas import tpu as pltpu
from jax.sharding import Mesh, PartitionSpec as P

LAT = 512
NOPE = 128
ROPE = 64
VD = 128
BLOCK = 128
HEADS = 4
TOK = 128
ROWS = HEADS * TOK
SLOTS = 4
STEP = 4
LOG2E = 1.4426950408889634
SCALE2 = (NOPE + ROPE) ** -0.5 * LOG2E
LOW = -1e30
STAT = HEADS * VD
MSG = STAT + 128

VMEM = pltpu.VMEM
SMEM = pltpu.SMEM


def dot_nn(a, b):
    return lax.dot_general(a, b, (((1,), (0,)), ((), ())), preferred_element_type=jnp.float32)


def dot_nt(a, b):
    return lax.dot_general(a, b, (((1,), (1,)), ((), ())), preferred_element_type=jnp.float32)


def plan_kernel(ids, table, lens, lists, counts):
    yl, x, k = ids[0], ids[1], ids[2]
    for s in range(SLOTS):
        limit = lens[yl * 8 + ((x + s) % 4) * 2 + k]

        def scan(m, carry):
            found, valid = carry
            block = table[yl * 8 + ((x + s) % 4) * 2 + k, m]
            owner = block >> 2
            here = ((owner >> 1) & 3) == x

            @pl.when(here)
            def _():
                source = ((owner >> 3) ^ yl) + 2 * ((owner & 1) ^ k)
                lists[s * 16 + found] = source * 4 + (block & 3)

            step = here.astype(jnp.int32)
            return found + step, valid + step * jnp.minimum(limit - m * BLOCK, BLOCK)

        blocks = jnp.minimum((limit + BLOCK - 1) // BLOCK, 32)
        found, valid = lax.fori_loop(0, blocks, scan, (jnp.int32(0), jnp.int32(0)))
        counts[s] = found
        counts[SLOTS + s] = valid


def plan(ids, table, lens):
    scalar = pl.BlockSpec(memory_space=SMEM)
    return pl.pallas_call(
        plan_kernel,
        out_shape=[jax.ShapeDtypeStruct((SLOTS * 16,), jnp.int32), jax.ShapeDtypeStruct((2 * SLOTS,), jnp.int32)],
        in_specs=[scalar] * 3,
        out_specs=[scalar] * 2,
        compiler_params=pltpu.CompilerParams(vmem_limit_bytes=2**20),
        name="plan",
    )(ids, table, lens)


def prepare_kernel(counts, *refs):
    queries = refs[:SLOTS]
    w_uk, q_lat, q_rot = refs[SLOTS : SLOTS + 3]
    for h in range(HEADS):
        rows = slice(h * TOK, (h + 1) * TOK)
        part = jnp.concatenate([q[:, h * NOPE : (h + 1) * NOPE] for q in queries], axis=0)
        part = dot_nn(part, w_uk[h]).astype(jnp.bfloat16)
        first = HEADS * NOPE + h * ROPE
        for s in range(SLOTS):
            q_lat[s, rows, :] = part[s * TOK : (s + 1) * TOK]
            q_rot[s, rows, :] = queries[s][:, first : first + ROPE]


def attention_kernel(slots, own, lists, counts, q_lat, q_rot, *refs):
    count = len(slots)
    refs = list(refs)

    def take(n):
        got = refs[:n]
        del refs[:n]
        return got

    pools = take(4)
    (w_uv,) = take(1)
    new_latent, new_rope = take(2) if own else (None, None)
    outs = take(count)
    keys, rots, acc, top, tot, latents, levels = refs
    keys[...] = jnp.zeros_like(keys)
    rots[...] = jnp.zeros_like(rots)

    def wide(value, times):
        return jnp.concatenate([value] * times, axis=1)

    def begin(score, latent):
        best = jnp.broadcast_to(jnp.max(score, axis=1, keepdims=True), (ROWS, 128))
        times = score.shape[1] // 128
        weight = jnp.exp2((score - wide(best, times)) * SCALE2)
        top[...] = best
        tot[...] = sum(weight[:, i * 128 : (i + 1) * 128] for i in range(times))
        acc[...] = dot_nn(weight.astype(jnp.bfloat16), latent)

    def scores(slot, found, valid, q, r, chunk):
        for b in range(STEP):
            part = slice(b * BLOCK, (b + 1) * BLOCK)
            code = lists[slot * 16 + chunk * STEP + b]
            first = pl.multiple_of((code & 3) * BLOCK, BLOCK)
            for j in range(4):

                @pl.when(jnp.logical_and(chunk * STEP + b < found, (code >> 2) == j))
                def _():
                    keys[part, :] = pools[j][pl.ds(first, BLOCK), :]
                    rots[:, part] = pools[j][4 * BLOCK :, pl.ds(first, BLOCK)]

        score = dot_nt(q, keys[...]) + dot_nn(r, rots[...])
        seen = lax.broadcasted_iota(jnp.int32, score.shape, 1) < valid - chunk * STEP * BLOCK
        return jnp.where(seen, score, LOW)

    def one_slot(s, carry):
        slot = s + slots[0]
        found, valid = counts[slot], counts[SLOTS + slot]
        q, r = q_lat[slot], q_rot[slot]
        if own:
            score = dot_nt(q, new_latent[...]) + dot_nn(r, new_rope[...])
            at = lax.broadcasted_iota(jnp.int32, score.shape, 0) % TOK
            seen = lax.broadcasted_iota(jnp.int32, score.shape, 1) <= at
            begin(jnp.where(seen, score, LOW), new_latent[...])
        else:
            begin(scores(slot, found, valid, q, r, 0), keys[...])

        def step(chunk, inner):
            score = scores(slot, found, valid, q_lat[slot], q_rot[slot], chunk)
            before = top[...]
            best = jnp.maximum(before, jnp.max(score, axis=1, keepdims=True))
            keep = jnp.exp2((before - best) * SCALE2)
            weight = jnp.exp2((score - wide(best, STEP)) * SCALE2)
            top[...] = best
            tot[...] = tot[...] * keep + sum(weight[:, i * 128 : (i + 1) * 128] for i in range(STEP))
            acc[...] = acc[...] * wide(keep, 4) + dot_nn(weight.astype(jnp.bfloat16), keys[...])
            return inner

        lax.fori_loop(0 if own else 1, (found + STEP - 1) // STEP, step, 0)
        total = jnp.broadcast_to(jnp.sum(tot[...], axis=1, keepdims=True), (ROWS, 128))
        latents[s] = (acc[...] * wide(1.0 / total, 4)).astype(jnp.bfloat16)
        level = top[...] * SCALE2 + jnp.log2(total)
        levels[s] = level if own else jnp.where(found > 0, level, LOW)
        return carry

    lax.fori_loop(0, count, one_slot, 0)
    lane = lax.broadcasted_iota(jnp.int32, (TOK, 128), 1)
    for h in range(HEADS):
        rows = slice(h * TOK, (h + 1) * TOK)
        part = jnp.concatenate([latents[s, rows, :] for s in range(count)], axis=0)
        part = dot_nn(part, w_uv[h]).astype(jnp.bfloat16)
        for s in range(count):
            outs[s][:, h * VD : (h + 1) * VD] = part[s * TOK : (s + 1) * TOK]
    for s in range(count):
        level = levels[s, 0:TOK, :]
        for h in range(1, HEADS):
            level = jnp.where(lane % HEADS == h, levels[s, h * TOK : (h + 1) * TOK, :], level)
        high = level.astype(jnp.bfloat16).astype(jnp.float32)
        middle = (level - high).astype(jnp.bfloat16).astype(jnp.float32)
        low = level - high - middle
        stat = jnp.where(lane < HEADS, high, jnp.where(lane < 2 * HEADS, middle, low))
        outs[s][:, STAT:] = stat.astype(jnp.bfloat16)


def attention(slots, own, lists, counts, q_lat, q_rot, pools, w_uv, fresh):
    count = len(slots)
    full = pl.BlockSpec(memory_space=VMEM)
    scalar = pl.BlockSpec(memory_space=SMEM)
    return pl.pallas_call(
        functools.partial(attention_kernel, slots, own),
        out_shape=[jax.ShapeDtypeStruct((TOK, MSG), jnp.bfloat16)] * count,
        in_specs=[scalar] * 2 + [full] * (9 if own else 7),
        out_specs=[full] * count,
        scratch_shapes=[
            pltpu.VMEM((STEP * BLOCK, LAT), jnp.bfloat16),
            pltpu.VMEM((ROPE, STEP * BLOCK), jnp.bfloat16),
            pltpu.VMEM((ROWS, LAT), jnp.float32),
            pltpu.VMEM((ROWS, 128), jnp.float32),
            pltpu.VMEM((ROWS, 128), jnp.float32),
            pltpu.VMEM((count, ROWS, LAT), jnp.bfloat16),
            pltpu.VMEM((count, ROWS, 128), jnp.float32),
        ],
        compiler_params=pltpu.CompilerParams(vmem_limit_bytes=24 * 2**20),
        name="attend",
    )(lists, counts, q_lat, q_rot, *pools, w_uv, *fresh)


def combine_kernel(ids, *refs):
    parts, outs, total = refs[:SLOTS], refs[SLOTS : SLOTS + 4], refs[SLOTS + 4]
    a = ids[4]
    stats = [p[:, STAT:].astype(jnp.float32) for p in parts]
    for h in range(HEADS):
        columns = slice(h * VD, (h + 1) * VD)
        levels = [
            s[:, h : h + 1] + s[:, HEADS + h : HEADS + h + 1] + s[:, 2 * HEADS + h : 2 * HEADS + h + 1]
            for s in stats
        ]
        best = functools.reduce(jnp.maximum, levels)
        shares = [jnp.exp2(v - best) for v in levels]
        inverse = 1.0 / sum(shares)
        total[:, columns] = sum(
            p[:, columns].astype(jnp.float32) * (share * inverse) for p, share in zip(parts, shares)
        )
    for d in range(4):
        first = pl.multiple_of((a ^ d) * 8, 8)
        rows = [total[pl.ds(first + q * 32, 8), :] for q in range(4)]
        outs[d][...] = jnp.concatenate(rows, axis=0).astype(jnp.bfloat16)


def join_kernel(*refs):
    for d in range(4):
        refs[4][:, d * 512 : (d + 1) * 512] = refs[d][...]


def pack_kernel(q_nope, q_rope, pool_latent, pool_rope, query, pool, sems):
    moves = [(q_nope, query.at[:, : HEADS * NOPE]), (q_rope, query.at[:, HEADS * NOPE :])]
    for i in range(4):
        moves.append((pool_latent.at[i], pool.at[i * BLOCK : (i + 1) * BLOCK, :]))
        moves.append((pool_rope.at[i], pool.at[4 * BLOCK :, i * BLOCK : (i + 1) * BLOCK]))
    copies = [pltpu.make_async_copy(src, dst, sems.at[i]) for i, (src, dst) in enumerate(moves)]
    for copy in copies:
        copy.start()
    for copy in copies:
        copy.wait()


def pack(*args):
    return pl.pallas_call(
        pack_kernel,
        out_shape=[
            jax.ShapeDtypeStruct((TOK, HEADS * (NOPE + ROPE)), jnp.bfloat16),
            jax.ShapeDtypeStruct((4 * BLOCK + ROPE, LAT), jnp.bfloat16),
        ],
        in_specs=[pl.BlockSpec(memory_space=pltpu.HBM)] * 4,
        out_specs=[pl.BlockSpec(memory_space=VMEM)] * 2,
        scratch_shapes=[pltpu.SemaphoreType.DMA((10,))],
        compiler_params=pltpu.CompilerParams(vmem_limit_bytes=56 * 2**20),
        name="pack",
    )(*args)


def pair_kernel(one, two, out):
    out[0] = one[...]
    out[1] = two[...]


def rest_kernel(*refs):
    out = refs[4]
    for i in range(4):
        out[i] = refs[i // 2][i % 2]
    out[4] = refs[2][...]
    out[5] = refs[3][...]


def project_kernel(ids, *refs):
    heads, mine, other = refs[:4], refs[4:6], refs[6:8]
    outs, total = refs[8:12], refs[12]
    zb = ids[3]
    rows = jnp.concatenate([h[...] for h in heads], axis=0)
    for side_y in range(2):
        sides = []
        for pieces in (mine, other):
            value = None
            for d in range(4):
                m, dz = side_y * 2 + (d & 1), d >> 1
                weight = pieces[0][dz] if m == 0 else pieces[1][(0, 4, 0, 2)[m] + dz]
                part = dot_nt(weight, rows[:, d * 512 : (d + 1) * 512])
                value = part if value is None else value + part
            sides.append(value)
        total[:, side_y * 896 : (side_y + 1) * 896] = jnp.concatenate(sides, axis=0).T
    for d in range(4):
        first = pl.multiple_of(((zb + d) % 4) * 8, 8)
        parts = [total[pl.ds(first + s * 32, 8), :] for s in range(4)]
        outs[d][...] = jnp.concatenate(parts, axis=0).astype(jnp.bfloat16)


def share_kernel(*refs):
    total = sum(p[...].astype(jnp.float32) for p in refs[:4])
    for s in range(4):
        refs[4 + s][...] = total[s * 8 : (s + 1) * 8]


def place_kernel(ids, *refs):
    parts, out = refs[:4], refs[4]
    yl, x, k = ids[0], ids[1], ids[2]
    for s in range(4):
        for side_y in range(2):
            first = ((yl ^ side_y) * 4 + (x - s + 4) % 4) * 896
            columns = pl.ds(pl.multiple_of(first, 128), 896)
            value = parts[s][:, side_y * 896 : (side_y + 1) * 896]
            swapped = jnp.concatenate([value[:, 448:], value[:, :448]], axis=1)
            out[:, columns] = jnp.where(k == 0, value, swapped).astype(jnp.bfloat16)


def tie_kernel(*refs):
    pass


def tie(values, others):
    free = pl.BlockSpec(memory_space=pl.ANY)
    return pl.pallas_call(
        tie_kernel,
        out_shape=[jax.ShapeDtypeStruct(v.shape, v.dtype) for v in values],
        in_specs=[free] * (len(values) + len(others)),
        out_specs=[free] * len(values),
        input_output_aliases={i: i for i in range(len(values))},
        compiler_params=pltpu.CompilerParams(vmem_limit_bytes=2**20),
        name="tie",
    )(*values, *others)


def simple(kernel, name, out_shape, args, scratch=()):
    full = pl.BlockSpec(memory_space=VMEM)
    return pl.pallas_call(
        kernel,
        out_shape=out_shape,
        in_specs=[pl.BlockSpec(memory_space=SMEM) if arg.dtype == jnp.int32 else full for arg in args],
        out_specs=jax.tree.map(lambda _: full, out_shape),
        scratch_shapes=scratch,
        compiler_params=pltpu.CompilerParams(vmem_limit_bytes=16 * 2**20),
        name=name,
    )(*args)


def turn(value, axis, size, shift):
    return lax.ppermute(value, axis, [((i + shift) % size, i) for i in range(size)])


def flip(value, axis, size, bits):
    return lax.ppermute(value, axis, [(i, i ^ bits) for i in range(size)])


def local(
    q_nope,
    q_rope,
    new_latent,
    new_rope,
    pool_latent,
    pool_rope,
    block_table,
    prefix_len,
    w_uk,
    w_uv,
    w_out,
):
    ids = jnp.stack(
        [
            lax.axis_index("yl"),
            lax.axis_index("x"),
            lax.axis_index("k"),
            lax.axis_index("zb"),
            lax.axis_index("z0") * 2 + lax.axis_index("yh"),
        ]
    ).astype(jnp.int32)
    query, pool = pack(q_nope, q_rope, pool_latent, pool_rope)
    weight = w_out.T

    queries = [query] + [turn(query, "x", 4, s) for s in (1, 2, 3)]
    pool_y = flip(pool, "yl", 2, 1)
    weight_z = flip(weight, "z0", 2, 1)
    lists, counts = plan(ids, block_table, prefix_len)
    pool_y, counts, weight_z = tie([pool_y, counts, weight_z], queries[1:])
    q_lat, q_rot = simple(
        prepare_kernel,
        "prepare",
        [
            jax.ShapeDtypeStruct((SLOTS, ROWS, LAT), jnp.bfloat16),
            jax.ShapeDtypeStruct((SLOTS, ROWS, ROPE), jnp.bfloat16),
        ],
        [counts, *queries, w_uk],
    )
    pool_k = flip(pool, "k", 2, 1)
    pool_yk = flip(pool_y, "k", 2, 1)
    pair = simple(
        pair_kernel, "pair", jax.ShapeDtypeStruct((2, 448, 512), jnp.bfloat16), [weight, weight_z]
    )
    ring = ("yl", "yh")
    mine = [pair, flip(pair, ring, 4, 2), flip(pair, ring, 4, 3)]
    other = [flip(pair, "k", 2, 1)]
    pool_k, other[0] = tie([pool_k, other[0]], [])
    pools = [pool, pool_y, pool_k, pool_yk]

    away = attention((1, 2, 3), False, lists, counts, q_lat, q_rot, pools, w_uv, ())
    came = [
        lax.ppermute(part, "x", [(i, (i + s) % 4) for i in range(4)]) for s, part in zip((1, 2, 3), away)
    ]
    (home,) = attention((0,), True, lists, counts, q_lat, q_rot, pools, w_uv, (new_latent, new_rope[0]))
    mine[1], mine[2] = tie([mine[1], mine[2]], [*came, home])
    far = [flip(mine[2][0], ring, 4, 2), flip(mine[1][1], ring, 4, 3)]
    heads = simple(
        combine_kernel,
        "combine",
        [jax.ShapeDtypeStruct((32, HEADS * VD), jnp.bfloat16)] * 4,
        [ids, home, *came],
        scratch=[pltpu.VMEM((TOK, HEADS * VD), jnp.float32)],
    )
    heads = [heads[0]] + [flip(heads[d], ("z0", "yh"), 4, d) for d in (1, 2, 3)]
    heads = simple(join_kernel, "join", jax.ShapeDtypeStruct((32, 2048), jnp.bfloat16), heads)
    rest = simple(
        rest_kernel, "rest", jax.ShapeDtypeStruct((6, 448, 512), jnp.bfloat16), tie([*mine[1:], *far], [heads])
    )
    mine = [pair, rest]
    other.append(flip(rest, "k", 2, 1))
    heads = [heads] + [turn(heads, "x", 4, s) for s in (1, 2, 3)]
    partial = simple(
        project_kernel,
        "project",
        [jax.ShapeDtypeStruct((32, 1792), jnp.bfloat16)] * 4,
        [ids, *heads, *mine, *other],
        scratch=[pltpu.VMEM((TOK, 1792), jnp.float32)],
    )
    sums = [partial[0]] + [
        lax.ppermute(partial[d], "zb", [(i, (i + d) % 4) for i in range(4)]) for d in (1, 2, 3)
    ]
    pieces = simple(share_kernel, "share", [jax.ShapeDtypeStruct((8, 1792), jnp.float32)] * 4, sums)
    pieces = [pieces[0]] + [
        lax.ppermute(pieces[s], "x", [(i, (i + s) % 4) for i in range(4)]) for s in (1, 2, 3)
    ]
    return simple(place_kernel, "place", jax.ShapeDtypeStruct((8, 7168), jnp.bfloat16), [ids, *pieces])


def solution(mesh):
    fine = Mesh(mesh.devices.reshape(2, 4, 2, 4, 2, 2), ("yl", "x", "k", "zb", "z0", "yh"))
    cache, head = ("yl", "x", "k"), ("zb", "z0", "yh")
    return jax.shard_map(
        local,
        mesh=fine,
        in_specs=(
            P(cache, head),
            P(cache, head),
            P(cache, None),
            P(cache, None, None),
            P(cache, None, None),
            P(cache, None, None),
            P(),
            P(),
            P(head, None, None),
            P(head, None, None),
            P(head, cache),
        ),
        out_specs=P(cache + head, None),
        check_vma=False,
    )
```

```python
import functools

import jax
import jax.numpy as jnp
from jax import lax
from jax.experimental import pallas as pl
from jax.experimental.pallas import tpu as pltpu
from jax.sharding import Mesh, PartitionSpec as P

LAT = 512
NOPE = 128
ROPE = 64
VD = 128
BLOCK = 128
HEADS = 4
TOK = 128
ROWS = HEADS * TOK
SLOTS = 4
STEP = 4
LOG2E = 1.4426950408889634
SCALE2 = (NOPE + ROPE) ** -0.5 * LOG2E
LOW = -1e30
STAT = HEADS * VD
MSG = STAT + 128

VMEM = pltpu.VMEM
SMEM = pltpu.SMEM


def dot_nn(a, b):
    return lax.dot_general(a, b, (((1,), (0,)), ((), ())), preferred_element_type=jnp.float32)


def dot_nt(a, b):
    return lax.dot_general(a, b, (((1,), (1,)), ((), ())), preferred_element_type=jnp.float32)


def plan_kernel(ids, table, lens, lists, counts):
    yl, x, k = ids[0], ids[1], ids[2]
    for s in range(SLOTS):
        limit = lens[yl * 8 + ((x + s) % 4) * 2 + k]

        def scan(m, carry):
            found, valid = carry
            block = table[yl * 8 + ((x + s) % 4) * 2 + k, m]
            owner = block >> 2
            here = ((owner >> 1) & 3) == x

            @pl.when(here)
            def _():
                source = ((owner >> 3) ^ yl) + 2 * ((owner & 1) ^ k)
                lists[s * 16 + found] = source * 4 + (block & 3)

            step = here.astype(jnp.int32)
            return found + step, valid + step * jnp.minimum(limit - m * BLOCK, BLOCK)

        blocks = jnp.minimum((limit + BLOCK - 1) // BLOCK, 32)
        found, valid = lax.fori_loop(0, blocks, scan, (jnp.int32(0), jnp.int32(0)))
        counts[s] = found
        counts[SLOTS + s] = valid


def plan(ids, table, lens):
    scalar = pl.BlockSpec(memory_space=SMEM)
    return pl.pallas_call(
        plan_kernel,
        out_shape=[jax.ShapeDtypeStruct((SLOTS * 16,), jnp.int32), jax.ShapeDtypeStruct((2 * SLOTS,), jnp.int32)],
        in_specs=[scalar] * 3,
        out_specs=[scalar] * 2,
        compiler_params=pltpu.CompilerParams(vmem_limit_bytes=2**20),
        name="plan",
    )(ids, table, lens)


def prepare_kernel(counts, *refs):
    queries = refs[:SLOTS]
    w_uk, q_lat, q_rot = refs[SLOTS : SLOTS + 3]
    for h in range(HEADS):
        rows = slice(h * TOK, (h + 1) * TOK)
        part = jnp.concatenate([q[:, h * NOPE : (h + 1) * NOPE] for q in queries], axis=0)
        part = dot_nn(part, w_uk[h]).astype(jnp.bfloat16)
        first = HEADS * NOPE + h * ROPE
        for s in range(SLOTS):
            q_lat[s, rows, :] = part[s * TOK : (s + 1) * TOK]
            q_rot[s, rows, :] = queries[s][:, first : first + ROPE]


def attention_kernel(slots, own, lists, counts, q_lat, q_rot, *refs):
    count = len(slots)
    refs = list(refs)

    def take(n):
        got = refs[:n]
        del refs[:n]
        return got

    pools = take(4)
    (w_uv,) = take(1)
    new_latent, new_rope = take(2) if own else (None, None)
    outs = take(count)
    keys, rots, acc, top, tot, latents, levels = refs
    keys[...] = jnp.zeros_like(keys)
    rots[...] = jnp.zeros_like(rots)

    def wide(value, times):
        return jnp.concatenate([value] * times, axis=1)

    def begin(score, latent):
        best = jnp.broadcast_to(jnp.max(score, axis=1, keepdims=True), (ROWS, 128))
        times = score.shape[1] // 128
        weight = jnp.exp2((score - wide(best, times)) * SCALE2)
        top[...] = best
        tot[...] = sum(weight[:, i * 128 : (i + 1) * 128] for i in range(times))
        acc[...] = dot_nn(weight.astype(jnp.bfloat16), latent)

    def scores(slot, found, valid, q, r, chunk):
        for b in range(STEP):
            part = slice(b * BLOCK, (b + 1) * BLOCK)
            code = lists[slot * 16 + chunk * STEP + b]
            first = pl.multiple_of((code & 3) * BLOCK, BLOCK)
            for j in range(4):

                @pl.when(jnp.logical_and(chunk * STEP + b < found, (code >> 2) == j))
                def _():
                    keys[part, :] = pools[j][pl.ds(first, BLOCK), :]
                    rots[:, part] = pools[j][4 * BLOCK :, pl.ds(first, BLOCK)]

        score = dot_nt(q, keys[...]) + dot_nn(r, rots[...])
        seen = lax.broadcasted_iota(jnp.int32, score.shape, 1) < valid - chunk * STEP * BLOCK
        return jnp.where(seen, score, LOW)

    def one_slot(s, carry):
        slot = s + slots[0]
        found, valid = counts[slot], counts[SLOTS + slot]
        q, r = q_lat[slot], q_rot[slot]
        if own:
            score = dot_nt(q, new_latent[...]) + dot_nn(r, new_rope[...])
            at = lax.broadcasted_iota(jnp.int32, score.shape, 0) % TOK
            seen = lax.broadcasted_iota(jnp.int32, score.shape, 1) <= at
            begin(jnp.where(seen, score, LOW), new_latent[...])
        else:
            begin(scores(slot, found, valid, q, r, 0), keys[...])

        def step(chunk, inner):
            score = scores(slot, found, valid, q_lat[slot], q_rot[slot], chunk)
            before = top[...]
            best = jnp.maximum(before, jnp.max(score, axis=1, keepdims=True))
            keep = jnp.exp2((before - best) * SCALE2)
            weight = jnp.exp2((score - wide(best, STEP)) * SCALE2)
            top[...] = best
            tot[...] = tot[...] * keep + sum(weight[:, i * 128 : (i + 1) * 128] for i in range(STEP))
            acc[...] = acc[...] * wide(keep, 4) + dot_nn(weight.astype(jnp.bfloat16), keys[...])
            return inner

        lax.fori_loop(0 if own else 1, (found + STEP - 1) // STEP, step, 0)
        total = jnp.broadcast_to(jnp.sum(tot[...], axis=1, keepdims=True), (ROWS, 128))
        latents[s] = (acc[...] * wide(1.0 / total, 4)).astype(jnp.bfloat16)
        level = top[...] * SCALE2 + jnp.log2(total)
        levels[s] = level if own else jnp.where(found > 0, level, LOW)
        return carry

    lax.fori_loop(0, count, one_slot, 0)
    lane = lax.broadcasted_iota(jnp.int32, (TOK, 128), 1)
    for h in range(HEADS):
        rows = slice(h * TOK, (h + 1) * TOK)
        part = jnp.concatenate([latents[s, rows, :] for s in range(count)], axis=0)
        part = dot_nn(part, w_uv[h]).astype(jnp.bfloat16)
        for s in range(count):
            outs[s][:, h * VD : (h + 1) * VD] = part[s * TOK : (s + 1) * TOK]
    for s in range(count):
        level = levels[s, 0:TOK, :]
        for h in range(1, HEADS):
            level = jnp.where(lane % HEADS == h, levels[s, h * TOK : (h + 1) * TOK, :], level)
        high = level.astype(jnp.bfloat16).astype(jnp.float32)
        middle = (level - high).astype(jnp.bfloat16).astype(jnp.float32)
        low = level - high - middle
        stat = jnp.where(lane < HEADS, high, jnp.where(lane < 2 * HEADS, middle, low))
        outs[s][:, STAT:] = stat.astype(jnp.bfloat16)


def attention(slots, own, lists, counts, q_lat, q_rot, pools, w_uv, fresh):
    count = len(slots)
    full = pl.BlockSpec(memory_space=VMEM)
    scalar = pl.BlockSpec(memory_space=SMEM)
    return pl.pallas_call(
        functools.partial(attention_kernel, slots, own),
        out_shape=[jax.ShapeDtypeStruct((TOK, MSG), jnp.bfloat16)] * count,
        in_specs=[scalar] * 2 + [full] * (9 if own else 7),
        out_specs=[full] * count,
        scratch_shapes=[
            pltpu.VMEM((STEP * BLOCK, LAT), jnp.bfloat16),
            pltpu.VMEM((ROPE, STEP * BLOCK), jnp.bfloat16),
            pltpu.VMEM((ROWS, LAT), jnp.float32),
            pltpu.VMEM((ROWS, 128), jnp.float32),
            pltpu.VMEM((ROWS, 128), jnp.float32),
            pltpu.VMEM((count, ROWS, LAT), jnp.bfloat16),
            pltpu.VMEM((count, ROWS, 128), jnp.float32),
        ],
        compiler_params=pltpu.CompilerParams(vmem_limit_bytes=24 * 2**20),
        name="attend",
    )(lists, counts, q_lat, q_rot, *pools, w_uv, *fresh)


def combine_kernel(ids, *refs):
    parts, outs, total = refs[:SLOTS], refs[SLOTS : SLOTS + 4], refs[SLOTS + 4]
    a = ids[4]
    stats = [p[:, STAT:].astype(jnp.float32) for p in parts]
    for h in range(HEADS):
        columns = slice(h * VD, (h + 1) * VD)
        levels = [
            s[:, h : h + 1] + s[:, HEADS + h : HEADS + h + 1] + s[:, 2 * HEADS + h : 2 * HEADS + h + 1]
            for s in stats
        ]
        best = functools.reduce(jnp.maximum, levels)
        shares = [jnp.exp2(v - best) for v in levels]
        inverse = 1.0 / sum(shares)
        total[:, columns] = sum(
            p[:, columns].astype(jnp.float32) * (share * inverse) for p, share in zip(parts, shares)
        )
    for d in range(4):
        first = pl.multiple_of((a ^ d) * 8, 8)
        rows = [total[pl.ds(first + q * 32, 8), :] for q in range(4)]
        outs[d][...] = jnp.concatenate(rows, axis=0).astype(jnp.bfloat16)


def join_kernel(*refs):
    for d in range(4):
        refs[4][:, d * 512 : (d + 1) * 512] = refs[d][...]


def pack_kernel(q_nope, q_rope, pool_latent, pool_rope, query, pool, sems):
    moves = [(q_nope, query.at[:, : HEADS * NOPE]), (q_rope, query.at[:, HEADS * NOPE :])]
    for i in range(4):
        moves.append((pool_latent.at[i], pool.at[i * BLOCK : (i + 1) * BLOCK, :]))
        moves.append((pool_rope.at[i], pool.at[4 * BLOCK :, i * BLOCK : (i + 1) * BLOCK]))
    copies = [pltpu.make_async_copy(src, dst, sems.at[i]) for i, (src, dst) in enumerate(moves)]
    for copy in copies:
        copy.start()
    for copy in copies:
        copy.wait()


def pack(*args):
    return pl.pallas_call(
        pack_kernel,
        out_shape=[
            jax.ShapeDtypeStruct((TOK, HEADS * (NOPE + ROPE)), jnp.bfloat16),
            jax.ShapeDtypeStruct((4 * BLOCK + ROPE, LAT), jnp.bfloat16),
        ],
        in_specs=[pl.BlockSpec(memory_space=pltpu.HBM)] * 4,
        out_specs=[pl.BlockSpec(memory_space=VMEM)] * 2,
        scratch_shapes=[pltpu.SemaphoreType.DMA((10,))],
        compiler_params=pltpu.CompilerParams(vmem_limit_bytes=56 * 2**20),
        name="pack",
    )(*args)


def pair_kernel(one, two, out):
    out[0] = one[...]
    out[1] = two[...]


def stack_kernel(*refs):
    for s in range(4):
        refs[4][s] = refs[s][...]


def project_kernel(ids, own, other, pair, near, next_, far_one, far_two, *refs):
    outs, total = refs[:4], refs[4]
    zb = ids[3]
    rows = jnp.concatenate([own[...].reshape(TOK, 2048), other[...].reshape(TOK, 2048)], axis=0)
    sides = []
    for side_y in range(2):
        value = None
        for d in range(4):
            dz = d >> 1
            if side_y == 0:
                weight = pair[dz] if d & 1 == 0 else (far_one, far_two)[dz][...]
            else:
                weight = (near, next_)[d & 1][dz]
            part = dot_nt(weight, rows[:, d * 512 : (d + 1) * 512])
            value = part if value is None else value + part
        sides.append(value)
    total[...] = jnp.concatenate(sides, axis=0).T
    for d in range(4):
        first = pl.multiple_of(((zb + d) % 4) * 8, 8)
        parts = [total[pl.ds(first + s * 32, 8), :] for s in range(8)]
        outs[d][...] = jnp.concatenate(parts, axis=0).astype(jnp.bfloat16)


def share_kernel(*refs):
    total = sum(p[...].astype(jnp.float32) for p in refs[:4])
    refs[4][...] = total[:32]
    refs[5][...] = total[32:]


def merge_kernel(keep, got, *outs):
    for s in range(4):
        outs[s][:, :896] = keep[s * 8 : (s + 1) * 8, :]
        outs[s][:, 896:] = got[s * 8 : (s + 1) * 8, :]


def place_kernel(ids, *refs):
    parts, out = refs[:4], refs[4]
    yl, x, k = ids[0], ids[1], ids[2]
    for s in range(4):
        for side_y in range(2):
            first = ((yl ^ side_y) * 4 + (x - s + 4) % 4) * 896
            columns = pl.ds(pl.multiple_of(first, 128), 896)
            mine = parts[s][:, side_y * 448 : (side_y + 1) * 448]
            other = parts[s][:, 896 + side_y * 448 : 896 + (side_y + 1) * 448]
            value = jnp.where(
                k == 0, jnp.concatenate([mine, other], axis=1), jnp.concatenate([other, mine], axis=1)
            )
            out[:, columns] = value.astype(jnp.bfloat16)


def tie_kernel(*refs):
    pass


def tie(values, others):
    free = pl.BlockSpec(memory_space=pl.ANY)
    return pl.pallas_call(
        tie_kernel,
        out_shape=[jax.ShapeDtypeStruct(v.shape, v.dtype) for v in values],
        in_specs=[free] * (len(values) + len(others)),
        out_specs=[free] * len(values),
        input_output_aliases={i: i for i in range(len(values))},
        compiler_params=pltpu.CompilerParams(vmem_limit_bytes=2**20),
        name="tie",
    )(*values, *others)


def simple(kernel, name, out_shape, args, scratch=()):
    full = pl.BlockSpec(memory_space=VMEM)
    return pl.pallas_call(
        kernel,
        out_shape=out_shape,
        in_specs=[pl.BlockSpec(memory_space=SMEM) if arg.dtype == jnp.int32 else full for arg in args],
        out_specs=jax.tree.map(lambda _: full, out_shape),
        scratch_shapes=scratch,
        compiler_params=pltpu.CompilerParams(vmem_limit_bytes=16 * 2**20),
        name=name,
    )(*args)


def turn(value, axis, size, shift):
    return lax.ppermute(value, axis, [((i + shift) % size, i) for i in range(size)])


def flip(value, axis, size, bits):
    return lax.ppermute(value, axis, [(i, i ^ bits) for i in range(size)])


def local(
    q_nope,
    q_rope,
    new_latent,
    new_rope,
    pool_latent,
    pool_rope,
    block_table,
    prefix_len,
    w_uk,
    w_uv,
    w_out,
):
    ids = jnp.stack(
        [
            lax.axis_index("yl"),
            lax.axis_index("x"),
            lax.axis_index("k"),
            lax.axis_index("zb"),
            lax.axis_index("z0") * 2 + lax.axis_index("yh"),
        ]
    ).astype(jnp.int32)
    query, pool = pack(q_nope, q_rope, pool_latent, pool_rope)
    weight = w_out.T

    queries = [query] + [turn(query, "x", 4, s) for s in (1, 2, 3)]
    pool_y = flip(pool, "yl", 2, 1)
    weight_z = flip(weight, "z0", 2, 1)
    lists, counts = plan(ids, block_table, prefix_len)
    pool_y, counts, weight_z = tie([pool_y, counts, weight_z], queries[1:])
    q_lat, q_rot = simple(
        prepare_kernel,
        "prepare",
        [
            jax.ShapeDtypeStruct((SLOTS, ROWS, LAT), jnp.bfloat16),
            jax.ShapeDtypeStruct((SLOTS, ROWS, ROPE), jnp.bfloat16),
        ],
        [counts, *queries, w_uk],
    )
    pool_k = flip(pool, "k", 2, 1)
    pool_yk = flip(pool_y, "k", 2, 1)
    pair = simple(
        pair_kernel, "pair", jax.ShapeDtypeStruct((2, 448, 512), jnp.bfloat16), [weight, weight_z]
    )
    ring = ("yl", "yh")
    mine = [pair, flip(pair, ring, 4, 2), flip(pair, ring, 4, 3)]
    pools = [pool, pool_y, pool_k, pool_yk]

    away = attention((1, 2, 3), False, lists, counts, q_lat, q_rot, pools, w_uv, ())
    came = [
        lax.ppermute(part, "x", [(i, (i + s) % 4) for i in range(4)]) for s, part in zip((1, 2, 3), away)
    ]
    (home,) = attention((0,), True, lists, counts, q_lat, q_rot, pools, w_uv, (new_latent, new_rope[0]))
    heads = simple(
        combine_kernel,
        "combine",
        [jax.ShapeDtypeStruct((32, HEADS * VD), jnp.bfloat16)] * 4,
        [ids, home, *came],
        scratch=[pltpu.VMEM((TOK, HEADS * VD), jnp.float32)],
    )
    heads = [heads[0]] + [flip(heads[d], ("z0", "yh"), 4, d) for d in (1, 2, 3)]
    heads = simple(join_kernel, "join", jax.ShapeDtypeStruct((32, 2048), jnp.bfloat16), heads)
    heads, mine[1], mine[2] = tie([heads, mine[1], mine[2]], [])
    far = [flip(mine[2][0], ring, 4, 2), flip(mine[1][1], ring, 4, 3)]
    heads = [heads] + [turn(heads, "x", 4, s) for s in (1, 2, 3)]
    heads[3], *far = tie([heads[3], *far], [])
    heads = simple(stack_kernel, "stack", jax.ShapeDtypeStruct((4, 32, 2048), jnp.bfloat16), heads)
    partial = simple(
        project_kernel,
        "project",
        [jax.ShapeDtypeStruct((64, 896), jnp.bfloat16)] * 4,
        [ids, heads, flip(heads, "k", 2, 1), *mine, *far],
        scratch=[pltpu.VMEM((256, 896), jnp.float32)],
    )
    sums = [partial[0]] + [
        lax.ppermute(partial[d], "zb", [(i, (i + d) % 4) for i in range(4)]) for d in (1, 2, 3)
    ]
    keep, give = simple(share_kernel, "share", [jax.ShapeDtypeStruct((32, 896), jnp.float32)] * 2, sums)
    pieces = simple(
        merge_kernel,
        "merge",
        [jax.ShapeDtypeStruct((8, 1792), jnp.float32)] * 4,
        [keep, flip(give, "k", 2, 1)],
    )
    pieces = [pieces[0]] + [
        lax.ppermute(pieces[s], "x", [(i, (i + s) % 4) for i in range(4)]) for s in (1, 2, 3)
    ]
    return simple(place_kernel, "place", jax.ShapeDtypeStruct((8, 7168), jnp.bfloat16), [ids, *pieces])


def solution(mesh):
    fine = Mesh(mesh.devices.reshape(2, 4, 2, 4, 2, 2), ("yl", "x", "k", "zb", "z0", "yh"))
    cache, head = ("yl", "x", "k"), ("zb", "z0", "yh")
    return jax.shard_map(
        local,
        mesh=fine,
        in_specs=(
            P(cache, head),
            P(cache, head),
            P(cache, None),
            P(cache, None, None),
            P(cache, None, None),
            P(cache, None, None),
            P(),
            P(),
            P(head, None, None),
            P(head, None, None),
            P(head, cache),
        ),
        out_specs=P(cache + head, None),
        check_vma=False,
    )
```

```python
import functools

import jax
import jax.numpy as jnp
from jax import lax
from jax.experimental import pallas as pl
from jax.experimental.pallas import tpu as pltpu
from jax.sharding import Mesh, PartitionSpec as P

LAT = 512
NOPE = 128
ROPE = 64
VD = 128
BLOCK = 128
HEADS = 4
TOK = 128
ROWS = HEADS * TOK
SLOTS = 4
STEP = 4
LOG2E = 1.4426950408889634
SCALE2 = (NOPE + ROPE) ** -0.5 * LOG2E
LOW = -1e30
STAT = HEADS * VD
MSG = STAT + 128

VMEM = pltpu.VMEM
SMEM = pltpu.SMEM


def dot_nn(a, b):
    return lax.dot_general(a, b, (((1,), (0,)), ((), ())), preferred_element_type=jnp.float32)


def dot_nt(a, b):
    return lax.dot_general(a, b, (((1,), (1,)), ((), ())), preferred_element_type=jnp.float32)


def plan_kernel(ids, table, lens, lists, counts):
    yl, x, k = ids[0], ids[1], ids[2]
    for s in range(SLOTS):
        limit = lens[yl * 8 + ((x + s) % 4) * 2 + k]

        def scan(m, carry):
            found, valid = carry
            block = table[yl * 8 + ((x + s) % 4) * 2 + k, m]
            owner = block >> 2
            here = ((owner >> 1) & 3) == x

            @pl.when(here)
            def _():
                source = ((owner >> 3) ^ yl) + 2 * ((owner & 1) ^ k)
                lists[s * 16 + found] = source * 4 + (block & 3)

            step = here.astype(jnp.int32)
            return found + step, valid + step * jnp.minimum(limit - m * BLOCK, BLOCK)

        blocks = jnp.minimum((limit + BLOCK - 1) // BLOCK, 32)
        found, valid = lax.fori_loop(0, blocks, scan, (jnp.int32(0), jnp.int32(0)))
        counts[s] = found
        counts[SLOTS + s] = valid


def plan(ids, table, lens):
    scalar = pl.BlockSpec(memory_space=SMEM)
    return pl.pallas_call(
        plan_kernel,
        out_shape=[jax.ShapeDtypeStruct((SLOTS * 16,), jnp.int32), jax.ShapeDtypeStruct((2 * SLOTS,), jnp.int32)],
        in_specs=[scalar] * 3,
        out_specs=[scalar] * 2,
        compiler_params=pltpu.CompilerParams(vmem_limit_bytes=2**20),
        name="plan",
    )(ids, table, lens)


def prepare_kernel(counts, *refs):
    queries = refs[:SLOTS]
    w_uk, q_lat, q_rot = refs[SLOTS : SLOTS + 3]
    for h in range(HEADS):
        rows = slice(h * TOK, (h + 1) * TOK)
        part = jnp.concatenate([q[:, h * NOPE : (h + 1) * NOPE] for q in queries], axis=0)
        part = dot_nn(part, w_uk[h]).astype(jnp.bfloat16)
        first = HEADS * NOPE + h * ROPE
        for s in range(SLOTS):
            q_lat[s, rows, :] = part[s * TOK : (s + 1) * TOK]
            q_rot[s, rows, :] = queries[s][:, first : first + ROPE]


def attention_kernel(slots, own, lists, counts, q_lat, q_rot, *refs):
    count = len(slots)
    refs = list(refs)

    def take(n):
        got = refs[:n]
        del refs[:n]
        return got

    pools = take(4)
    (w_uv,) = take(1)
    new_latent, new_rope = take(2) if own else (None, None)
    outs = take(count)
    keys, rots, acc, top, tot, latents, levels = refs
    keys[...] = jnp.zeros_like(keys)
    rots[...] = jnp.zeros_like(rots)

    def wide(value, times):
        return jnp.concatenate([value] * times, axis=1)

    def begin(score, latent):
        best = jnp.broadcast_to(jnp.max(score, axis=1, keepdims=True), (ROWS, 128))
        times = score.shape[1] // 128
        weight = jnp.exp2((score - wide(best, times)) * SCALE2)
        top[...] = best
        tot[...] = sum(weight[:, i * 128 : (i + 1) * 128] for i in range(times))
        acc[...] = dot_nn(weight.astype(jnp.bfloat16), latent)

    def scores(slot, found, valid, q, r, chunk):
        for b in range(STEP):
            part = slice(b * BLOCK, (b + 1) * BLOCK)
            code = lists[slot * 16 + chunk * STEP + b]
            first = pl.multiple_of((code & 3) * BLOCK, BLOCK)
            for j in range(4):

                @pl.when(jnp.logical_and(chunk * STEP + b < found, (code >> 2) == j))
                def _():
                    keys[part, :] = pools[j][pl.ds(first, BLOCK), :]
                    rots[:, part] = pools[j][4 * BLOCK :, pl.ds(first, BLOCK)]

        score = dot_nt(q, keys[...]) + dot_nn(r, rots[...])
        seen = lax.broadcasted_iota(jnp.int32, score.shape, 1) < valid - chunk * STEP * BLOCK
        return jnp.where(seen, score, LOW)

    def one_slot(s, carry):
        slot = s + slots[0]
        found, valid = counts[slot], counts[SLOTS + slot]
        q, r = q_lat[slot], q_rot[slot]
        if own:
            score = dot_nt(q, new_latent[...]) + dot_nn(r, new_rope[...])
            at = lax.broadcasted_iota(jnp.int32, score.shape, 0) % TOK
            seen = lax.broadcasted_iota(jnp.int32, score.shape, 1) <= at
            begin(jnp.where(seen, score, LOW), new_latent[...])
        else:
            begin(scores(slot, found, valid, q, r, 0), keys[...])

        def step(chunk, inner):
            score = scores(slot, found, valid, q_lat[slot], q_rot[slot], chunk)
            before = top[...]
            best = jnp.maximum(before, jnp.max(score, axis=1, keepdims=True))
            keep = jnp.exp2((before - best) * SCALE2)
            weight = jnp.exp2((score - wide(best, STEP)) * SCALE2)
            top[...] = best
            tot[...] = tot[...] * keep + sum(weight[:, i * 128 : (i + 1) * 128] for i in range(STEP))
            acc[...] = acc[...] * wide(keep, 4) + dot_nn(weight.astype(jnp.bfloat16), keys[...])
            return inner

        lax.fori_loop(0 if own else 1, (found + STEP - 1) // STEP, step, 0)
        total = jnp.broadcast_to(jnp.sum(tot[...], axis=1, keepdims=True), (ROWS, 128))
        latents[s] = (acc[...] * wide(1.0 / total, 4)).astype(jnp.bfloat16)
        level = top[...] * SCALE2 + jnp.log2(total)
        levels[s] = level if own else jnp.where(found > 0, level, LOW)
        return carry

    lax.fori_loop(0, count, one_slot, 0)
    lane = lax.broadcasted_iota(jnp.int32, (TOK, 128), 1)
    for h in range(HEADS):
        rows = slice(h * TOK, (h + 1) * TOK)
        part = jnp.concatenate([latents[s, rows, :] for s in range(count)], axis=0)
        part = dot_nn(part, w_uv[h]).astype(jnp.bfloat16)
        for s in range(count):
            outs[s][:, h * VD : (h + 1) * VD] = part[s * TOK : (s + 1) * TOK]
    for s in range(count):
        level = levels[s, 0:TOK, :]
        for h in range(1, HEADS):
            level = jnp.where(lane % HEADS == h, levels[s, h * TOK : (h + 1) * TOK, :], level)
        high = level.astype(jnp.bfloat16).astype(jnp.float32)
        middle = (level - high).astype(jnp.bfloat16).astype(jnp.float32)
        low = level - high - middle
        stat = jnp.where(lane < HEADS, high, jnp.where(lane < 2 * HEADS, middle, low))
        outs[s][:, STAT:] = stat.astype(jnp.bfloat16)


def attention(slots, own, lists, counts, q_lat, q_rot, pools, w_uv, fresh):
    count = len(slots)
    full = pl.BlockSpec(memory_space=VMEM)
    scalar = pl.BlockSpec(memory_space=SMEM)
    return pl.pallas_call(
        functools.partial(attention_kernel, slots, own),
        out_shape=[jax.ShapeDtypeStruct((TOK, MSG), jnp.bfloat16)] * count,
        in_specs=[scalar] * 2 + [full] * (9 if own else 7),
        out_specs=[full] * count,
        scratch_shapes=[
            pltpu.VMEM((STEP * BLOCK, LAT), jnp.bfloat16),
            pltpu.VMEM((ROPE, STEP * BLOCK), jnp.bfloat16),
            pltpu.VMEM((ROWS, LAT), jnp.float32),
            pltpu.VMEM((ROWS, 128), jnp.float32),
            pltpu.VMEM((ROWS, 128), jnp.float32),
            pltpu.VMEM((count, ROWS, LAT), jnp.bfloat16),
            pltpu.VMEM((count, ROWS, 128), jnp.float32),
        ],
        compiler_params=pltpu.CompilerParams(vmem_limit_bytes=24 * 2**20),
        name="attend",
    )(lists, counts, q_lat, q_rot, *pools, w_uv, *fresh)


def combine_kernel(ids, *refs):
    parts, outs, total = refs[:SLOTS], refs[SLOTS : SLOTS + 4], refs[SLOTS + 4]
    a = ids[4]
    stats = [p[:, STAT:].astype(jnp.float32) for p in parts]
    for h in range(HEADS):
        columns = slice(h * VD, (h + 1) * VD)
        levels = [
            s[:, h : h + 1] + s[:, HEADS + h : HEADS + h + 1] + s[:, 2 * HEADS + h : 2 * HEADS + h + 1]
            for s in stats
        ]
        best = functools.reduce(jnp.maximum, levels)
        shares = [jnp.exp2(v - best) for v in levels]
        inverse = 1.0 / sum(shares)
        total[:, columns] = sum(
            p[:, columns].astype(jnp.float32) * (share * inverse) for p, share in zip(parts, shares)
        )
    for d in range(4):
        first = pl.multiple_of((a ^ d) * 8, 8)
        rows = [total[pl.ds(first + q * 32, 8), :] for q in range(4)]
        outs[d][...] = jnp.concatenate(rows, axis=0).astype(jnp.bfloat16)


def join_kernel(*refs):
    for d in range(4):
        refs[4][:, d * 512 : (d + 1) * 512] = refs[d][...]


def pack_kernel(q_nope, q_rope, pool_latent, pool_rope, query, pool, sems):
    moves = [(q_nope, query.at[:, : HEADS * NOPE]), (q_rope, query.at[:, HEADS * NOPE :])]
    for i in range(4):
        moves.append((pool_latent.at[i], pool.at[i * BLOCK : (i + 1) * BLOCK, :]))
        moves.append((pool_rope.at[i], pool.at[4 * BLOCK :, i * BLOCK : (i + 1) * BLOCK]))
    copies = [pltpu.make_async_copy(src, dst, sems.at[i]) for i, (src, dst) in enumerate(moves)]
    for copy in copies:
        copy.start()
    for copy in copies:
        copy.wait()


def pack(*args):
    return pl.pallas_call(
        pack_kernel,
        out_shape=[
            jax.ShapeDtypeStruct((TOK, HEADS * (NOPE + ROPE)), jnp.bfloat16),
            jax.ShapeDtypeStruct((4 * BLOCK + ROPE, LAT), jnp.bfloat16),
        ],
        in_specs=[pl.BlockSpec(memory_space=pltpu.HBM)] * 4,
        out_specs=[pl.BlockSpec(memory_space=pltpu.HBM)] * 2,
        scratch_shapes=[pltpu.SemaphoreType.DMA((10,))],
        compiler_params=pltpu.CompilerParams(vmem_limit_bytes=56 * 2**20),
        name="pack",
    )(*args)


def pair_kernel(one, two, out):
    out[0] = one[...]
    out[1] = two[...]


def project_kernel(ids, *refs):
    heads = refs[:8]
    pair, near, next_, far_one, far_two = refs[8:13]
    outs, total = refs[13:17], refs[17]
    zb = ids[3]
    rows = jnp.concatenate([h[...] for h in heads], axis=0)
    sides = []
    for side_y in range(2):
        value = None
        for d in range(4):
            dz = d >> 1
            if side_y == 0:
                weight = pair[dz] if d & 1 == 0 else (far_one, far_two)[dz][...]
            else:
                weight = (near, next_)[d & 1][dz]
            part = dot_nt(weight, rows[:, d * 512 : (d + 1) * 512])
            value = part if value is None else value + part
        sides.append(value)
    total[...] = jnp.concatenate(sides, axis=0).T
    for d in range(4):
        first = pl.multiple_of(((zb + d) % 4) * 8, 8)
        parts = [total[pl.ds(first + s * 32, 8), :] for s in range(8)]
        outs[d][...] = jnp.concatenate(parts, axis=0).astype(jnp.bfloat16)


def share_kernel(*refs):
    total = sum(p[...].astype(jnp.float32) for p in refs[:4])
    refs[4][...] = total[:32]
    refs[5][...] = total[32:]


def merge_kernel(keep, got, *outs):
    for s in range(4):
        outs[s][:, :896] = keep[s * 8 : (s + 1) * 8, :]
        outs[s][:, 896:] = got[s * 8 : (s + 1) * 8, :]


def place_kernel(ids, *refs):
    parts, out = refs[:4], refs[4]
    yl, x, k = ids[0], ids[1], ids[2]
    for s in range(4):
        for side_y in range(2):
            first = ((yl ^ side_y) * 4 + (x - s + 4) % 4) * 896
            columns = pl.ds(pl.multiple_of(first, 128), 896)
            mine = parts[s][:, side_y * 448 : (side_y + 1) * 448]
            other = parts[s][:, 896 + side_y * 448 : 896 + (side_y + 1) * 448]
            value = jnp.where(
                k == 0, jnp.concatenate([mine, other], axis=1), jnp.concatenate([other, mine], axis=1)
            )
            out[:, columns] = value.astype(jnp.bfloat16)


def tie_kernel(*refs):
    pass


def tie(values, others):
    free = pl.BlockSpec(memory_space=pl.ANY)
    return pl.pallas_call(
        tie_kernel,
        out_shape=[jax.ShapeDtypeStruct(v.shape, v.dtype) for v in values],
        in_specs=[free] * (len(values) + len(others)),
        out_specs=[free] * len(values),
        input_output_aliases={i: i for i in range(len(values))},
        compiler_params=pltpu.CompilerParams(vmem_limit_bytes=2**20),
        name="tie",
    )(*values, *others)


def simple(kernel, name, out_shape, args, scratch=()):
    full = pl.BlockSpec(memory_space=VMEM)
    return pl.pallas_call(
        kernel,
        out_shape=out_shape,
        in_specs=[pl.BlockSpec(memory_space=SMEM) if arg.dtype == jnp.int32 else full for arg in args],
        out_specs=jax.tree.map(lambda _: full, out_shape),
        scratch_shapes=scratch,
        compiler_params=pltpu.CompilerParams(vmem_limit_bytes=16 * 2**20),
        name=name,
    )(*args)


def turn(value, axis, size, shift):
    return lax.ppermute(value, axis, [((i + shift) % size, i) for i in range(size)])


def flip(value, axis, size, bits):
    return lax.ppermute(value, axis, [(i, i ^ bits) for i in range(size)])


def local(
    q_nope,
    q_rope,
    new_latent,
    new_rope,
    pool_latent,
    pool_rope,
    block_table,
    prefix_len,
    w_uk,
    w_uv,
    w_out,
):
    ids = jnp.stack(
        [
            lax.axis_index("yl"),
            lax.axis_index("x"),
            lax.axis_index("k"),
            lax.axis_index("zb"),
            lax.axis_index("z0") * 2 + lax.axis_index("yh"),
        ]
    ).astype(jnp.int32)
    query, pool = pack(q_nope, q_rope, pool_latent, pool_rope)
    weight = w_out.T

    queries = [query] + [turn(query, "x", 4, s) for s in (1, 2, 3)]
    pool_y = flip(pool, "yl", 2, 1)
    weight_z = flip(weight, "z0", 2, 1)
    lists, counts = plan(ids, block_table, prefix_len)
    pool_y, counts, weight_z = tie([pool_y, counts, weight_z], queries[1:])
    q_lat, q_rot = simple(
        prepare_kernel,
        "prepare",
        [
            jax.ShapeDtypeStruct((SLOTS, ROWS, LAT), jnp.bfloat16),
            jax.ShapeDtypeStruct((SLOTS, ROWS, ROPE), jnp.bfloat16),
        ],
        [counts, *queries, w_uk],
    )
    pool_k = flip(pool, "k", 2, 1)
    pool_yk = flip(pool_y, "k", 2, 1)
    pair = simple(
        pair_kernel, "pair", jax.ShapeDtypeStruct((2, 448, 512), jnp.bfloat16), [weight, weight_z]
    )
    ring = ("yl", "yh")
    mine = [pair, flip(pair, ring, 4, 2), flip(pair, ring, 4, 3)]
    pools = [pool, pool_y, pool_k, pool_yk]

    away = attention((1, 2, 3), False, lists, counts, q_lat, q_rot, pools, w_uv, ())
    came = [
        lax.ppermute(part, "x", [(i, (i + s) % 4) for i in range(4)]) for s, part in zip((1, 2, 3), away)
    ]
    (home,) = attention((0,), True, lists, counts, q_lat, q_rot, pools, w_uv, (new_latent, new_rope[0]))
    heads = simple(
        combine_kernel,
        "combine",
        [jax.ShapeDtypeStruct((32, HEADS * VD), jnp.bfloat16)] * 4,
        [ids, home, *came],
        scratch=[pltpu.VMEM((TOK, HEADS * VD), jnp.float32)],
    )
    heads = [heads[0]] + [flip(heads[d], ("z0", "yh"), 4, d) for d in (1, 2, 3)]
    heads = simple(join_kernel, "join", jax.ShapeDtypeStruct((32, 2048), jnp.bfloat16), heads)
    heads, mine[1], mine[2] = tie([heads, mine[1], mine[2]], [])
    far = [flip(mine[2][0], ring, 4, 2), flip(mine[1][1], ring, 4, 3)]
    heads = [heads] + [turn(heads, "x", 4, s) for s in (1, 2, 3)]
    heads[1], *far = tie([heads[1], *far], [])
    partial = simple(
        project_kernel,
        "project",
        [jax.ShapeDtypeStruct((64, 896), jnp.bfloat16)] * 4,
        [ids, *heads, *[flip(h, "k", 2, 1) for h in heads], *mine, *far],
        scratch=[pltpu.VMEM((256, 896), jnp.float32)],
    )
    sums = [partial[0]] + [
        lax.ppermute(partial[d], "zb", [(i, (i + d) % 4) for i in range(4)]) for d in (1, 2, 3)
    ]
    keep, give = simple(share_kernel, "share", [jax.ShapeDtypeStruct((32, 896), jnp.float32)] * 2, sums)
    pieces = simple(
        merge_kernel,
        "merge",
        [jax.ShapeDtypeStruct((8, 1792), jnp.float32)] * 4,
        [keep, flip(give, "k", 2, 1)],
    )
    pieces = [pieces[0]] + [
        lax.ppermute(pieces[s], "x", [(i, (i + s) % 4) for i in range(4)]) for s in (1, 2, 3)
    ]
    return simple(place_kernel, "place", jax.ShapeDtypeStruct((8, 7168), jnp.bfloat16), [ids, *pieces])


def solution(mesh):
    fine = Mesh(mesh.devices.reshape(2, 4, 2, 4, 2, 2), ("yl", "x", "k", "zb", "z0", "yh"))
    cache, head = ("yl", "x", "k"), ("zb", "z0", "yh")
    return jax.shard_map(
        local,
        mesh=fine,
        in_specs=(
            P(cache, head),
            P(cache, head),
            P(cache, None),
            P(cache, None, None),
            P(cache, None, None),
            P(cache, None, None),
            P(),
            P(),
            P(head, None, None),
            P(head, None, None),
            P(head, cache),
        ),
        out_specs=P(cache + head, None),
        check_vma=False,
    )
```

```python
import functools

import jax
import jax.numpy as jnp
from jax import lax
from jax.experimental import pallas as pl
from jax.experimental.pallas import tpu as pltpu
from jax.sharding import Mesh, PartitionSpec as P

LAT = 512
NOPE = 128
ROPE = 64
VD = 128
BLOCK = 128
HEADS = 4
TOK = 128
ROWS = HEADS * TOK
SLOTS = 4
STEP = 4
LOG2E = 1.4426950408889634
SCALE2 = (NOPE + ROPE) ** -0.5 * LOG2E
LOW = -1e30
STAT = HEADS * VD
MSG = STAT + 128

VMEM = pltpu.VMEM
SMEM = pltpu.SMEM


def dot_nn(a, b):
    return lax.dot_general(a, b, (((1,), (0,)), ((), ())), preferred_element_type=jnp.float32)


def dot_nt(a, b):
    return lax.dot_general(a, b, (((1,), (1,)), ((), ())), preferred_element_type=jnp.float32)


def plan_kernel(ids, table, lens, lists, counts):
    yl, x, k = ids[0], ids[1], ids[2]
    for s in range(SLOTS):
        limit = lens[yl * 8 + ((x + s) % 4) * 2 + k]

        def scan(m, carry):
            found, valid = carry
            block = table[yl * 8 + ((x + s) % 4) * 2 + k, m]
            owner = block >> 2
            here = ((owner >> 1) & 3) == x

            @pl.when(here)
            def _():
                source = ((owner >> 3) ^ yl) + 2 * ((owner & 1) ^ k)
                lists[s * 16 + found] = source * 4 + (block & 3)

            step = here.astype(jnp.int32)
            return found + step, valid + step * jnp.minimum(limit - m * BLOCK, BLOCK)

        blocks = jnp.minimum((limit + BLOCK - 1) // BLOCK, 32)
        found, valid = lax.fori_loop(0, blocks, scan, (jnp.int32(0), jnp.int32(0)))
        counts[s] = found
        counts[SLOTS + s] = valid


def plan(ids, table, lens):
    scalar = pl.BlockSpec(memory_space=SMEM)
    return pl.pallas_call(
        plan_kernel,
        out_shape=[jax.ShapeDtypeStruct((SLOTS * 16,), jnp.int32), jax.ShapeDtypeStruct((2 * SLOTS,), jnp.int32)],
        in_specs=[scalar] * 3,
        out_specs=[scalar] * 2,
        compiler_params=pltpu.CompilerParams(vmem_limit_bytes=2**20),
        name="plan",
    )(ids, table, lens)


def prepare_kernel(counts, *refs):
    queries = refs[:SLOTS]
    w_uk, q_lat, q_rot = refs[SLOTS : SLOTS + 3]
    for h in range(HEADS):
        rows = slice(h * TOK, (h + 1) * TOK)
        part = jnp.concatenate([q[:, h * NOPE : (h + 1) * NOPE] for q in queries], axis=0)
        part = dot_nn(part, w_uk[h]).astype(jnp.bfloat16)
        first = HEADS * NOPE + h * ROPE
        for s in range(SLOTS):
            q_lat[s, rows, :] = part[s * TOK : (s + 1) * TOK]
            q_rot[s, rows, :] = queries[s][:, first : first + ROPE]


def attention_kernel(slots, own, lists, counts, q_lat, q_rot, *refs):
    count = len(slots)
    refs = list(refs)

    def take(n):
        got = refs[:n]
        del refs[:n]
        return got

    pools = take(4)
    (w_uv,) = take(1)
    new_latent, new_rope = take(2) if own else (None, None)
    outs = take(count)
    keys, rots, acc, top, tot, latents, levels = refs
    keys[...] = jnp.zeros_like(keys)
    rots[...] = jnp.zeros_like(rots)

    def wide(value, times):
        return jnp.concatenate([value] * times, axis=1)

    def begin(score, latent):
        best = jnp.broadcast_to(jnp.max(score, axis=1, keepdims=True), (ROWS, 128))
        times = score.shape[1] // 128
        weight = jnp.exp2((score - wide(best, times)) * SCALE2)
        top[...] = best
        tot[...] = sum(weight[:, i * 128 : (i + 1) * 128] for i in range(times))
        acc[...] = dot_nn(weight.astype(jnp.bfloat16), latent)

    def scores(slot, found, valid, q, r, chunk):
        for b in range(STEP):
            part = slice(b * BLOCK, (b + 1) * BLOCK)
            code = lists[slot * 16 + chunk * STEP + b]
            first = pl.multiple_of((code & 3) * BLOCK, BLOCK)
            for j in range(4):

                @pl.when(jnp.logical_and(chunk * STEP + b < found, (code >> 2) == j))
                def _():
                    keys[part, :] = pools[j][pl.ds(first, BLOCK), :]
                    rots[:, part] = pools[j][4 * BLOCK :, pl.ds(first, BLOCK)]

        score = dot_nt(q, keys[...]) + dot_nn(r, rots[...])
        seen = lax.broadcasted_iota(jnp.int32, score.shape, 1) < valid - chunk * STEP * BLOCK
        return jnp.where(seen, score, LOW)

    def one_slot(s, carry):
        slot = s + slots[0]
        found, valid = counts[slot], counts[SLOTS + slot]
        q, r = q_lat[slot], q_rot[slot]
        if own:
            score = dot_nt(q, new_latent[...]) + dot_nn(r, new_rope[...])
            at = lax.broadcasted_iota(jnp.int32, score.shape, 0) % TOK
            seen = lax.broadcasted_iota(jnp.int32, score.shape, 1) <= at
            begin(jnp.where(seen, score, LOW), new_latent[...])
        else:
            begin(scores(slot, found, valid, q, r, 0), keys[...])

        def step(chunk, inner):
            score = scores(slot, found, valid, q_lat[slot], q_rot[slot], chunk)
            before = top[...]
            best = jnp.maximum(before, jnp.max(score, axis=1, keepdims=True))
            keep = jnp.exp2((before - best) * SCALE2)
            weight = jnp.exp2((score - wide(best, STEP)) * SCALE2)
            top[...] = best
            tot[...] = tot[...] * keep + sum(weight[:, i * 128 : (i + 1) * 128] for i in range(STEP))
            acc[...] = acc[...] * wide(keep, 4) + dot_nn(weight.astype(jnp.bfloat16), keys[...])
            return inner

        lax.fori_loop(0 if own else 1, (found + STEP - 1) // STEP, step, 0)
        total = jnp.broadcast_to(jnp.sum(tot[...], axis=1, keepdims=True), (ROWS, 128))
        latents[s] = (acc[...] * wide(1.0 / total, 4)).astype(jnp.bfloat16)
        level = top[...] * SCALE2 + jnp.log2(total)
        levels[s] = level if own else jnp.where(found > 0, level, LOW)
        return carry

    lax.fori_loop(0, count, one_slot, 0)
    lane = lax.broadcasted_iota(jnp.int32, (TOK, 128), 1)
    for h in range(HEADS):
        rows = slice(h * TOK, (h + 1) * TOK)
        part = jnp.concatenate([latents[s, rows, :] for s in range(count)], axis=0)
        part = dot_nn(part, w_uv[h]).astype(jnp.bfloat16)
        for s in range(count):
            outs[s][:, h * VD : (h + 1) * VD] = part[s * TOK : (s + 1) * TOK]
    for s in range(count):
        level = levels[s, 0:TOK, :]
        for h in range(1, HEADS):
            level = jnp.where(lane % HEADS == h, levels[s, h * TOK : (h + 1) * TOK, :], level)
        high = level.astype(jnp.bfloat16).astype(jnp.float32)
        middle = (level - high).astype(jnp.bfloat16).astype(jnp.float32)
        low = level - high - middle
        stat = jnp.where(lane < HEADS, high, jnp.where(lane < 2 * HEADS, middle, low))
        outs[s][:, STAT:] = stat.astype(jnp.bfloat16)


def attention(slots, own, lists, counts, q_lat, q_rot, pools, w_uv, fresh):
    count = len(slots)
    full = pl.BlockSpec(memory_space=VMEM)
    scalar = pl.BlockSpec(memory_space=SMEM)
    return pl.pallas_call(
        functools.partial(attention_kernel, slots, own),
        out_shape=[jax.ShapeDtypeStruct((TOK, MSG), jnp.bfloat16)] * count,
        in_specs=[scalar] * 2 + [full] * (9 if own else 7),
        out_specs=[full] * count,
        scratch_shapes=[
            pltpu.VMEM((STEP * BLOCK, LAT), jnp.bfloat16),
            pltpu.VMEM((ROPE, STEP * BLOCK), jnp.bfloat16),
            pltpu.VMEM((ROWS, LAT), jnp.float32),
            pltpu.VMEM((ROWS, 128), jnp.float32),
            pltpu.VMEM((ROWS, 128), jnp.float32),
            pltpu.VMEM((count, ROWS, LAT), jnp.bfloat16),
            pltpu.VMEM((count, ROWS, 128), jnp.float32),
        ],
        compiler_params=pltpu.CompilerParams(vmem_limit_bytes=24 * 2**20),
        name="attend",
    )(lists, counts, q_lat, q_rot, *pools, w_uv, *fresh)


def combine_kernel(ids, *refs):
    parts, outs, total = refs[:SLOTS], refs[SLOTS : SLOTS + 4], refs[SLOTS + 4]
    a = ids[4]
    stats = [p[:, STAT:].astype(jnp.float32) for p in parts]
    for h in range(HEADS):
        columns = slice(h * VD, (h + 1) * VD)
        levels = [
            s[:, h : h + 1] + s[:, HEADS + h : HEADS + h + 1] + s[:, 2 * HEADS + h : 2 * HEADS + h + 1]
            for s in stats
        ]
        best = functools.reduce(jnp.maximum, levels)
        shares = [jnp.exp2(v - best) for v in levels]
        inverse = 1.0 / sum(shares)
        total[:, columns] = sum(
            p[:, columns].astype(jnp.float32) * (share * inverse) for p, share in zip(parts, shares)
        )
    for d in range(4):
        first = pl.multiple_of((a ^ d) * 8, 8)
        rows = [total[pl.ds(first + q * 32, 8), :] for q in range(4)]
        outs[d][...] = jnp.concatenate(rows, axis=0).astype(jnp.bfloat16)


def join_kernel(*refs):
    for d in range(4):
        refs[4][:, d * 512 : (d + 1) * 512] = refs[d][...]


def pack_kernel(q_nope, q_rope, pool_latent, pool_rope, query, pool, sems):
    moves = [(q_nope, query.at[:, : HEADS * NOPE]), (q_rope, query.at[:, HEADS * NOPE :])]
    for i in range(4):
        moves.append((pool_latent.at[i], pool.at[i * BLOCK : (i + 1) * BLOCK, :]))
        moves.append((pool_rope.at[i], pool.at[4 * BLOCK :, i * BLOCK : (i + 1) * BLOCK]))
    copies = [pltpu.make_async_copy(src, dst, sems.at[i]) for i, (src, dst) in enumerate(moves)]
    for copy in copies:
        copy.start()
    for copy in copies:
        copy.wait()


def pack(*args):
    return pl.pallas_call(
        pack_kernel,
        out_shape=[
            jax.ShapeDtypeStruct((TOK, HEADS * (NOPE + ROPE)), jnp.bfloat16),
            jax.ShapeDtypeStruct((4 * BLOCK + ROPE, LAT), jnp.bfloat16),
        ],
        in_specs=[pl.BlockSpec(memory_space=pltpu.HBM)] * 4,
        out_specs=[pl.BlockSpec(memory_space=VMEM)] * 2,
        scratch_shapes=[pltpu.SemaphoreType.DMA((10,))],
        compiler_params=pltpu.CompilerParams(vmem_limit_bytes=56 * 2**20),
        name="pack",
    )(*args)


def pair_kernel(one, two, out):
    out[0] = one[...]
    out[1] = two[...]


def project_kernel(ids, *refs):
    heads = refs[:8]
    pair, near, next_, far_one, far_two = refs[8:13]
    outs, total = refs[13:17], refs[17]
    zb = ids[3]
    rows = jnp.concatenate([h[...] for h in heads], axis=0)
    sides = []
    for side_y in range(2):
        value = None
        for d in range(4):
            dz = d >> 1
            if side_y == 0:
                weight = pair[dz] if d & 1 == 0 else (far_one, far_two)[dz][...]
            else:
                weight = (near, next_)[d & 1][dz]
            part = dot_nt(weight, rows[:, d * 512 : (d + 1) * 512])
            value = part if value is None else value + part
        sides.append(value)
    total[...] = jnp.concatenate(sides, axis=0).T
    for d in range(4):
        first = pl.multiple_of(((zb + d) % 4) * 8, 8)
        parts = [total[pl.ds(first + s * 32, 8), :] for s in range(8)]
        outs[d][...] = jnp.concatenate(parts, axis=0).astype(jnp.bfloat16)


def share_kernel(*refs):
    total = sum(p[...].astype(jnp.float32) for p in refs[:4])
    refs[4][...] = total[:32]
    refs[5][...] = total[32:]


def merge_kernel(keep, got, *outs):
    for s in range(4):
        outs[s][:, :896] = keep[s * 8 : (s + 1) * 8, :]
        outs[s][:, 896:] = got[s * 8 : (s + 1) * 8, :]


def place_kernel(ids, *refs):
    parts, out = refs[:4], refs[4]
    yl, x, k = ids[0], ids[1], ids[2]
    for s in range(4):
        for side_y in range(2):
            first = ((yl ^ side_y) * 4 + (x - s + 4) % 4) * 896
            columns = pl.ds(pl.multiple_of(first, 128), 896)
            mine = parts[s][:, side_y * 448 : (side_y + 1) * 448]
            other = parts[s][:, 896 + side_y * 448 : 896 + (side_y + 1) * 448]
            value = jnp.where(
                k == 0, jnp.concatenate([mine, other], axis=1), jnp.concatenate([other, mine], axis=1)
            )
            out[:, columns] = value.astype(jnp.bfloat16)


def tie_kernel(*refs):
    pass


def tie(values, others):
    free = pl.BlockSpec(memory_space=pl.ANY)
    return pl.pallas_call(
        tie_kernel,
        out_shape=[jax.ShapeDtypeStruct(v.shape, v.dtype) for v in values],
        in_specs=[free] * (len(values) + len(others)),
        out_specs=[free] * len(values),
        input_output_aliases={i: i for i in range(len(values))},
        compiler_params=pltpu.CompilerParams(vmem_limit_bytes=2**20),
        name="tie",
    )(*values, *others)


def simple(kernel, name, out_shape, args, scratch=()):
    full = pl.BlockSpec(memory_space=VMEM)
    return pl.pallas_call(
        kernel,
        out_shape=out_shape,
        in_specs=[pl.BlockSpec(memory_space=SMEM) if arg.dtype == jnp.int32 else full for arg in args],
        out_specs=jax.tree.map(lambda _: full, out_shape),
        scratch_shapes=scratch,
        compiler_params=pltpu.CompilerParams(vmem_limit_bytes=16 * 2**20),
        name=name,
    )(*args)


def turn(value, axis, size, shift):
    return lax.ppermute(value, axis, [((i + shift) % size, i) for i in range(size)])


def flip(value, axis, size, bits):
    return lax.ppermute(value, axis, [(i, i ^ bits) for i in range(size)])


def local(
    q_nope,
    q_rope,
    new_latent,
    new_rope,
    pool_latent,
    pool_rope,
    block_table,
    prefix_len,
    w_uk,
    w_uv,
    w_out,
):
    ids = jnp.stack(
        [
            lax.axis_index("yl"),
            lax.axis_index("x"),
            lax.axis_index("k"),
            lax.axis_index("zb"),
            lax.axis_index("z0") * 2 + lax.axis_index("yh"),
        ]
    ).astype(jnp.int32)
    query, pool = pack(q_nope, q_rope, pool_latent, pool_rope)
    weight = w_out.T

    queries = [query] + [turn(query, "x", 4, s) for s in (1, 2, 3)]
    pool_y = flip(pool, "yl", 2, 1)
    weight_z = flip(weight, "z0", 2, 1)
    lists, counts = plan(ids, block_table, prefix_len)
    pool_y, counts, weight_z = tie([pool_y, counts, weight_z], queries[1:])
    q_lat, q_rot = simple(
        prepare_kernel,
        "prepare",
        [
            jax.ShapeDtypeStruct((SLOTS, ROWS, LAT), jnp.bfloat16),
            jax.ShapeDtypeStruct((SLOTS, ROWS, ROPE), jnp.bfloat16),
        ],
        [counts, *queries, w_uk],
    )
    pool_k = flip(pool, "k", 2, 1)
    pool_yk = flip(pool_y, "k", 2, 1)
    pair = simple(
        pair_kernel, "pair", jax.ShapeDtypeStruct((2, 448, 512), jnp.bfloat16), [weight, weight_z]
    )
    ring = ("yl", "yh")
    mine = [pair, flip(pair, ring, 4, 2), flip(pair, ring, 4, 3)]
    pools = [pool, pool_y, pool_k, pool_yk]

    away = attention((1, 2, 3), False, lists, counts, q_lat, q_rot, pools, w_uv, ())
    came = [
        lax.ppermute(part, "x", [(i, (i + s) % 4) for i in range(4)]) for s, part in zip((1, 2, 3), away)
    ]
    (home,) = attention((0,), True, lists, counts, q_lat, q_rot, pools, w_uv, (new_latent, new_rope[0]))
    heads = simple(
        combine_kernel,
        "combine",
        [jax.ShapeDtypeStruct((32, HEADS * VD), jnp.bfloat16)] * 4,
        [ids, home, *came],
        scratch=[pltpu.VMEM((TOK, HEADS * VD), jnp.float32)],
    )
    heads = [heads[0]] + [flip(heads[d], ("z0", "yh"), 4, d) for d in (1, 2, 3)]
    heads = simple(join_kernel, "join", jax.ShapeDtypeStruct((32, 2048), jnp.bfloat16), heads)
    heads, mine[1], mine[2] = tie([heads, mine[1], mine[2]], [])
    far = [flip(mine[2][0], ring, 4, 2), flip(mine[1][1], ring, 4, 3)]
    heads = [heads] + [turn(heads, "x", 4, s) for s in (1, 2, 3)]
    heads[1], *far = tie([heads[1], *far], [])
    partial = simple(
        project_kernel,
        "project",
        [jax.ShapeDtypeStruct((64, 896), jnp.bfloat16)] * 4,
        [ids, *heads, *[flip(h, "k", 2, 1) for h in heads], *mine, *far],
        scratch=[pltpu.VMEM((256, 896), jnp.float32)],
    )
    sums = [partial[0]] + [
        lax.ppermute(partial[d], "zb", [(i, (i + d) % 4) for i in range(4)]) for d in (1, 2, 3)
    ]
    keep, give = simple(share_kernel, "share", [jax.ShapeDtypeStruct((32, 896), jnp.float32)] * 2, sums)
    pieces = simple(
        merge_kernel,
        "merge",
        [jax.ShapeDtypeStruct((8, 1792), jnp.float32)] * 4,
        [keep, flip(give, "k", 2, 1)],
    )
    pieces = [pieces[0]] + [
        lax.ppermute(pieces[s], "x", [(i, (i + s) % 4) for i in range(4)]) for s in (1, 2, 3)
    ]
    return simple(place_kernel, "place", jax.ShapeDtypeStruct((8, 7168), jnp.bfloat16), [ids, *pieces])


def solution(mesh):
    fine = Mesh(mesh.devices.reshape(2, 4, 2, 4, 2, 2), ("yl", "x", "k", "zb", "z0", "yh"))
    cache, head = ("yl", "x", "k"), ("zb", "z0", "yh")
    return jax.shard_map(
        local,
        mesh=fine,
        in_specs=(
            P(cache, head),
            P(cache, head),
            P(cache, None),
            P(cache, None, None),
            P(cache, None, None),
            P(cache, None, None),
            P(),
            P(),
            P(head, None, None),
            P(head, None, None),
            P(head, cache),
        ),
        out_specs=P(cache + head, None),
        check_vma=False,
    )
```

```python
import functools

import jax
import jax.numpy as jnp
from jax import lax
from jax.experimental import pallas as pl
from jax.experimental.pallas import tpu as pltpu
from jax.sharding import Mesh, PartitionSpec as P

LAT = 512
NOPE = 128
ROPE = 64
VD = 128
BLOCK = 128
HEADS = 4
TOK = 128
ROWS = HEADS * TOK
SLOTS = 4
STEP = 4
LOG2E = 1.4426950408889634
SCALE2 = (NOPE + ROPE) ** -0.5 * LOG2E
LOW = -1e30
STAT = HEADS * VD
MSG = STAT + 128

VMEM = pltpu.VMEM
SMEM = pltpu.SMEM


def dot_nn(a, b):
    return lax.dot_general(a, b, (((1,), (0,)), ((), ())), preferred_element_type=jnp.float32)


def dot_nt(a, b):
    return lax.dot_general(a, b, (((1,), (1,)), ((), ())), preferred_element_type=jnp.float32)


def plan_kernel(ids, table, lens, lists, counts):
    yl, x, k = ids[0], ids[1], ids[2]
    for s in range(SLOTS):
        limit = lens[yl * 8 + ((x + s) % 4) * 2 + k]

        def scan(m, carry):
            found, valid = carry
            block = table[yl * 8 + ((x + s) % 4) * 2 + k, m]
            owner = block >> 2
            here = ((owner >> 1) & 3) == x

            @pl.when(here)
            def _():
                source = ((owner >> 3) ^ yl) + 2 * ((owner & 1) ^ k)
                lists[s * 16 + found] = source * 4 + (block & 3)

            step = here.astype(jnp.int32)
            return found + step, valid + step * jnp.minimum(limit - m * BLOCK, BLOCK)

        blocks = jnp.minimum((limit + BLOCK - 1) // BLOCK, 32)
        found, valid = lax.fori_loop(0, blocks, scan, (jnp.int32(0), jnp.int32(0)))
        counts[s] = found
        counts[SLOTS + s] = valid


def plan(ids, table, lens):
    scalar = pl.BlockSpec(memory_space=SMEM)
    return pl.pallas_call(
        plan_kernel,
        out_shape=[jax.ShapeDtypeStruct((SLOTS * 16,), jnp.int32), jax.ShapeDtypeStruct((2 * SLOTS,), jnp.int32)],
        in_specs=[scalar] * 3,
        out_specs=[scalar] * 2,
        compiler_params=pltpu.CompilerParams(vmem_limit_bytes=2**20),
        name="plan",
    )(ids, table, lens)


def prepare_kernel(counts, *refs):
    queries = refs[:SLOTS]
    w_uk, q_lat, q_rot = refs[SLOTS : SLOTS + 3]
    for h in range(HEADS):
        rows = slice(h * TOK, (h + 1) * TOK)
        part = jnp.concatenate([q[:, h * NOPE : (h + 1) * NOPE] for q in queries], axis=0)
        part = dot_nn(part, w_uk[h]).astype(jnp.bfloat16)
        first = HEADS * NOPE + h * ROPE
        for s in range(SLOTS):
            q_lat[s, rows, :] = part[s * TOK : (s + 1) * TOK]
            q_rot[s, rows, :] = queries[s][:, first : first + ROPE]


def attention_kernel(slots, own, lists, counts, q_lat, q_rot, *refs):
    count = len(slots)
    refs = list(refs)

    def take(n):
        got = refs[:n]
        del refs[:n]
        return got

    pools = take(4)
    (w_uv,) = take(1)
    new_latent, new_rope = take(2) if own else (None, None)
    outs = take(count)
    keys, rots, acc, top, tot, latents, levels = refs
    keys[...] = jnp.zeros_like(keys)
    rots[...] = jnp.zeros_like(rots)

    def wide(value, times):
        return jnp.concatenate([value] * times, axis=1)

    def begin(score, latent):
        best = jnp.broadcast_to(jnp.max(score, axis=1, keepdims=True), (ROWS, 128))
        times = score.shape[1] // 128
        weight = jnp.exp2((score - wide(best, times)) * SCALE2)
        top[...] = best
        tot[...] = sum(weight[:, i * 128 : (i + 1) * 128] for i in range(times))
        acc[...] = dot_nn(weight.astype(jnp.bfloat16), latent)

    def scores(slot, found, valid, q, r, chunk):
        for b in range(STEP):
            part = slice(b * BLOCK, (b + 1) * BLOCK)
            code = lists[slot * 16 + chunk * STEP + b]
            first = pl.multiple_of((code & 3) * BLOCK, BLOCK)
            for j in range(4):

                @pl.when(jnp.logical_and(chunk * STEP + b < found, (code >> 2) == j))
                def _():
                    keys[part, :] = pools[j][pl.ds(first, BLOCK), :]
                    rots[:, part] = pools[j][4 * BLOCK :, pl.ds(first, BLOCK)]

        score = dot_nt(q, keys[...]) + dot_nn(r, rots[...])
        seen = lax.broadcasted_iota(jnp.int32, score.shape, 1) < valid - chunk * STEP * BLOCK
        return jnp.where(seen, score, LOW)

    def one_slot(s, carry):
        slot = s + slots[0]
        found, valid = counts[slot], counts[SLOTS + slot]
        q, r = q_lat[slot], q_rot[slot]
        if own:
            score = dot_nt(q, new_latent[...]) + dot_nn(r, new_rope[...])
            at = lax.broadcasted_iota(jnp.int32, score.shape, 0) % TOK
            seen = lax.broadcasted_iota(jnp.int32, score.shape, 1) <= at
            begin(jnp.where(seen, score, LOW), new_latent[...])
        else:
            begin(scores(slot, found, valid, q, r, 0), keys[...])

        def step(chunk, inner):
            score = scores(slot, found, valid, q_lat[slot], q_rot[slot], chunk)
            before = top[...]
            best = jnp.maximum(before, jnp.max(score, axis=1, keepdims=True))
            keep = jnp.exp2((before - best) * SCALE2)
            weight = jnp.exp2((score - wide(best, STEP)) * SCALE2)
            top[...] = best
            tot[...] = tot[...] * keep + sum(weight[:, i * 128 : (i + 1) * 128] for i in range(STEP))
            acc[...] = acc[...] * wide(keep, 4) + dot_nn(weight.astype(jnp.bfloat16), keys[...])
            return inner

        lax.fori_loop(0 if own else 1, (found + STEP - 1) // STEP, step, 0)
        total = jnp.broadcast_to(jnp.sum(tot[...], axis=1, keepdims=True), (ROWS, 128))
        latents[s] = (acc[...] * wide(1.0 / total, 4)).astype(jnp.bfloat16)
        level = top[...] * SCALE2 + jnp.log2(total)
        levels[s] = level if own else jnp.where(found > 0, level, LOW)
        return carry

    lax.fori_loop(0, count, one_slot, 0)
    lane = lax.broadcasted_iota(jnp.int32, (TOK, 128), 1)
    for h in range(HEADS):
        rows = slice(h * TOK, (h + 1) * TOK)
        part = jnp.concatenate([latents[s, rows, :] for s in range(count)], axis=0)
        part = dot_nn(part, w_uv[h]).astype(jnp.bfloat16)
        for s in range(count):
            outs[s][:, h * VD : (h + 1) * VD] = part[s * TOK : (s + 1) * TOK]
    for s in range(count):
        level = levels[s, 0:TOK, :]
        for h in range(1, HEADS):
            level = jnp.where(lane % HEADS == h, levels[s, h * TOK : (h + 1) * TOK, :], level)
        high = level.astype(jnp.bfloat16).astype(jnp.float32)
        middle = (level - high).astype(jnp.bfloat16).astype(jnp.float32)
        low = level - high - middle
        stat = jnp.where(lane < HEADS, high, jnp.where(lane < 2 * HEADS, middle, low))
        outs[s][:, STAT:] = stat.astype(jnp.bfloat16)


def attention(slots, own, lists, counts, q_lat, q_rot, pools, w_uv, fresh):
    count = len(slots)
    full = pl.BlockSpec(memory_space=VMEM)
    scalar = pl.BlockSpec(memory_space=SMEM)
    return pl.pallas_call(
        functools.partial(attention_kernel, slots, own),
        out_shape=[jax.ShapeDtypeStruct((TOK, MSG), jnp.bfloat16)] * count,
        in_specs=[scalar] * 2 + [full] * (9 if own else 7),
        out_specs=[full] * count,
        scratch_shapes=[
            pltpu.VMEM((STEP * BLOCK, LAT), jnp.bfloat16),
            pltpu.VMEM((ROPE, STEP * BLOCK), jnp.bfloat16),
            pltpu.VMEM((ROWS, LAT), jnp.float32),
            pltpu.VMEM((ROWS, 128), jnp.float32),
            pltpu.VMEM((ROWS, 128), jnp.float32),
            pltpu.VMEM((count, ROWS, LAT), jnp.bfloat16),
            pltpu.VMEM((count, ROWS, 128), jnp.float32),
        ],
        compiler_params=pltpu.CompilerParams(vmem_limit_bytes=24 * 2**20),
        name="attend",
    )(lists, counts, q_lat, q_rot, *pools, w_uv, *fresh)


def combine_kernel(ids, *refs):
    parts, outs, total = refs[:SLOTS], refs[SLOTS : SLOTS + 4], refs[SLOTS + 4]
    a = ids[4]
    stats = [p[:, STAT:].astype(jnp.float32) for p in parts]
    for h in range(HEADS):
        columns = slice(h * VD, (h + 1) * VD)
        levels = [
            s[:, h : h + 1] + s[:, HEADS + h : HEADS + h + 1] + s[:, 2 * HEADS + h : 2 * HEADS + h + 1]
            for s in stats
        ]
        best = functools.reduce(jnp.maximum, levels)
        shares = [jnp.exp2(v - best) for v in levels]
        inverse = 1.0 / sum(shares)
        total[:, columns] = sum(
            p[:, columns].astype(jnp.float32) * (share * inverse) for p, share in zip(parts, shares)
        )
    for d in range(4):
        first = pl.multiple_of((a ^ d) * 8, 8)
        rows = [total[pl.ds(first + q * 32, 8), :] for q in range(4)]
        outs[d][...] = jnp.concatenate(rows, axis=0).astype(jnp.bfloat16)


def join_kernel(*refs):
    for d in range(4):
        refs[4][:, d * 512 : (d + 1) * 512] = refs[d][...]


def pack_kernel(q_nope, q_rope, pool_latent, pool_rope, query, pool, sems):
    moves = [(q_nope, query.at[:, : HEADS * NOPE]), (q_rope, query.at[:, HEADS * NOPE :])]
    for i in range(4):
        moves.append((pool_latent.at[i], pool.at[i * BLOCK : (i + 1) * BLOCK, :]))
        moves.append((pool_rope.at[i], pool.at[4 * BLOCK :, i * BLOCK : (i + 1) * BLOCK]))
    copies = [pltpu.make_async_copy(src, dst, sems.at[i]) for i, (src, dst) in enumerate(moves)]
    for copy in copies:
        copy.start()
    for copy in copies:
        copy.wait()


def pack(*args):
    return pl.pallas_call(
        pack_kernel,
        out_shape=[
            jax.ShapeDtypeStruct((TOK, HEADS * (NOPE + ROPE)), jnp.bfloat16),
            jax.ShapeDtypeStruct((4 * BLOCK + ROPE, LAT), jnp.bfloat16),
        ],
        in_specs=[pl.BlockSpec(memory_space=pltpu.HBM)] * 4,
        out_specs=[pl.BlockSpec(memory_space=VMEM)] * 2,
        scratch_shapes=[pltpu.SemaphoreType.DMA((10,))],
        compiler_params=pltpu.CompilerParams(vmem_limit_bytes=56 * 2**20),
        name="pack",
    )(*args)


def pair_kernel(one, two, out):
    out[0] = one[...]
    out[1] = two[...]


def stack_kernel(*refs):
    for s in range(4):
        refs[4][s] = refs[s][...]


def project_kernel(ids, own, other, pair, near, next_, far_one, far_two, *refs):
    outs, total = refs[:4], refs[4]
    zb = ids[3]
    rows = jnp.concatenate([own[...].reshape(TOK, 2048), other[...].reshape(TOK, 2048)], axis=0)
    sides = []
    for side_y in range(2):
        value = None
        for d in range(4):
            dz = d >> 1
            if side_y == 0:
                weight = pair[dz] if d & 1 == 0 else (far_one, far_two)[dz][...]
            else:
                weight = (near, next_)[d & 1][dz]
            part = dot_nt(weight, rows[:, d * 512 : (d + 1) * 512])
            value = part if value is None else value + part
        sides.append(value)
    total[...] = jnp.concatenate(sides, axis=0).T
    for d in range(4):
        first = pl.multiple_of(((zb + d) % 4) * 8, 8)
        parts = [total[pl.ds(first + s * 32, 8), :] for s in range(8)]
        outs[d][...] = jnp.concatenate(parts, axis=0).astype(jnp.bfloat16)


def share_kernel(*refs):
    total = sum(p[...].astype(jnp.float32) for p in refs[:4])
    refs[4][...] = total[:32].astype(jnp.bfloat16)
    refs[5][...] = total[32:].astype(jnp.bfloat16)


def merge_kernel(keep, got, *outs):
    own, other = keep[...].astype(jnp.float32), got[...].astype(jnp.float32)
    for s in range(4):
        rows = slice(s * 8, (s + 1) * 8)
        outs[s][...] = jnp.concatenate([own[rows], other[rows]], axis=0).astype(jnp.bfloat16)


def place_kernel(ids, *refs):
    parts, out = refs[:4], refs[4]
    yl, x, k = ids[0], ids[1], ids[2]
    for core in range(2):

        @pl.when(k == core)
        def _():
            for s in range(4):
                value = parts[s][...].astype(jnp.float32)
                pair = (value[:8], value[8:]) if core == 0 else (value[8:], value[:8])
                for side_y in range(2):
                    first = ((yl ^ side_y) * 4 + (x - s + 4) % 4) * 896
                    cut = slice(side_y * 448, (side_y + 1) * 448)
                    joined = jnp.concatenate([pair[0][:, cut], pair[1][:, cut]], axis=1)
                    out[:, pl.ds(pl.multiple_of(first, 128), 896)] = joined.astype(jnp.bfloat16)


def tie_kernel(*refs):
    pass


def tie(values, others):
    free = pl.BlockSpec(memory_space=pl.ANY)
    return pl.pallas_call(
        tie_kernel,
        out_shape=[jax.ShapeDtypeStruct(v.shape, v.dtype) for v in values],
        in_specs=[free] * (len(values) + len(others)),
        out_specs=[free] * len(values),
        input_output_aliases={i: i for i in range(len(values))},
        compiler_params=pltpu.CompilerParams(vmem_limit_bytes=2**20),
        name="tie",
    )(*values, *others)


def simple(kernel, name, out_shape, args, scratch=()):
    full = pl.BlockSpec(memory_space=VMEM)
    return pl.pallas_call(
        kernel,
        out_shape=out_shape,
        in_specs=[pl.BlockSpec(memory_space=SMEM) if arg.dtype == jnp.int32 else full for arg in args],
        out_specs=jax.tree.map(lambda _: full, out_shape),
        scratch_shapes=scratch,
        compiler_params=pltpu.CompilerParams(vmem_limit_bytes=16 * 2**20),
        name=name,
    )(*args)


def turn(value, axis, size, shift):
    return lax.ppermute(value, axis, [((i + shift) % size, i) for i in range(size)])


def flip(value, axis, size, bits):
    return lax.ppermute(value, axis, [(i, i ^ bits) for i in range(size)])


def local(
    q_nope,
    q_rope,
    new_latent,
    new_rope,
    pool_latent,
    pool_rope,
    block_table,
    prefix_len,
    w_uk,
    w_uv,
    w_out,
):
    ids = jnp.stack(
        [
            lax.axis_index("yl"),
            lax.axis_index("x"),
            lax.axis_index("k"),
            lax.axis_index("zb"),
            lax.axis_index("z0") * 2 + lax.axis_index("yh"),
        ]
    ).astype(jnp.int32)
    query, pool = pack(q_nope, q_rope, pool_latent, pool_rope)
    weight = w_out.T

    queries = [query] + [turn(query, "x", 4, s) for s in (1, 2, 3)]
    pool_y = flip(pool, "yl", 2, 1)
    weight_z = flip(weight, "z0", 2, 1)
    lists, counts = plan(ids, block_table, prefix_len)
    pool_y, counts, weight_z = tie([pool_y, counts, weight_z], queries[1:])
    q_lat, q_rot = simple(
        prepare_kernel,
        "prepare",
        [
            jax.ShapeDtypeStruct((SLOTS, ROWS, LAT), jnp.bfloat16),
            jax.ShapeDtypeStruct((SLOTS, ROWS, ROPE), jnp.bfloat16),
        ],
        [counts, *queries, w_uk],
    )
    pool_k = flip(pool, "k", 2, 1)
    pool_yk = flip(pool_y, "k", 2, 1)
    pair = simple(
        pair_kernel, "pair", jax.ShapeDtypeStruct((2, 448, 512), jnp.bfloat16), [weight, weight_z]
    )
    ring = ("yl", "yh")
    mine = [pair, flip(pair, ring, 4, 2), flip(pair, ring, 4, 3)]
    pools = [pool, pool_y, pool_k, pool_yk]

    away = attention((1, 2, 3), False, lists, counts, q_lat, q_rot, pools, w_uv, ())
    came = [
        lax.ppermute(part, "x", [(i, (i + s) % 4) for i in range(4)]) for s, part in zip((1, 2, 3), away)
    ]
    (home,) = attention((0,), True, lists, counts, q_lat, q_rot, pools, w_uv, (new_latent, new_rope[0]))
    heads = simple(
        combine_kernel,
        "combine",
        [jax.ShapeDtypeStruct((32, HEADS * VD), jnp.bfloat16)] * 4,
        [ids, home, *came],
        scratch=[pltpu.VMEM((TOK, HEADS * VD), jnp.float32)],
    )
    heads = [heads[0]] + [flip(heads[d], ("z0", "yh"), 4, d) for d in (1, 2, 3)]
    heads = simple(join_kernel, "join", jax.ShapeDtypeStruct((32, 2048), jnp.bfloat16), heads)
    heads, mine[1], mine[2] = tie([heads, mine[1], mine[2]], [])
    far = [flip(mine[2][0], ring, 4, 2), flip(mine[1][1], ring, 4, 3)]
    heads = [heads] + [turn(heads, "x", 4, s) for s in (1, 2, 3)]
    heads[3], *far = tie([heads[3], *far], [])
    heads = simple(stack_kernel, "stack", jax.ShapeDtypeStruct((4, 32, 2048), jnp.bfloat16), heads)
    partial = simple(
        project_kernel,
        "project",
        [jax.ShapeDtypeStruct((64, 896), jnp.bfloat16)] * 4,
        [ids, heads, flip(heads, "k", 2, 1), *mine, *far],
        scratch=[pltpu.VMEM((256, 896), jnp.float32)],
    )
    sums = [partial[0]] + [
        lax.ppermute(partial[d], "zb", [(i, (i + d) % 4) for i in range(4)]) for d in (1, 2, 3)
    ]
    keep, give = simple(share_kernel, "share", [jax.ShapeDtypeStruct((32, 896), jnp.bfloat16)] * 2, sums)
    pieces = simple(
        merge_kernel,
        "merge",
        [jax.ShapeDtypeStruct((16, 896), jnp.bfloat16)] * 4,
        [keep, flip(give, "k", 2, 1)],
    )
    pieces = [pieces[0]] + [
        lax.ppermute(pieces[s], "x", [(i, (i + s) % 4) for i in range(4)]) for s in (1, 2, 3)
    ]
    return simple(place_kernel, "place", jax.ShapeDtypeStruct((8, 7168), jnp.bfloat16), [ids, *pieces])


def solution(mesh):
    fine = Mesh(mesh.devices.reshape(2, 4, 2, 4, 2, 2), ("yl", "x", "k", "zb", "z0", "yh"))
    cache, head = ("yl", "x", "k"), ("zb", "z0", "yh")
    return jax.shard_map(
        local,
        mesh=fine,
        in_specs=(
            P(cache, head),
            P(cache, head),
            P(cache, None),
            P(cache, None, None),
            P(cache, None, None),
            P(cache, None, None),
            P(),
            P(),
            P(head, None, None),
            P(head, None, None),
            P(head, cache),
        ),
        out_specs=P(cache + head, None),
        check_vma=False,
    )
```

```python
import functools

import jax
import jax.numpy as jnp
from jax import lax
from jax.experimental import pallas as pl
from jax.experimental.pallas import tpu as pltpu
from jax.sharding import Mesh, PartitionSpec as P

LAT = 512
NOPE = 128
ROPE = 64
VD = 128
BLOCK = 128
HEADS = 4
TOK = 128
ROWS = HEADS * TOK
SLOTS = 4
STEP = 4
LOG2E = 1.4426950408889634
SCALE2 = (NOPE + ROPE) ** -0.5 * LOG2E
LOW = -1e30
STAT = HEADS * VD
MSG = STAT + 128

VMEM = pltpu.VMEM
SMEM = pltpu.SMEM


def dot_nn(a, b):
    return lax.dot_general(a, b, (((1,), (0,)), ((), ())), preferred_element_type=jnp.float32)


def dot_nt(a, b):
    return lax.dot_general(a, b, (((1,), (1,)), ((), ())), preferred_element_type=jnp.float32)


def plan_kernel(ids, table, lens, lists, counts):
    yl, x, k = ids[0], ids[1], ids[2]
    for s in range(SLOTS):
        limit = lens[yl * 8 + ((x + s) % 4) * 2 + k]

        def scan(m, carry):
            found, valid = carry
            block = table[yl * 8 + ((x + s) % 4) * 2 + k, m]
            owner = block >> 2
            here = ((owner >> 1) & 3) == x

            @pl.when(here)
            def _():
                source = ((owner >> 3) ^ yl) + 2 * ((owner & 1) ^ k)
                lists[s * 16 + found] = source * 4 + (block & 3)

            step = here.astype(jnp.int32)
            return found + step, valid + step * jnp.minimum(limit - m * BLOCK, BLOCK)

        blocks = jnp.minimum((limit + BLOCK - 1) // BLOCK, 32)
        found, valid = lax.fori_loop(0, blocks, scan, (jnp.int32(0), jnp.int32(0)))
        counts[s] = found
        counts[SLOTS + s] = valid


def plan(ids, table, lens):
    scalar = pl.BlockSpec(memory_space=SMEM)
    return pl.pallas_call(
        plan_kernel,
        out_shape=[jax.ShapeDtypeStruct((SLOTS * 16,), jnp.int32), jax.ShapeDtypeStruct((2 * SLOTS,), jnp.int32)],
        in_specs=[scalar] * 3,
        out_specs=[scalar] * 2,
        compiler_params=pltpu.CompilerParams(vmem_limit_bytes=2**20),
        name="plan",
    )(ids, table, lens)


def prepare_kernel(counts, *refs):
    queries = refs[:SLOTS]
    w_uk, q_lat, q_rot = refs[SLOTS : SLOTS + 3]
    for h in range(HEADS):
        rows = slice(h * TOK, (h + 1) * TOK)
        part = jnp.concatenate([q[:, h * NOPE : (h + 1) * NOPE] for q in queries], axis=0)
        part = dot_nn(part, w_uk[h]).astype(jnp.bfloat16)
        first = HEADS * NOPE + h * ROPE
        for s in range(SLOTS):
            q_lat[s, rows, :] = part[s * TOK : (s + 1) * TOK]
            q_rot[s, rows, :] = queries[s][:, first : first + ROPE]


def attention_kernel(slots, own, lists, counts, q_lat, q_rot, *refs):
    count = len(slots)
    refs = list(refs)

    def take(n):
        got = refs[:n]
        del refs[:n]
        return got

    pools = take(4)
    (w_uv,) = take(1)
    new_latent, new_rope = take(2) if own else (None, None)
    outs = take(count)
    keys, rots, acc, top, tot, latents, levels = refs
    keys[...] = jnp.zeros_like(keys)
    rots[...] = jnp.zeros_like(rots)

    def wide(value, times):
        return jnp.concatenate([value] * times, axis=1)

    def begin(score, latent):
        best = jnp.broadcast_to(jnp.max(score, axis=1, keepdims=True), (ROWS, 128))
        times = score.shape[1] // 128
        weight = jnp.exp2((score - wide(best, times)) * SCALE2)
        top[...] = best
        tot[...] = sum(weight[:, i * 128 : (i + 1) * 128] for i in range(times))
        acc[...] = dot_nn(weight.astype(jnp.bfloat16), latent)

    def scores(slot, found, valid, q, r, chunk):
        for b in range(STEP):
            part = slice(b * BLOCK, (b + 1) * BLOCK)
            code = lists[slot * 16 + chunk * STEP + b]
            first = pl.multiple_of((code & 3) * BLOCK, BLOCK)
            for j in range(4):

                @pl.when(jnp.logical_and(chunk * STEP + b < found, (code >> 2) == j))
                def _():
                    keys[part, :] = pools[j][pl.ds(first, BLOCK), :]
                    rots[:, part] = pools[j][4 * BLOCK :, pl.ds(first, BLOCK)]

        score = dot_nt(q, keys[...]) + dot_nn(r, rots[...])
        seen = lax.broadcasted_iota(jnp.int32, score.shape, 1) < valid - chunk * STEP * BLOCK
        return jnp.where(seen, score, LOW)

    def one_slot(s, carry):
        slot = s + slots[0]
        found, valid = counts[slot], counts[SLOTS + slot]
        q, r = q_lat[slot], q_rot[slot]
        if own:
            score = dot_nt(q, new_latent[...]) + dot_nn(r, new_rope[...])
            at = lax.broadcasted_iota(jnp.int32, score.shape, 0) % TOK
            seen = lax.broadcasted_iota(jnp.int32, score.shape, 1) <= at
            begin(jnp.where(seen, score, LOW), new_latent[...])
        else:
            begin(scores(slot, found, valid, q, r, 0), keys[...])

        def step(chunk, inner):
            score = scores(slot, found, valid, q_lat[slot], q_rot[slot], chunk)
            before = top[...]
            best = jnp.maximum(before, jnp.max(score, axis=1, keepdims=True))
            keep = jnp.exp2((before - best) * SCALE2)
            weight = jnp.exp2((score - wide(best, STEP)) * SCALE2)
            top[...] = best
            tot[...] = tot[...] * keep + sum(weight[:, i * 128 : (i + 1) * 128] for i in range(STEP))
            acc[...] = acc[...] * wide(keep, 4) + dot_nn(weight.astype(jnp.bfloat16), keys[...])
            return inner

        lax.fori_loop(0 if own else 1, (found + STEP - 1) // STEP, step, 0)
        total = jnp.broadcast_to(jnp.sum(tot[...], axis=1, keepdims=True), (ROWS, 128))
        latents[s] = (acc[...] * wide(1.0 / total, 4)).astype(jnp.bfloat16)
        level = top[...] * SCALE2 + jnp.log2(total)
        levels[s] = level if own else jnp.where(found > 0, level, LOW)
        return carry

    lax.fori_loop(0, count, one_slot, 0)
    lane = lax.broadcasted_iota(jnp.int32, (TOK, 128), 1)
    for h in range(HEADS):
        rows = slice(h * TOK, (h + 1) * TOK)
        part = jnp.concatenate([latents[s, rows, :] for s in range(count)], axis=0)
        part = dot_nn(part, w_uv[h]).astype(jnp.bfloat16)
        for s in range(count):
            outs[s][:, h * VD : (h + 1) * VD] = part[s * TOK : (s + 1) * TOK]
    for s in range(count):
        level = levels[s, 0:TOK, :]
        for h in range(1, HEADS):
            level = jnp.where(lane % HEADS == h, levels[s, h * TOK : (h + 1) * TOK, :], level)
        high = level.astype(jnp.bfloat16).astype(jnp.float32)
        middle = (level - high).astype(jnp.bfloat16).astype(jnp.float32)
        low = level - high - middle
        stat = jnp.where(lane < HEADS, high, jnp.where(lane < 2 * HEADS, middle, low))
        outs[s][:, STAT:] = stat.astype(jnp.bfloat16)


def attention(slots, own, lists, counts, q_lat, q_rot, pools, w_uv, fresh):
    count = len(slots)
    full = pl.BlockSpec(memory_space=VMEM)
    scalar = pl.BlockSpec(memory_space=SMEM)
    return pl.pallas_call(
        functools.partial(attention_kernel, slots, own),
        out_shape=[jax.ShapeDtypeStruct((TOK, MSG), jnp.bfloat16)] * count,
        in_specs=[scalar] * 2 + [full] * (9 if own else 7),
        out_specs=[full] * count,
        scratch_shapes=[
            pltpu.VMEM((STEP * BLOCK, LAT), jnp.bfloat16),
            pltpu.VMEM((ROPE, STEP * BLOCK), jnp.bfloat16),
            pltpu.VMEM((ROWS, LAT), jnp.float32),
            pltpu.VMEM((ROWS, 128), jnp.float32),
            pltpu.VMEM((ROWS, 128), jnp.float32),
            pltpu.VMEM((count, ROWS, LAT), jnp.bfloat16),
            pltpu.VMEM((count, ROWS, 128), jnp.float32),
        ],
        compiler_params=pltpu.CompilerParams(vmem_limit_bytes=24 * 2**20),
        name="attend",
    )(lists, counts, q_lat, q_rot, *pools, w_uv, *fresh)


def combine_kernel(ids, *refs):
    parts, outs, total = refs[:SLOTS], refs[SLOTS : SLOTS + 4], refs[SLOTS + 4]
    a = ids[4]
    stats = [p[:, STAT:].astype(jnp.float32) for p in parts]
    for h in range(HEADS):
        columns = slice(h * VD, (h + 1) * VD)
        levels = [
            s[:, h : h + 1] + s[:, HEADS + h : HEADS + h + 1] + s[:, 2 * HEADS + h : 2 * HEADS + h + 1]
            for s in stats
        ]
        best = functools.reduce(jnp.maximum, levels)
        shares = [jnp.exp2(v - best) for v in levels]
        inverse = 1.0 / sum(shares)
        total[:, columns] = sum(
            p[:, columns].astype(jnp.float32) * (share * inverse) for p, share in zip(parts, shares)
        )
    for d in range(4):
        first = pl.multiple_of((a ^ d) * 8, 8)
        rows = [total[pl.ds(first + q * 32, 8), :] for q in range(4)]
        outs[d][...] = jnp.concatenate(rows, axis=0).astype(jnp.bfloat16)


def join_kernel(*refs):
    for d in range(4):
        refs[4][:, d * 512 : (d + 1) * 512] = refs[d][...]


def pack_kernel(q_nope, q_rope, pool_latent, pool_rope, query, pool, sems):
    moves = [(q_nope, query.at[:, : HEADS * NOPE]), (q_rope, query.at[:, HEADS * NOPE :])]
    for i in range(4):
        moves.append((pool_latent.at[i], pool.at[i * BLOCK : (i + 1) * BLOCK, :]))
        moves.append((pool_rope.at[i], pool.at[4 * BLOCK :, i * BLOCK : (i + 1) * BLOCK]))
    copies = [pltpu.make_async_copy(src, dst, sems.at[i]) for i, (src, dst) in enumerate(moves)]
    for copy in copies:
        copy.start()
    for copy in copies:
        copy.wait()


def pack(*args):
    return pl.pallas_call(
        pack_kernel,
        out_shape=[
            jax.ShapeDtypeStruct((TOK, HEADS * (NOPE + ROPE)), jnp.bfloat16),
            jax.ShapeDtypeStruct((4 * BLOCK + ROPE, LAT), jnp.bfloat16),
        ],
        in_specs=[pl.BlockSpec(memory_space=pltpu.HBM)] * 4,
        out_specs=[pl.BlockSpec(memory_space=VMEM)] * 2,
        scratch_shapes=[pltpu.SemaphoreType.DMA((10,))],
        compiler_params=pltpu.CompilerParams(vmem_limit_bytes=56 * 2**20),
        name="pack",
    )(*args)


def pair_kernel(one, two, out):
    out[0] = one[...]
    out[1] = two[...]


def project_kernel(ids, *refs):
    heads = refs[:8]
    pair, near, next_, far_one, far_two = refs[8:13]
    outs, total = refs[13:17], refs[17]
    zb = ids[3]
    rows = jnp.concatenate([h[...] for h in heads], axis=0)
    sides = []
    for side_y in range(2):
        value = None
        for d in range(4):
            dz = d >> 1
            if side_y == 0:
                weight = pair[dz] if d & 1 == 0 else (far_one, far_two)[dz][...]
            else:
                weight = (near, next_)[d & 1][dz]
            part = dot_nt(weight, rows[:, d * 512 : (d + 1) * 512])
            value = part if value is None else value + part
        sides.append(value)
    total[...] = jnp.concatenate(sides, axis=0).T
    for d in range(4):
        first = pl.multiple_of((zb ^ d) * 8, 8)
        parts = [total[pl.ds(first + s * 32, 8), :] for s in range(8)]
        outs[d][...] = jnp.concatenate(parts, axis=0).astype(jnp.bfloat16)


def share_kernel(*refs):
    total = sum(p[...].astype(jnp.float32) for p in refs[:4])
    refs[4][...] = total[:32]
    refs[5][...] = total[32:]


def merge_kernel(keep, got, *outs):
    for s in range(4):
        outs[s][:, :896] = keep[s * 8 : (s + 1) * 8, :]
        outs[s][:, 896:] = got[s * 8 : (s + 1) * 8, :]


def place_kernel(ids, *refs):
    parts, out = refs[:4], refs[4]
    yl, x, k = ids[0], ids[1], ids[2]
    for s in range(4):
        for side_y in range(2):
            first = ((yl ^ side_y) * 4 + (x - s + 4) % 4) * 896
            columns = pl.ds(pl.multiple_of(first, 128), 896)
            mine = parts[s][:, side_y * 448 : (side_y + 1) * 448]
            other = parts[s][:, 896 + side_y * 448 : 896 + (side_y + 1) * 448]
            value = jnp.where(
                k == 0, jnp.concatenate([mine, other], axis=1), jnp.concatenate([other, mine], axis=1)
            )
            out[:, columns] = value.astype(jnp.bfloat16)


def tie_kernel(*refs):
    pass


def tie(values, others):
    free = pl.BlockSpec(memory_space=pl.ANY)
    return pl.pallas_call(
        tie_kernel,
        out_shape=[jax.ShapeDtypeStruct(v.shape, v.dtype) for v in values],
        in_specs=[free] * (len(values) + len(others)),
        out_specs=[free] * len(values),
        input_output_aliases={i: i for i in range(len(values))},
        compiler_params=pltpu.CompilerParams(vmem_limit_bytes=2**20),
        name="tie",
    )(*values, *others)


def simple(kernel, name, out_shape, args, scratch=()):
    full = pl.BlockSpec(memory_space=VMEM)
    return pl.pallas_call(
        kernel,
        out_shape=out_shape,
        in_specs=[pl.BlockSpec(memory_space=SMEM) if arg.dtype == jnp.int32 else full for arg in args],
        out_specs=jax.tree.map(lambda _: full, out_shape),
        scratch_shapes=scratch,
        compiler_params=pltpu.CompilerParams(vmem_limit_bytes=16 * 2**20),
        name=name,
    )(*args)


def turn(value, axis, size, shift):
    return lax.ppermute(value, axis, [((i + shift) % size, i) for i in range(size)])


def flip(value, axis, size, bits):
    return lax.ppermute(value, axis, [(i, i ^ bits) for i in range(size)])


def local(
    q_nope,
    q_rope,
    new_latent,
    new_rope,
    pool_latent,
    pool_rope,
    block_table,
    prefix_len,
    w_uk,
    w_uv,
    w_out,
):
    ids = jnp.stack(
        [
            lax.axis_index("yl"),
            lax.axis_index("x"),
            lax.axis_index("k"),
            lax.axis_index("zb"),
            lax.axis_index("z0") * 2 + lax.axis_index("yh"),
        ]
    ).astype(jnp.int32)
    query, pool = pack(q_nope, q_rope, pool_latent, pool_rope)
    weight = w_out.T

    queries = [query] + [turn(query, "x", 4, s) for s in (1, 2, 3)]
    pool_y = flip(pool, "yl", 2, 1)
    weight_z = flip(weight, "z0", 2, 1)
    lists, counts = plan(ids, block_table, prefix_len)
    pool_y, counts, weight_z = tie([pool_y, counts, weight_z], queries[1:])
    q_lat, q_rot = simple(
        prepare_kernel,
        "prepare",
        [
            jax.ShapeDtypeStruct((SLOTS, ROWS, LAT), jnp.bfloat16),
            jax.ShapeDtypeStruct((SLOTS, ROWS, ROPE), jnp.bfloat16),
        ],
        [counts, *queries, w_uk],
    )
    pool_k = flip(pool, "k", 2, 1)
    pool_yk = flip(pool_y, "k", 2, 1)
    pair = simple(
        pair_kernel, "pair", jax.ShapeDtypeStruct((2, 448, 512), jnp.bfloat16), [weight, weight_z]
    )
    ring = ("yl", "yh")
    mine = [pair, flip(pair, ring, 4, 2), flip(pair, ring, 4, 3)]
    pools = [pool, pool_y, pool_k, pool_yk]

    away = attention((1, 2, 3), False, lists, counts, q_lat, q_rot, pools, w_uv, ())
    came = [
        lax.ppermute(part, "x", [(i, (i + s) % 4) for i in range(4)]) for s, part in zip((1, 2, 3), away)
    ]
    (home,) = attention((0,), True, lists, counts, q_lat, q_rot, pools, w_uv, (new_latent, new_rope[0]))
    heads = simple(
        combine_kernel,
        "combine",
        [jax.ShapeDtypeStruct((32, HEADS * VD), jnp.bfloat16)] * 4,
        [ids, home, *came],
        scratch=[pltpu.VMEM((TOK, HEADS * VD), jnp.float32)],
    )
    heads = [heads[0]] + [flip(heads[d], ("z0", "yh"), 4, d) for d in (1, 2, 3)]
    heads = simple(join_kernel, "join", jax.ShapeDtypeStruct((32, 2048), jnp.bfloat16), heads)
    heads, mine[1], mine[2] = tie([heads, mine[1], mine[2]], [])
    far = [flip(mine[2][0], ring, 4, 2), flip(mine[1][1], ring, 4, 3)]
    heads = [heads] + [turn(heads, "x", 4, s) for s in (1, 2, 3)]
    heads[1], *far = tie([heads[1], *far], [])
    partial = simple(
        project_kernel,
        "project",
        [jax.ShapeDtypeStruct((64, 896), jnp.bfloat16)] * 4,
        [ids, *heads, *[flip(h, "k", 2, 1) for h in heads], *mine, *far],
        scratch=[pltpu.VMEM((256, 896), jnp.float32)],
    )
    sums = [partial[0]] + [flip(partial[d], "zb", 4, d) for d in (1, 2, 3)]
    keep, give = simple(share_kernel, "share", [jax.ShapeDtypeStruct((32, 896), jnp.float32)] * 2, sums)
    pieces = simple(
        merge_kernel,
        "merge",
        [jax.ShapeDtypeStruct((8, 1792), jnp.float32)] * 4,
        [keep, flip(give, "k", 2, 1)],
    )
    pieces = [pieces[0]] + [
        lax.ppermute(pieces[s], "x", [(i, (i + s) % 4) for i in range(4)]) for s in (1, 2, 3)
    ]
    return simple(place_kernel, "place", jax.ShapeDtypeStruct((8, 7168), jnp.bfloat16), [ids, *pieces])


def solution(mesh):
    fine = Mesh(mesh.devices.reshape(2, 4, 2, 4, 2, 2), ("yl", "x", "k", "zb", "z0", "yh"))
    cache, head = ("yl", "x", "k"), ("zb", "z0", "yh")
    return jax.shard_map(
        local,
        mesh=fine,
        in_specs=(
            P(cache, head),
            P(cache, head),
            P(cache, None),
            P(cache, None, None),
            P(cache, None, None),
            P(cache, None, None),
            P(),
            P(),
            P(head, None, None),
            P(head, None, None),
            P(head, cache),
        ),
        out_specs=P(cache + head, None),
        check_vma=False,
    )
```
